128 devices in a mesh: seq: 16 (over z, x), tp: 4 (over y), grp: 2 (over core).
Axes of the slice: x: 4, y: 4, z: 4, core: 2. Of those that a mesh axis runs over, the one named last changes fastest.
Arguments:
- group_hidden: bfloat16 [4, 512, 7168], P(None, 'seq', ('tp', 'grp')), may hold values from -6 to 6
- group_query: bfloat16 [4, 512, 128, 576], P(None, 'seq', ('tp', 'grp')), may hold values from -36 to 36
- past_cache: bfloat16 [4, 3072, 576], P(None, 'seq'), may hold values from -6 to 6
- past_len: int32 [4], replicated, may hold values from 1536 to 3072, as said below
- decode_hidden: bfloat16 [256, 2, 7168], P('seq', None, ('tp', 'grp')), may hold values from -6 to 6
- decode_query: bfloat16 [256, 2, 128, 576], P('seq', None, ('tp', 'grp')), may hold values from -36 to 36
- decode_pool: bfloat16 [512, 384, 576], P('seq'), may hold values from -6 to 6
- owner: int32 [256, 1], P('seq'), may hold values from 0 to 15; in each aligned block of 16 rows (0 to 15, 16 to 31, ...) at most 2 rows name the same one
- dec_len: int32 [256], P('seq'), may hold values from 1 to 382, as said below
- w_latent: bfloat16 [7168, 576], P(('tp', 'grp')), may hold values from -0.0625 to 0.0625
- kv_gain: float32 [512], replicated, may hold values from 0.5 to 1.5
- w_value: bfloat16 [128, 512, 128], P(('tp', 'grp')), may hold values from -0.25 to 0.25
Outputs:
- prefill_out: bfloat16 [4, 512, 128, 128], P(None, 'seq', ('tp', 'grp'))
- decode_out: bfloat16 [256, 2, 128, 128], P('seq', None, ('tp', 'grp'))
The draws below stay inside these ranges and needn't reach their ends.
Inputs may be any that keep to these rules, and one draw needn't show every extreme that they name: `past_len`: at least half of the earlier positions are cached; some prompt has all 3072. `dec_len`: leaves room for the two new rows; some request has 382. Among the 16 requests that arrive at one index of seq, at most 2 name the same owner.
All inputs are finite; a program needn't handle non-finite values.
Results may differ from the reference program's by a relative error of at most 0.02.
Values may be sent and summed in bfloat16 or wider, within the bound.
No kernel may reach another device: no remote copies, remote signals or barrier semaphores. Data moves between devices by JAX's collectives and lax.ppermute only.
A program may use at most 192 MiB of HBM per device.

```python
import math
import jax
import jax.numpy as jnp
import numpy as np
from jax import lax

D = 7168
H = 128
LAT = 512
ROPE = 64
VHEAD = 128
PROMPTS = 4
REQ_DEV = 16
PAIR_CAP = 2
MAXLEN = 384
PAST = 3072
GROUP = 512
REQS = 256
N_SEQ = 16


def shared_rows(key):
    base = jnp.clip(jax.random.normal(key, (PROMPTS, PAST, LAT + ROPE), jnp.float32), -6.0, 6.0)
    row_index = jnp.arange(PAST)
    paired = ((row_index % 2 == 1) & (row_index < PAST // 2))[None, :, None]
    return jnp.where(paired, base, base)


def aligned_queries(rows, queries, token_grid, head_grid, near_weight):
    picked_index = 2 * ((token_grid * 37 + head_grid * 11) % (PAST // 4))
    strength = jnp.where((token_grid + head_grid) % 3 == 0, 3.0, jnp.where((token_grid + head_grid) % 3 == 1, 4.0, 6.0))
    chosen = ((token_grid + 2 * head_grid) % 5 == 0) & (near_weight > 0.5)
    picked = rows[picked_index]
    return jnp.where(chosen[..., None], strength[..., None] * picked, queries)


def draw_past_cache(key, part):
    return shared_rows(key).astype(jnp.bfloat16)


def draw_group_query(key, part):
    near_weight = 0.0
    rows = shared_rows(key)
    key = jax.random.fold_in(key, 7)
    queries = jnp.clip(jax.random.normal(key, (PROMPTS, GROUP, H, LAT + ROPE), jnp.float32), -6.0, 6.0)
    token_grid = jnp.arange(GROUP)[:, None] + jnp.zeros((1, H), jnp.int32)
    head_grid = jnp.arange(H)[None, :] + jnp.zeros((GROUP, 1), jnp.int32)
    results = [aligned_queries(rows[prompt_index], queries[prompt_index], token_grid, head_grid, near_weight) for prompt_index in range(PROMPTS)]
    return jnp.stack(results, axis=0).astype(jnp.bfloat16)


def draw_decode_query(key, part):
    near_weight = 0.0
    rows = shared_rows(key)
    key = jax.random.fold_in(key, 9)
    queries = jnp.clip(jax.random.normal(key, (REQS * 2, H, LAT + ROPE), jnp.float32), -6.0, 6.0)
    token_grid = jnp.arange(REQS * 2)[:, None] + jnp.zeros((1, H), jnp.int32)
    head_grid = jnp.arange(H)[None, :] + jnp.zeros((REQS * 2, 1), jnp.int32)
    shaped = aligned_queries(rows[0], queries, token_grid, head_grid, near_weight)
    return shaped.reshape(REQS, 2, H, LAT + ROPE).astype(jnp.bfloat16)


def draw_past_len(key, part):
    key = jax.random.fold_in(key, 3)
    length_key, index_key = jax.random.split(key)
    lengths = jax.random.randint(length_key, (PROMPTS,), PAST // 2, PAST + 1, dtype=jnp.int32)
    fullest = jax.random.randint(index_key, (), 0, PROMPTS, dtype=jnp.int32)
    return jnp.where(jnp.arange(PROMPTS, dtype=jnp.int32) == fullest, PAST, lengths).astype(jnp.int32)


def draw_dec_len(key, part):
    key = jax.random.fold_in(key, 5)
    length_key, index_key = jax.random.split(key)
    lengths = jax.random.randint(length_key, (REQS,), 1, MAXLEN - 1, dtype=jnp.int32)
    fullest = jax.random.randint(index_key, (), 0, REQS, dtype=jnp.int32)
    return jnp.where(jnp.arange(REQS, dtype=jnp.int32) == fullest, MAXLEN - 2, lengths).astype(jnp.int32)


def steps_of(stream_key, shape, cuts, low, largest):
    def one(axis_at, shards_of):
        draws = jax.random.uniform(jax.random.fold_in(jax.random.fold_in(stream_key, 6), axis_at), (shards_of,), jnp.float32, low / len(cuts), largest / len(cuts))
        return jnp.repeat(jnp.exp(draws), shape[axis_at] // shards_of).reshape((-1,) + (1,) * (len(shape) - axis_at - 1))

    level = one(*cuts[0])
    for cut in cuts[1:]:
        level = level * one(*cut)
    return level


def assign_block(own_key, own, number, rows, count, top, reach, lean):
    order = jax.random.permutation(own_key, count)
    heavy_load, common = shares(count, rows * top, reach, lean, True), shares(count, rows * top, reach, lean, False)
    places = jnp.arange(count)

    def named(tallies, turn):
        used = int((tallies > 0).sum())
        fixed = max(1, used // 4)
        moved = fixed + (places - fixed + turn * (used - fixed)) % max(1, count - fixed)
        return jnp.zeros((count,), jnp.int32).at[order[jnp.where(places < fixed, places, moved)]].set(jnp.asarray(tallies, jnp.int32))

    tallies = jnp.where(number % 4 == 0, named(heavy_load, number // 4), named(common, number - number // 4 - 1))
    mixed = jax.random.permutation(jax.random.fold_in(own, 3), count)
    donor, receiver = mixed[0:count // 2 * 2:2], mixed[1:count // 2 * 2:2]
    room = jnp.minimum(tallies[donor] - 1, reach - tallies[receiver]) // 2
    room = jnp.where((donor == order[0]) | (receiver == order[0]) | (tallies[receiver] == 0), 0, jnp.maximum(room, 0))
    moved = jax.random.randint(jax.random.fold_in(own, 4), (count // 2,), 0, 1 << 20) % (room + 1)
    tallies = tallies.at[donor].add(-moved).at[receiver].add(moved)
    members = jnp.searchsorted(jnp.cumsum(tallies), jnp.arange(rows * top), side="right").astype(jnp.int32)
    table = members.reshape(top, rows).T
    table = table[jax.random.permutation(jax.random.fold_in(own, 1), rows)]
    turn = jax.random.randint(jax.random.fold_in(own, 2), (rows, 1), 0, top)
    return jnp.take_along_axis(table, (jnp.arange(top)[None, :] + turn) % top, axis=1)


def shares(count, total, limit, slope, full):
    portions = [(1 << 20) // math.isqrt(standing ** slope) + 1 for standing in range(1, count + 1)]
    largest = limit if full else min(limit, max(-(-total // count), total * portions[0] // sum(portions)))
    least = 1 if total - largest >= count - 1 else 0
    given, rest = [largest] + [least] * (count - 1), total - largest - least * (count - 1)
    while rest > 0:
        free = [i for i in range(1, count) if given[i] < largest] or [i for i in range(1, count) if given[i] < limit]
        whole, budget = sum([portions[i] for i in free]), rest
        for i in free:
            more = min(limit - given[i], max(1, budget * portions[i] // whole), rest)
            given[i] = given[i] + more
            rest = rest - more
    return np.array(given)


def bell_draw(rng, shape, width, reach, shards=(), kind=jnp.bfloat16):
    factor_of = steps_of(rng, shape, shards, -0.22, 0.18) if shards else 1.0
    values = jax.random.normal(rng, shape, jnp.float32) * width * factor_of
    return jnp.minimum(jnp.maximum(values, -reach), reach).astype(kind)


def setup_inputs(seed: int = 0) -> dict:
    arg_keys = jax.random.split(jax.random.key(seed), 13)
    group_hidden = bell_draw(arg_keys[0], (PROMPTS, GROUP, D), 1.0, 6.0, ((1, 16), (2, 8)))
    group_query = draw_group_query(jax.random.fold_in(arg_keys[12], 71), 0)
    past_cache = draw_past_cache(jax.random.fold_in(arg_keys[12], 71), 0)
    past_len = draw_past_len(jax.random.fold_in(arg_keys[12], 71), 0)
    decode_hidden = bell_draw(arg_keys[4], (REQS, 2, D), 1.0, 6.0, ((0, 16), (2, 8)))
    decode_query = draw_decode_query(jax.random.fold_in(arg_keys[12], 71), 0)
    decode_pool = bell_draw(arg_keys[6], (N_SEQ * N_SEQ * PAIR_CAP, MAXLEN, LAT + ROPE), 1.0, 6.0, ((0, 16),))
    owner_keys = jax.random.split(jax.random.fold_in(arg_keys[7], 1), REQS // REQ_DEV)
    owner_turns = jax.random.permutation(jax.random.fold_in(arg_keys[7], 3), REQS // REQ_DEV)
    owner = jax.vmap(lambda own, number: assign_block(jax.random.fold_in(arg_keys[7], 2), own, number, REQ_DEV, N_SEQ, 1, PAIR_CAP, 2))(owner_keys, owner_turns).reshape((REQS, 1))
    dec_len = draw_dec_len(jax.random.fold_in(arg_keys[12], 71), 0)
    w_latent = bell_draw(arg_keys[9], (D, LAT + ROPE), D ** -0.5, 0.0625, ((0, 8),))
    kv_gain = jnp.clip(1.0 + 0.1 * jax.random.normal(arg_keys[10], (LAT,), jnp.float32), 0.5, 1.5)
    w_value = bell_draw(arg_keys[11], (H, LAT, VHEAD), LAT ** -0.5, 0.25, ((0, 8),))
    return dict(group_hidden=group_hidden, group_query=group_query, past_cache=past_cache, past_len=past_len, decode_hidden=decode_hidden, decode_query=decode_query, decode_pool=decode_pool, owner=owner, dec_len=dec_len, w_latent=w_latent, kv_gain=kv_gain, w_value=w_value)


epsilon = 1e-06

def rotate(rope_part, positions):
    half_width = rope_part.shape[-1] // 2
    frequency = jnp.exp(-jnp.log(10000.0) * jnp.arange(half_width).astype(jnp.float32) / half_width)
    angles = positions.astype(jnp.float32)[..., None] * frequency
    cosine = jnp.cos(angles)
    sine_part = jnp.sin(angles)
    former = rope_part[..., :half_width]
    latter = rope_part[..., half_width:]
    return jnp.concatenate([former * cosine - latter * sine_part, latter * cosine + former * sine_part], axis=-1)

def make_rows(latent, kv_gain, positions):
    lat_width = kv_gain.shape[0]
    latent_part = latent[..., :lat_width]
    spread = lax.optimization_barrier(jnp.mean(latent_part * latent_part, axis=-1, keepdims=True))
    normed = latent_part * lax.rsqrt(spread + epsilon) * kv_gain
    return jnp.concatenate([normed, rotate(latent[..., lat_width:], positions)], axis=-1).astype(jnp.bfloat16)

def attend(queries, key_rows, allowed):
    scale = (VHEAD + ROPE) ** (-0.5)
    scores = jnp.einsum('qc,kc->qk', queries.astype(jnp.float32), key_rows.astype(jnp.float32)) * scale
    masked = jnp.where(allowed, scores, -jnp.inf)
    highest = lax.optimization_barrier(jnp.max(masked, axis=-1, keepdims=True))
    weights = jnp.where(allowed, jnp.exp(masked - highest), 0.0)
    probabilities = (weights / lax.optimization_barrier(jnp.sum(weights, axis=-1, keepdims=True))).astype(jnp.bfloat16)
    values = key_rows[:, :LAT].astype(jnp.float32)
    return jnp.einsum('qk,kc->qc', probabilities.astype(jnp.float32), values).astype(jnp.bfloat16)

def reference(group_hidden, group_query, past_cache, past_len, decode_hidden, decode_query, decode_pool, owner, dec_len, w_latent, kv_gain, w_value):
    weight_full = w_latent.astype(jnp.float32)
    value_full = w_value.astype(jnp.float32)
    group_latent = jnp.einsum('ptd,dc->ptc', group_hidden.astype(jnp.float32), weight_full)
    decode_latent = jnp.einsum('rsd,dc->rsc', decode_hidden.astype(jnp.float32), weight_full)
    group_positions = past_len[:, None] + jnp.arange(GROUP, dtype=jnp.int32)[None, :]
    group_rows = make_rows(group_latent, kv_gain, group_positions)
    step_pair = jnp.arange(2, dtype=jnp.int32)
    decode_positions = past_len[0] + GROUP + dec_len[:, None] + step_pair[None, :]
    decode_rows = make_rows(decode_latent, kv_gain, decode_positions)
    prefix_all = jnp.concatenate([past_cache, group_rows], axis=1)
    key_index = jnp.arange(PAST + GROUP, dtype=jnp.int32)
    token_index = jnp.arange(GROUP, dtype=jnp.int32)

    def one_prompt(prompt_index):
        key_rows = prefix_all[prompt_index]
        allowed = jnp.where(key_index[None, :] < PAST, key_index[None, :] < past_len[prompt_index], key_index[None, :] - PAST <= token_index[:, None])

        def one_head(head_index):
            latent_out = attend(group_query[prompt_index, :, head_index, :], key_rows, allowed)
            return jnp.dot(latent_out, w_value[head_index], preferred_element_type=jnp.float32).astype(jnp.bfloat16)
        return lax.map(one_head, jnp.arange(H))
    prefill_heads = lax.map(one_prompt, jnp.arange(PROMPTS))
    prefill_out = jnp.transpose(prefill_heads, (0, 2, 1, 3))
    targets = owner[:, 0].reshape(N_SEQ, REQ_DEV)
    request_order = jnp.arange(REQ_DEV, dtype=jnp.int32)
    earlier = (targets[:, :, None] == targets[:, None, :]) & (request_order[None, None, :] < request_order[None, :, None])
    slot_rank = lax.optimization_barrier(jnp.sum(earlier.astype(jnp.int32), axis=2))
    arrival = jnp.arange(N_SEQ, dtype=jnp.int32)[:, None]
    slot_index = (targets * (N_SEQ * PAIR_CAP) + arrival * PAIR_CAP + slot_rank).reshape(REQS)
    prefix_rows = prefix_all[0]
    prefix_allowed = jnp.where(key_index < PAST, key_index < past_len[0], True)
    cache_index = jnp.arange(MAXLEN, dtype=jnp.int32)
    query_step = jnp.repeat(step_pair, H)

    def one_request(request_index):
        key_rows = jnp.concatenate([prefix_rows, decode_pool[slot_index[request_index]], decode_rows[request_index]], axis=0)
        allowed = jnp.concatenate([jnp.broadcast_to(prefix_allowed[None, :], (2 * H, PAST + GROUP)), jnp.broadcast_to((cache_index < dec_len[request_index])[None, :], (2 * H, MAXLEN)), step_pair[None, :] <= query_step[:, None]], axis=1)
        queries = decode_query[request_index].reshape(2 * H, LAT + ROPE)
        latent_out = attend(queries, key_rows, allowed).reshape(2, H, LAT)
        return jnp.einsum('shc,hcv->shv', latent_out.astype(jnp.float32), value_full).astype(jnp.bfloat16)
    decode_out = lax.map(one_request, jnp.arange(REQS))
    return (prefill_out, decode_out)
```

```python
import functools

import jax
import jax.numpy as jnp
from jax import lax
from jax.experimental import pallas as pl
from jax.experimental.pallas import tpu as pltpu
from jax.sharding import PartitionSpec as P

epsilon = 1e-06
negative = -1e30
log2_e = 1.4426950408889634
NT = (((1,), (1,)), ((), ()))
NN = (((1,), (0,)), ((), ()))
VMEM_BYTES = 56 * 2**20


def rotate(rope_part, positions):
    half_width = rope_part.shape[-1] // 2
    frequency = jnp.exp(-jnp.log(10000.0) * jnp.arange(half_width).astype(jnp.float32) / half_width)
    angles = positions.astype(jnp.float32)[..., None] * frequency
    cosine = jnp.cos(angles)
    sine_part = jnp.sin(angles)
    former = rope_part[..., :half_width]
    latter = rope_part[..., half_width:]
    return jnp.concatenate(
        [former * cosine - latter * sine_part, latter * cosine + former * sine_part], axis=-1
    )


def make_rows(latent, kv_gain, positions):
    lat_width = kv_gain.shape[0]
    latent_part = latent[..., :lat_width]
    spread = jnp.mean(latent_part * latent_part, axis=-1, keepdims=True)
    normed = latent_part * lax.rsqrt(spread + epsilon) * kv_gain
    return jnp.concatenate([normed, rotate(latent[..., lat_width:], positions)], axis=-1).astype(
        jnp.bfloat16
    )


def dot(left, right, dims):
    return lax.dot_general(left, right, dims, preferred_element_type=jnp.float32)


def key_scores(queries, keys, lat, dims):
    if dims is NT:
        return dot(queries[:, :lat], keys[:, :lat], NT) + dot(queries[:, lat:], keys[:, lat:], NT)
    return dot(queries[:, :lat], keys[:lat], NN) + dot(queries[:, lat:], keys[lat:], NN)


def lane_fold(op, total, block):
    for start in range(0, block.shape[1], 128):
        part = block[:, start : start + 128]
        total = part if total is None else op(total, part)
    return total


def attend_body(shape, info, q_ref, past_ref, group_ref, token_ref, *rest):
    tile, lat, factor, head_local, decode, chunk = shape
    if decode:
        fresh_ref, out_ref, lse_ref, hold = rest
    else:
        out_ref, hold = rest
    rows = q_ref.shape[0]
    pieces, piece_rows, width = past_ref.shape
    step = chunk // piece_rows
    past_count = pieces // step
    past_total = pieces * piece_rows
    half_past = past_total // 2
    past_len = info[0] if decode else info[pl.program_id(0)]

    def past_keys(j):
        return past_ref[j * step : (j + 1) * step].reshape(chunk, width)

    def group_keys():
        return group_ref[...].reshape(group_ref.shape[0] * group_ref.shape[1], width)

    group_total = group_ref.shape[0] * group_ref.shape[1]
    for i in range(rows // tile):
        span = pl.ds(i * tile, tile)
        queries = q_ref[span, :]
        row = lax.broadcasted_iota(jnp.int32, (tile, 1), 0) + i * tile
        highest = None
        for j in range(past_count):
            scores = key_scores(queries, past_keys(j), lat, NT)
            if (j + 1) * chunk > half_past:
                place = lax.broadcasted_iota(jnp.int32, (1, chunk), 1) + j * chunk
                scores = jnp.where(place < past_len, scores, negative)
            hold[i % 2, :, j * chunk : (j + 1) * chunk] = scores
            highest = lane_fold(jnp.maximum, highest, scores)
        scores = key_scores(queries, group_keys(), lat, NT)
        if not decode:
            token = info[4] + row // head_local
            scores = jnp.where(token_ref[...] <= token, scores, negative)
        hold[i % 2, :, past_total : past_total + group_total] = scores
        highest = lane_fold(jnp.maximum, highest, scores)
        if decode:
            fresh = fresh_ref[...]
            scores = key_scores(queries, fresh, lat, NT)
            place = lax.broadcasted_iota(jnp.int32, (1, fresh.shape[0]), 1)
            request = row // (2 * head_local)
            last = row // head_local
            scores = jnp.where((place >= 2 * request) & (place <= last), scores, negative)
            fresh_span = slice(past_total + group_total, past_total + group_total + fresh.shape[0])
            hold[i % 2, :, fresh_span] = scores
            highest = lane_fold(jnp.maximum, highest, scores)
        peak = jnp.max(highest, axis=1, keepdims=True)
        total = None
        summed = None
        parts = [
            (slice(j * chunk, (j + 1) * chunk), functools.partial(past_keys, j))
            for j in range(past_count)
        ]
        parts.append((slice(past_total, past_total + group_total), group_keys))
        if decode:
            parts.append((fresh_span, lambda: fresh_ref[...]))
        for place, keys in parts:
            weights = jnp.exp2((hold[i % 2, :, place] - peak) * factor)
            total = lane_fold(jnp.add, total, weights)
            part = dot(weights.astype(jnp.bfloat16), keys()[:, :lat], NN)
            summed = part if summed is None else summed + part
        total = jnp.sum(total, axis=1, keepdims=True)
        out_ref[span, :] = (summed / total).astype(jnp.bfloat16)
        if decode:
            lse = peak * factor + jnp.log2(total)
            lse_ref[span, :] = jnp.broadcast_to(lse, (tile, lse_ref.shape[1]))


def attend(info, query, past, group, token, fresh, lat, factor, head_local):
    decode = fresh is not None
    count, rows, width = query.shape
    pieces, _, piece_rows, _ = past.shape
    group_pieces, _, group_rows, _ = group.shape
    keys = pieces * piece_rows + group_pieces * group_rows
    tile = min(256, rows)
    chunk = 768
    in_specs = [
        pl.BlockSpec((None, rows, width), lambda p, _: (p, 0, 0)),
        pl.BlockSpec((pieces, None, piece_rows, width), lambda p, _: (0, p, 0, 0)),
        pl.BlockSpec((group_pieces, None, group_rows, width), lambda p, _: (0, p, 0, 0)),
        pl.BlockSpec(token.shape, lambda p, _: (0, 0)),
    ]
    operands = [query, past, group, token]
    out_specs = [pl.BlockSpec((None, rows, lat), lambda p, _: (p, 0, 0))]
    out_shape = [jax.ShapeDtypeStruct((count, rows, lat), jnp.bfloat16)]
    if decode:
        in_specs.append(pl.BlockSpec(fresh.shape, lambda p, _: (0, 0)))
        operands.append(fresh)
        keys += fresh.shape[0]
        out_specs.append(pl.BlockSpec((None, rows, 128), lambda p, _: (p, 0, 0)))
        out_shape.append(jax.ShapeDtypeStruct((count, rows, 128), jnp.float32))
    shape = (tile, lat, factor, head_local, decode, chunk)
    return pl.pallas_call(
        functools.partial(attend_body, shape),
        grid_spec=pltpu.PrefetchScalarGridSpec(
            num_scalar_prefetch=1,
            grid=(count,),
            in_specs=in_specs,
            out_specs=out_specs,
            scratch_shapes=[pltpu.VMEM((2, tile, keys), jnp.float32)],
        ),
        out_shape=out_shape,
        compiler_params=pltpu.CompilerParams(vmem_limit_bytes=VMEM_BYTES),
        cost_estimate=pl.CostEstimate(
            flops=2 * count * rows * keys * (768 + lat),
            bytes_accessed=2 * count * (keys + 2 * rows) * width,
            transcendentals=count * rows * keys,
        ),
        name="attend_decode" if decode else "attend_prefill",
    )(info, *operands)


def dispatch_body(source, length, q_ref, out_ref):
    slots, rows, width = out_ref.shape
    lat_rope = q_ref.shape[2]
    lane = lax.broadcasted_iota(jnp.int32, (rows, width - lat_rope), 1)
    for slot in range(slots):
        out_ref[slot, :, :lat_rope] = q_ref[source[slot]]
        size = length[slot]
        tail = jnp.where(lane < 32, size // 16, size % 16)
        out_ref[slot, :, lat_rope:] = tail.astype(jnp.float32).astype(jnp.bfloat16)


def dispatch_queries(source, length, query, width):
    slots = source.shape[0]
    _, rows, _ = query.shape
    smem = pl.BlockSpec(memory_space=pltpu.SMEM)
    vmem = pl.BlockSpec(memory_space=pltpu.VMEM)
    return pl.pallas_call(
        dispatch_body,
        in_specs=[smem, smem, vmem],
        out_specs=vmem,
        out_shape=jax.ShapeDtypeStruct((slots, rows, width), jnp.bfloat16),
        compiler_params=pltpu.CompilerParams(vmem_limit_bytes=VMEM_BYTES),
        name="dispatch_queries",
    )(source, length, query)


def cache_body(lat, factor, batch, order, length, used, q_ref, *rest):
    pool_refs = rest[:batch]
    out_ref, lse_ref = rest[batch:]
    step = pl.program_id(0)
    rows = q_ref.shape[1]
    width, cache_rows = pool_refs[0].shape

    @pl.when(step * batch < used[0])
    def _():
        place = lax.broadcasted_iota(jnp.int32, (1, cache_rows), 1)
        lane = lax.broadcasted_iota(jnp.int32, (rows, lse_ref.shape[2]), 1)
        slots = [order[step * batch + b] for b in range(batch)]
        scores = [
            key_scores(q_ref[slots[b], :, :width], pool_refs[b][...], lat, NN)
            for b in range(batch)
        ]
        for b in range(batch):
            masked = jnp.where(place < length[slots[b]], scores[b], negative)
            peak = jnp.max(masked, axis=1, keepdims=True)
            weights = jnp.exp2((masked - peak) * factor)
            total = jnp.sum(weights, axis=1, keepdims=True)
            summed = dot(weights.astype(jnp.bfloat16), pool_refs[b][:lat], NT)
            out_ref[slots[b]] = (summed / total).astype(jnp.bfloat16)
            lse = peak * factor + jnp.log2(total)
            high = lse.astype(jnp.bfloat16).astype(jnp.float32)
            middle = (lse - high).astype(jnp.bfloat16).astype(jnp.float32)
            low = lse - high - middle
            lse_ref[slots[b]] = jnp.where(
                lane == 0, high, jnp.where(lane == 1, middle, low)
            ).astype(jnp.bfloat16)


def attend_cache(order, length, used, query, pool, lat, factor):
    batch = 4
    slots, rows, padded = query.shape
    _, width, cache_rows = pool.shape
    whole = pl.BlockSpec((slots, rows, padded), lambda i, *_: (0, 0, 0))

    def pool_spec(b):
        return pl.BlockSpec(
            (None, width, cache_rows), lambda i, order, *_: (order[i * batch + b], 0, 0)
        )

    return pl.pallas_call(
        functools.partial(cache_body, lat, factor, batch),
        grid_spec=pltpu.PrefetchScalarGridSpec(
            num_scalar_prefetch=3,
            grid=(slots // batch,),
            in_specs=[whole] + [pool_spec(b) for b in range(batch)],
            out_specs=[
                pl.BlockSpec((slots, rows, lat), lambda i, *_: (0, 0, 0)),
                pl.BlockSpec((slots, rows, 128), lambda i, *_: (0, 0, 0)),
            ],
        ),
        out_shape=[
            jax.ShapeDtypeStruct((slots, rows, lat), jnp.bfloat16),
            jax.ShapeDtypeStruct((slots, rows, 128), jnp.bfloat16),
        ],
        compiler_params=pltpu.CompilerParams(vmem_limit_bytes=VMEM_BYTES),
        cost_estimate=pl.CostEstimate(
            flops=2 * slots * 128 * cache_rows * (width + lat),
            bytes_accessed=2 * slots * cache_rows * width,
            transcendentals=slots * rows * cache_rows,
        ),
        name="attend_cache",
    )(order, length, used, query, *([pool] * batch))


def merge_body(slot, back_ref, near_ref, near_lse_ref, out_ref):
    count = near_ref.shape[0]
    width = near_ref.shape[2]
    for r in range(count):
        back = back_ref[slot[r]].astype(jnp.float32)
        far = back[:, :width]
        far_lse = back[:, width : width + 1] + back[:, width + 1 : width + 2]
        far_lse = far_lse + back[:, width + 2 : width + 3]
        near_lse = near_lse_ref[r][:, :1]
        peak = jnp.maximum(far_lse, near_lse)
        far_part = jnp.exp2(far_lse - peak)
        near_part = jnp.exp2(near_lse - peak)
        mixed = far * far_part + near_ref[r] * near_part
        out_ref[r] = (mixed / (far_part + near_part)).astype(jnp.bfloat16)


def merge_decode(slot, back, near, near_lse):
    smem = pl.BlockSpec(memory_space=pltpu.SMEM)
    vmem = pl.BlockSpec(memory_space=pltpu.VMEM)
    return pl.pallas_call(
        merge_body,
        in_specs=[smem, vmem, vmem, vmem],
        out_specs=vmem,
        out_shape=jax.ShapeDtypeStruct(near.shape, jnp.bfloat16),
        compiler_params=pltpu.CompilerParams(vmem_limit_bytes=VMEM_BYTES),
        name="merge_decode",
    )(slot, back, near, near_lse)


def swap_core(value):
    return lax.ppermute(value, "grp", [(0, 1), (1, 0)])


def fetch_tp(value, shift):
    return lax.ppermute(value, "tp", [((i + shift) % 4, i) for i in range(4)])


def fetch_x(value, shift):
    return lax.ppermute(
        value, "seq", [(i // 4 * 4 + (i + shift) % 4, i) for i in range(16)]
    )


def fetch_z(value, shift):
    return lax.ppermute(value, "seq", [((i + 4 * shift) % 16, i) for i in range(16)])


def on_device(
    group_hidden,
    group_query,
    past_cache,
    past_len,
    decode_hidden,
    decode_query,
    decode_pool,
    owner,
    dec_len,
    w_latent,
    kv_gain,
    w_value,
):
    seq_count = lax.axis_size("seq")
    seq_place = lax.axis_index("seq")
    tp_place = lax.axis_index("tp")
    core = lax.axis_index("grp")
    z_place, x_place = seq_place // 4, seq_place % 4
    prompt_count, group_local, head_local, row_width = group_query.shape
    past_local = past_cache.shape[1]
    request_local = decode_query.shape[0]
    lat = kv_gain.shape[0]
    value_width = w_value.shape[2]
    slot_count = decode_pool.shape[0]
    pair_limit = slot_count // seq_count
    query_pairs = 2 * head_local
    factor = (value_width + row_width - lat) ** (-0.5) * log2_e

    half = past_local // 2
    past_half = lax.dynamic_slice_in_dim(past_cache, core * half, half, axis=1)
    past_all = lax.all_gather(past_half, ("seq", "grp"), axis=0, tiled=False)

    targets = owner[:, 0]
    request_order = jnp.arange(request_local, dtype=jnp.int32)
    earlier = (targets[:, None] == targets[None, :]) & (
        request_order[None, :] < request_order[:, None]
    )
    slot_rank = jnp.sum(earlier.astype(jnp.int32), axis=1)
    destination = targets * pair_limit + slot_rank
    matches = jnp.arange(slot_count, dtype=jnp.int32)[:, None] == destination[None, :]
    source = jnp.sum(jnp.where(matches, request_order[None, :], 0), axis=1)
    send_length = jnp.sum(jnp.where(matches, dec_len[None, :], 0), axis=1)
    send_query = dispatch_queries(
        source,
        send_length,
        decode_query.reshape(request_local, query_pairs, row_width),
        row_width + 64,
    )
    arrived = lax.all_to_all(
        send_query.reshape(seq_count, pair_limit * query_pairs, row_width + 64),
        "seq",
        split_axis=0,
        concat_axis=0,
        tiled=True,
    ).reshape(slot_count, query_pairs, row_width + 64)
    marks = arrived[:, 0, row_width:].astype(jnp.float32)
    slot_length = (marks[:, 0] * 16 + marks[:, 32]).astype(jnp.int32)

    part_tokens = group_local // 8
    part_pairs = 2 * request_local // 8
    part_rows = prompt_count * part_tokens + part_pairs
    hidden_group = group_hidden.reshape(prompt_count, 8, part_tokens, -1).transpose(1, 0, 2, 3)
    hidden_decode = decode_hidden.reshape(8, part_pairs, -1)
    hidden = jnp.concatenate(
        [hidden_group.reshape(8, prompt_count * part_tokens, -1), hidden_decode], axis=1
    )
    partial = jnp.einsum("krd,dc->krc", hidden, w_latent, preferred_element_type=jnp.float32)
    partial = partial.astype(jnp.bfloat16).reshape(4, 2, part_rows, row_width)
    keep = lax.dynamic_index_in_dim(partial, core, axis=1, keepdims=False)
    give = lax.dynamic_index_in_dim(partial, 1 - core, axis=1, keepdims=False)
    pair_sum = (keep.astype(jnp.float32) + swap_core(give).astype(jnp.float32)).astype(jnp.bfloat16)
    latent = lax.dynamic_index_in_dim(pair_sum, tp_place, axis=0, keepdims=False)
    latent = latent.astype(jnp.float32)
    for shift in range(1, 4):
        sent = lax.dynamic_index_in_dim(
            pair_sum, (tp_place - shift) % 4, axis=0, keepdims=False
        )
        latent = latent + fetch_tp(sent, shift).astype(jnp.float32)
    part = tp_place * 2 + core
    token = part * part_tokens + jnp.arange(part_tokens, dtype=jnp.int32)
    group_positions = past_len[:, None] + seq_place * group_local + token[None, :]
    pair_index = part * part_pairs + jnp.arange(part_pairs, dtype=jnp.int32)
    decode_positions = (
        past_len[0] + group_local * seq_count + dec_len[pair_index // 2] + pair_index % 2
    )
    positions = jnp.concatenate([group_positions.reshape(-1), decode_positions])
    rows_own = make_rows(latent, kv_gain, positions)
    rows_tp = [rows_own] + [fetch_tp(rows_own, shift) for shift in range(1, 4)]
    tp_order = (tp_place + jnp.arange(4, dtype=jnp.int32)) % 4
    rows_tp = jnp.stack(rows_tp)

    fresh_own = rows_tp[:, prompt_count * part_tokens :]
    fresh_other = swap_core(fresh_own)
    fresh_even = jnp.where(core == 0, fresh_own, fresh_other)
    fresh_odd = jnp.where(core == 0, fresh_other, fresh_own)
    fresh = jnp.stack([fresh_even, fresh_odd], axis=1)
    fresh = fresh[(jnp.arange(4, dtype=jnp.int32) - tp_place) % 4]
    fresh = fresh.reshape(2 * request_local, row_width)
    fresh = jnp.pad(fresh, ((0, 128 - 2 * request_local), (0, 0)))

    group_own = rows_tp[:, : prompt_count * part_tokens].reshape(
        4, prompt_count, part_tokens, row_width
    )
    group_own = group_own.transpose(1, 0, 2, 3).reshape(prompt_count, 4 * part_tokens, row_width)
    group_x = jnp.stack([group_own] + [fetch_x(group_own, shift) for shift in range(1, 4)])
    group_z = jnp.stack([group_x] + [fetch_z(group_x, shift) for shift in range(1, 4)])
    group_z = group_z.reshape(16, prompt_count, 4 * part_tokens, row_width)
    group_all = jnp.concatenate([group_z, swap_core(group_z)], axis=0)
    ring = jnp.arange(4, dtype=jnp.int32)
    holder = ((z_place + ring) % 4)[:, None] * 4 + ((x_place + ring) % 4)[None, :]
    cores = jnp.stack([core, 1 - core])
    key_token = (
        holder.reshape(1, 16, 1, 1) * group_local
        + (tp_order.reshape(1, 1, 4, 1) * 2 + cores.reshape(2, 1, 1, 1)) * part_tokens
        + jnp.arange(part_tokens, dtype=jnp.int32).reshape(1, 1, 1, part_tokens)
    ).reshape(1, seq_count * group_local)

    is_used = slot_length > 0
    used_rank = jnp.cumsum(is_used.astype(jnp.int32)) - 1
    used = jnp.sum(is_used.astype(jnp.int32))
    slots = jnp.arange(slot_count, dtype=jnp.int32)
    wanted = jnp.minimum(slots, jnp.maximum(used - 1, 0))
    order = jnp.sum(
        jnp.where(is_used[None, :] & (used_rank[None, :] == wanted[:, None]), slots[None, :], 0),
        axis=1,
    )
    cache_latent, cache_lse = attend_cache(
        order, slot_length, used.reshape(1), arrived, jnp.swapaxes(decode_pool, 1, 2), lat, factor
    )
    cache_value = jnp.einsum(
        "nshc,hcv->nshv",
        cache_latent.reshape(slot_count, 2, head_local, lat),
        w_value,
        preferred_element_type=jnp.float32,
    ).astype(jnp.bfloat16)
    back = jnp.concatenate(
        [cache_value.reshape(slot_count, query_pairs, value_width), cache_lse], axis=-1
    )
    back = lax.all_to_all(
        back.reshape(seq_count, pair_limit * query_pairs, 2 * value_width),
        "seq",
        split_axis=0,
        concat_axis=0,
        tiled=True,
    ).reshape(slot_count, query_pairs, 2 * value_width)

    info = jnp.concatenate([past_len, (seq_place * group_local)[None]]).astype(jnp.int32)
    near_latent, near_lse = attend(
        info,
        decode_query.reshape(1, request_local * query_pairs, row_width),
        past_all,
        group_all,
        key_token,
        fresh,
        lat,
        factor,
        head_local,
    )
    near = jnp.einsum(
        "rshc,hcv->rshv",
        near_latent.reshape(request_local, 2, head_local, lat),
        w_value,
        preferred_element_type=jnp.float32,
    )
    decode_out = merge_decode(
        destination,
        back,
        near.reshape(request_local, query_pairs, value_width),
        near_lse.reshape(request_local, query_pairs, 128),
    ).reshape(request_local, 2, head_local, value_width)

    (prefill_latent,) = attend(
        info,
        group_query.reshape(prompt_count, group_local * head_local, row_width),
        past_all,
        group_all,
        key_token,
        None,
        lat,
        factor,
        head_local,
    )
    prefill_out = jnp.einsum(
        "pthc,hcv->pthv",
        prefill_latent.reshape(prompt_count, group_local, head_local, lat),
        w_value,
        preferred_element_type=jnp.float32,
    ).astype(jnp.bfloat16)
    return (prefill_out, decode_out)


def solution(mesh):
    in_specs = (
        P(None, "seq", ("tp", "grp")),
        P(None, "seq", ("tp", "grp"), None),
        P(None, "seq", None),
        P(),
        P("seq", None, ("tp", "grp")),
        P("seq", None, ("tp", "grp"), None),
        P("seq", None, None),
        P("seq", None),
        P("seq"),
        P(("tp", "grp"), None),
        P(),
        P(("tp", "grp"), None, None),
    )
    out_specs = (P(None, "seq", ("tp", "grp"), None), P("seq", None, ("tp", "grp"), None))
    return jax.shard_map(
        on_device, mesh=mesh, in_specs=in_specs, out_specs=out_specs, check_vma=False
    )
```

```python
import functools

import jax
import jax.numpy as jnp
from jax import lax
from jax.experimental import pallas as pl
from jax.experimental.pallas import tpu as pltpu
from jax.sharding import PartitionSpec as P

epsilon = 1e-06
negative = -1e30
log2_e = 1.4426950408889634
NT = (((1,), (1,)), ((), ()))
NN = (((1,), (0,)), ((), ()))
VMEM_BYTES = 56 * 2**20


def rotate(rope_part, positions):
    half_width = rope_part.shape[-1] // 2
    frequency = jnp.exp(-jnp.log(10000.0) * jnp.arange(half_width).astype(jnp.float32) / half_width)
    angles = positions.astype(jnp.float32)[..., None] * frequency
    cosine = jnp.cos(angles)
    sine_part = jnp.sin(angles)
    former = rope_part[..., :half_width]
    latter = rope_part[..., half_width:]
    return jnp.concatenate(
        [former * cosine - latter * sine_part, latter * cosine + former * sine_part], axis=-1
    )


def make_rows(latent, kv_gain, positions):
    lat_width = kv_gain.shape[0]
    latent_part = latent[..., :lat_width]
    spread = jnp.mean(latent_part * latent_part, axis=-1, keepdims=True)
    normed = latent_part * lax.rsqrt(spread + epsilon) * kv_gain
    return jnp.concatenate([normed, rotate(latent[..., lat_width:], positions)], axis=-1).astype(
        jnp.bfloat16
    )


def dot(left, right, dims):
    return lax.dot_general(left, right, dims, preferred_element_type=jnp.float32)


def key_scores(queries, keys, lat, dims):
    if dims is NT:
        return dot(queries[:, :lat], keys[:, :lat], NT) + dot(queries[:, lat:], keys[:, lat:], NT)
    return dot(queries[:, :lat], keys[:lat], NN) + dot(queries[:, lat:], keys[lat:], NN)


def lane_fold(op, total, block):
    for start in range(0, block.shape[1], 128):
        part = block[:, start : start + 128]
        total = part if total is None else op(total, part)
    return total


def attend_rows(shape, q_ref, out_ref, lse_ref, hold, past_keys, past_len, others, row_masks):
    tile, lat, factor, chunk, past_count = shape
    rows = q_ref.shape[0]
    for i in range(rows // tile):
        span = pl.ds(i * tile, tile)
        queries = q_ref[span, :]
        row = lax.broadcasted_iota(jnp.int32, (tile, 1), 0) + i * tile
        highest = None
        parts = []
        end = 0
        for j in range(past_count + len(others)):
            keys = functools.partial(past_keys, j) if j < past_count else others[j - past_count]
            block = keys()
            scores = key_scores(queries, block, lat, NT)
            if j >= past_count:
                mask = row_masks[j - past_count](row)
                if mask is not None:
                    scores = jnp.where(mask, scores, negative)
            elif (j + 1) * chunk > past_count * chunk // 2:
                place = lax.broadcasted_iota(jnp.int32, (1, chunk), 1) + j * chunk
                scores = jnp.where(place < past_len, scores, negative)
            place = slice(end, end + block.shape[0])
            end += block.shape[0]
            parts.append((place, keys))
            hold[i % 2, :, place] = scores
            highest = lane_fold(jnp.maximum, highest, scores)
        peak = jnp.max(highest, axis=1, keepdims=True)
        total = None
        summed = None
        for place, keys in parts:
            weights = jnp.exp2((hold[i % 2, :, place] - peak) * factor)
            total = lane_fold(jnp.add, total, weights)
            part = dot(weights.astype(jnp.bfloat16), keys()[:, :lat], NN)
            summed = part if summed is None else summed + part
        total = jnp.sum(total, axis=1, keepdims=True)
        out_ref[span, :] = (summed / total).astype(jnp.bfloat16)
        if lse_ref is not None:
            lse = peak * factor + jnp.log2(total)
            lse_ref[span, :] = jnp.broadcast_to(lse, (tile, lse_ref.shape[1]))


def group_masks(info, token_ref, head_local):
    def mask(c):
        return lambda row: token_ref[c : c + 1, :] <= info[4] + row // head_local

    return [mask(0), mask(1)]


def later_body(
    shape, head_local, first, info, q_ref, past_ref, near_ref, far_ref, token_ref, out_ref, hold
):
    chunk, past_count = shape[3:]
    pieces, piece_rows, width = past_ref.shape
    step = pieces // past_count

    def past_keys(j):
        return past_ref[j * step : (j + 1) * step].reshape(chunk, width)

    attend_rows(
        shape,
        q_ref,
        out_ref,
        None,
        hold,
        past_keys,
        info[first + pl.program_id(0)],
        [lambda: near_ref[...], lambda: far_ref[...]],
        group_masks(info, token_ref, head_local),
    )


def first_body(
    shape, head_local, pieces, info, q_ref, dq_ref, near_ref, far_ref, token_ref, fresh_ref, *rest
):
    chunk, past_count = shape[3:]
    piece_refs = rest[:pieces]
    out_ref, decode_ref, lse_ref, hold, past, arrive = rest[pieces:]
    holders, piece_rows, width = past.shape
    step = holders // past_count
    z_place, x_place, core = info[6], info[7], info[8]
    copies = []
    for c in range(2):
        side = core if c == 0 else 1 - core
        for dz in range(4):
            for dx in range(4):
                holder = lax.rem(z_place + dz, 4) * 4 + lax.rem(x_place + dx, 4)
                copies.append(
                    pltpu.make_async_copy(
                        piece_refs[c * 4 + dz].at[dx],
                        past.at[holder * 2 + side],
                        arrive.at[c * 16 + dz * 4 + dx],
                    )
                )
    for copy in copies:
        copy.start()
    for copy in copies:
        copy.wait()

    def past_keys(j):
        return past[j * step : (j + 1) * step].reshape(chunk, width)

    group = [lambda: near_ref[...], lambda: far_ref[...]]
    attend_rows(
        shape,
        q_ref,
        out_ref,
        None,
        hold,
        past_keys,
        info[0],
        group,
        group_masks(info, token_ref, head_local),
    )

    def fresh_mask(row):
        place = lax.broadcasted_iota(jnp.int32, (1, fresh_ref.shape[0]), 1)
        return (place >= row // (2 * head_local) * 2) & (place <= row // head_local)

    attend_rows(
        shape,
        dq_ref,
        decode_ref,
        lse_ref,
        hold,
        past_keys,
        info[0],
        group + [lambda: fresh_ref[...]],
        [lambda row: None, lambda row: None, fresh_mask],
    )


def attend_later(info, query, past, near, far, token, first, lat, factor, head_local):
    count = past.shape[1]
    _, rows, width = query.shape
    pieces, _, piece_rows, _ = past.shape
    keys = pieces * piece_rows + 2 * near.shape[1]
    tile = min(256, rows)
    chunk = 768
    shape = (tile, lat, factor, chunk, pieces * piece_rows // chunk)

    def group_place(p, info):
        return (lax.rem(p + first + info[5], 4), 0, 0)

    group_spec = pl.BlockSpec((None, near.shape[1], width), group_place)
    return pl.pallas_call(
        functools.partial(later_body, shape, head_local, first),
        grid_spec=pltpu.PrefetchScalarGridSpec(
            num_scalar_prefetch=1,
            grid=(count,),
            in_specs=[
                pl.BlockSpec((None, rows, width), lambda p, _: (p + first, 0, 0)),
                pl.BlockSpec((pieces, None, piece_rows, width), lambda p, _: (0, p, 0, 0)),
                group_spec,
                group_spec,
                pl.BlockSpec(token.shape, lambda p, _: (0, 0)),
            ],
            out_specs=pl.BlockSpec((None, rows, lat), lambda p, _: (p, 0, 0)),
            scratch_shapes=[pltpu.VMEM((2, tile, keys), jnp.float32)],
        ),
        out_shape=jax.ShapeDtypeStruct((count, rows, lat), jnp.bfloat16),
        compiler_params=pltpu.CompilerParams(vmem_limit_bytes=VMEM_BYTES),
        cost_estimate=pl.CostEstimate(
            flops=2 * count * rows * keys * (768 + lat),
            bytes_accessed=2 * count * (keys + 2 * rows) * width,
            transcendentals=count * rows * keys,
        ),
        name="attend_later",
    )(info, query, past, near, far, token)


def attend_first(info, query, decode_query, past, near, far, token, fresh, lat, factor, head_local):
    _, rows, width = query.shape
    decode_rows = decode_query.shape[0]
    holders = 2 * 16
    piece_rows = past[0].shape[1]
    keys = holders * piece_rows + 2 * near.shape[1] + fresh.shape[0]
    tile = min(256, rows)
    chunk = 768
    shape = (tile, lat, factor, chunk, holders * piece_rows // chunk)
    group_spec = pl.BlockSpec((None, near.shape[1], width), lambda p, info: (info[5], 0, 0))
    return pl.pallas_call(
        functools.partial(first_body, shape, head_local, len(past)),
        grid_spec=pltpu.PrefetchScalarGridSpec(
            num_scalar_prefetch=1,
            grid=(1,),
            in_specs=[
                pl.BlockSpec((None, rows, width), lambda p, _: (0, 0, 0)),
                pl.BlockSpec(decode_query.shape, lambda p, _: (0, 0)),
                group_spec,
                group_spec,
                pl.BlockSpec(token.shape, lambda p, _: (0, 0)),
                pl.BlockSpec(fresh.shape, lambda p, _: (0, 0)),
            ]
            + [pl.BlockSpec(memory_space=pl.ANY)] * len(past),
            out_specs=[
                pl.BlockSpec((None, rows, lat), lambda p, _: (0, 0, 0)),
                pl.BlockSpec((decode_rows, lat), lambda p, _: (0, 0)),
                pl.BlockSpec((decode_rows, 128), lambda p, _: (0, 0)),
            ],
            scratch_shapes=[
                pltpu.VMEM((2, tile, keys), jnp.float32),
                pltpu.VMEM((holders, piece_rows, width), jnp.bfloat16),
                pltpu.SemaphoreType.DMA((32,)),
            ],
        ),
        out_shape=[
            jax.ShapeDtypeStruct((1, rows, lat), jnp.bfloat16),
            jax.ShapeDtypeStruct((decode_rows, lat), jnp.bfloat16),
            jax.ShapeDtypeStruct((decode_rows, 128), jnp.float32),
        ],
        compiler_params=pltpu.CompilerParams(vmem_limit_bytes=VMEM_BYTES),
        cost_estimate=pl.CostEstimate(
            flops=2 * (rows + decode_rows) * keys * (768 + lat),
            bytes_accessed=2 * (keys + 2 * rows + 2 * decode_rows) * width,
            transcendentals=(rows + decode_rows) * keys,
        ),
        name="attend_first",
    )(info, query, decode_query, near, far, token, fresh, *past)


def dispatch_body(source, length, q_ref, out_ref):
    slots, rows, width = out_ref.shape
    lat_rope = q_ref.shape[2]
    lane = lax.broadcasted_iota(jnp.int32, (rows, width - lat_rope), 1)
    for slot in range(slots):
        out_ref[slot, :, :lat_rope] = q_ref[source[slot]]
        size = length[slot]
        tail = jnp.where(lane < 32, size >> 4, size & 15)
        out_ref[slot, :, lat_rope:] = tail.astype(jnp.float32).astype(jnp.bfloat16)


def dispatch_queries(source, length, query, width):
    slots = source.shape[0]
    _, rows, _ = query.shape
    smem = pl.BlockSpec(memory_space=pltpu.SMEM)
    vmem = pl.BlockSpec(memory_space=pltpu.VMEM)
    return pl.pallas_call(
        dispatch_body,
        in_specs=[smem, smem, vmem],
        out_specs=vmem,
        out_shape=jax.ShapeDtypeStruct((slots, rows, width), jnp.bfloat16),
        compiler_params=pltpu.CompilerParams(vmem_limit_bytes=VMEM_BYTES),
        name="dispatch_queries",
    )(source, length, query)


def cache_body(lat, factor, batch, order, length, used, q_ref, *rest):
    pool_refs = rest[:batch]
    out_ref, lse_ref = rest[batch:]
    step = pl.program_id(0)
    rows = q_ref.shape[1]
    width, cache_rows = pool_refs[0].shape

    @pl.when(step * batch < used[0])
    def _():
        place = lax.broadcasted_iota(jnp.int32, (1, cache_rows), 1)
        lane = lax.broadcasted_iota(jnp.int32, (rows, lse_ref.shape[2]), 1)
        slots = [order[step * batch + b] for b in range(batch)]
        scores = [
            key_scores(q_ref[slots[b], :, :width], pool_refs[b][...], lat, NN)
            for b in range(batch)
        ]
        for b in range(batch):
            masked = jnp.where(place < length[slots[b]], scores[b], negative)
            peak = jnp.max(masked, axis=1, keepdims=True)
            weights = jnp.exp2((masked - peak) * factor)
            total = jnp.sum(weights, axis=1, keepdims=True)
            summed = dot(weights.astype(jnp.bfloat16), pool_refs[b][:lat], NT)
            out_ref[slots[b]] = (summed / total).astype(jnp.bfloat16)
            lse = peak * factor + jnp.log2(total)
            high = lse.astype(jnp.bfloat16).astype(jnp.float32)
            middle = (lse - high).astype(jnp.bfloat16).astype(jnp.float32)
            low = lse - high - middle
            lse_ref[slots[b]] = jnp.where(
                lane == 0, high, jnp.where(lane == 1, middle, low)
            ).astype(jnp.bfloat16)


def attend_cache(order, length, used, query, pool, lat, factor):
    batch = 4
    slots, rows, padded = query.shape
    _, width, cache_rows = pool.shape
    whole = pl.BlockSpec((slots, rows, padded), lambda i, *_: (0, 0, 0))

    def pool_spec(b):
        return pl.BlockSpec(
            (None, width, cache_rows), lambda i, order, *_: (order[i * batch + b], 0, 0)
        )

    return pl.pallas_call(
        functools.partial(cache_body, lat, factor, batch),
        grid_spec=pltpu.PrefetchScalarGridSpec(
            num_scalar_prefetch=3,
            grid=(slots // batch,),
            in_specs=[whole] + [pool_spec(b) for b in range(batch)],
            out_specs=[
                pl.BlockSpec((slots, rows, lat), lambda i, *_: (0, 0, 0)),
                pl.BlockSpec((slots, rows, 128), lambda i, *_: (0, 0, 0)),
            ],
        ),
        out_shape=[
            jax.ShapeDtypeStruct((slots, rows, lat), jnp.bfloat16),
            jax.ShapeDtypeStruct((slots, rows, 128), jnp.bfloat16),
        ],
        compiler_params=pltpu.CompilerParams(vmem_limit_bytes=VMEM_BYTES),
        cost_estimate=pl.CostEstimate(
            flops=2 * slots * 128 * cache_rows * (width + lat),
            bytes_accessed=2 * slots * cache_rows * width,
            transcendentals=slots * rows * cache_rows,
        ),
        name="attend_cache",
    )(order, length, used, query, *([pool] * batch))


def merge_body(slot, back_ref, near_ref, near_lse_ref, out_ref):
    count = near_ref.shape[0]
    width = near_ref.shape[2]
    for r in range(count):
        back = back_ref[slot[r]].astype(jnp.float32)
        far = back[:, :width]
        far_lse = back[:, width : width + 1] + back[:, width + 1 : width + 2]
        far_lse = far_lse + back[:, width + 2 : width + 3]
        near_lse = near_lse_ref[r][:, :1]
        peak = jnp.maximum(far_lse, near_lse)
        far_part = jnp.exp2(far_lse - peak)
        near_part = jnp.exp2(near_lse - peak)
        mixed = far * far_part + near_ref[r] * near_part
        out_ref[r] = (mixed / (far_part + near_part)).astype(jnp.bfloat16)


def merge_decode(slot, back, near, near_lse):
    smem = pl.BlockSpec(memory_space=pltpu.SMEM)
    vmem = pl.BlockSpec(memory_space=pltpu.VMEM)
    return pl.pallas_call(
        merge_body,
        in_specs=[smem, vmem, vmem, vmem],
        out_specs=vmem,
        out_shape=jax.ShapeDtypeStruct(near.shape, jnp.bfloat16),
        compiler_params=pltpu.CompilerParams(vmem_limit_bytes=VMEM_BYTES),
        name="merge_decode",
    )(slot, back, near, near_lse)


def swap_core(value):
    return lax.ppermute(value, "grp", [(0, 1), (1, 0)])


def fetch_tp(value, shift):
    return lax.ppermute(value, "tp", [((i + shift) % 4, i) for i in range(4)])


def fetch_x(value, shift):
    return lax.ppermute(
        value, "seq", [(i // 4 * 4 + (i + shift) % 4, i) for i in range(16)]
    )


def fetch_z(value, shift):
    return lax.ppermute(value, "seq", [((i + 4 * shift) % 16, i) for i in range(16)])


def on_device(
    group_hidden,
    group_query,
    past_cache,
    past_len,
    decode_hidden,
    decode_query,
    decode_pool,
    owner,
    dec_len,
    w_latent,
    kv_gain,
    w_value,
):
    seq_count = lax.axis_size("seq")
    seq_place = lax.axis_index("seq")
    tp_place = lax.axis_index("tp")
    core = lax.axis_index("grp")
    z_place, x_place = seq_place >> 2, seq_place & 3
    prompt_count, group_local, head_local, row_width = group_query.shape
    past_local = past_cache.shape[1]
    request_local = decode_query.shape[0]
    lat = kv_gain.shape[0]
    value_width = w_value.shape[2]
    slot_count = decode_pool.shape[0]
    pair_limit = slot_count // seq_count
    query_pairs = 2 * head_local
    factor = (value_width + row_width - lat) ** (-0.5) * log2_e

    half = past_local // 2
    past_half = lax.dynamic_slice_in_dim(past_cache, core * half, half, axis=1)
    past_later = lax.all_gather(past_half[1:], ("seq", "grp"), axis=0, tiled=False)
    past_x = [past_half[0]] + [fetch_x(past_half[0], shift) for shift in range(1, 4)]
    past_x = jnp.stack(past_x)
    past_first = [past_x] + [fetch_z(past_x, shift) for shift in range(1, 4)]
    past_first = past_first + [swap_core(piece) for piece in past_first]

    targets = owner[:, 0]
    request_order = jnp.arange(request_local, dtype=jnp.int32)
    earlier = (targets[:, None] == targets[None, :]) & (
        request_order[None, :] < request_order[:, None]
    )
    slot_rank = jnp.sum(earlier.astype(jnp.int32), axis=1)
    destination = targets * pair_limit + slot_rank
    matches = jnp.arange(slot_count, dtype=jnp.int32)[:, None] == destination[None, :]
    source = jnp.sum(jnp.where(matches, request_order[None, :], 0), axis=1)
    send_length = jnp.sum(jnp.where(matches, dec_len[None, :], 0), axis=1)
    send_query = dispatch_queries(
        source,
        send_length,
        decode_query.reshape(request_local, query_pairs, row_width),
        row_width + 64,
    )
    arrived = lax.all_to_all(
        send_query.reshape(seq_count, pair_limit * query_pairs, row_width + 64),
        "seq",
        split_axis=0,
        concat_axis=0,
        tiled=True,
    ).reshape(slot_count, query_pairs, row_width + 64)
    marks = arrived[:, 0, row_width:].astype(jnp.float32)
    slot_length = (marks[:, 0] * 16 + marks[:, 32]).astype(jnp.int32)

    half_tokens = group_local // 2
    pairs = 2 * request_local
    partial_group = jnp.einsum(
        "ptd,dc->ptc", group_hidden, w_latent, preferred_element_type=jnp.float32
    ).astype(jnp.bfloat16)
    partial_group = partial_group.reshape(prompt_count, 2, half_tokens, row_width)
    partial_decode = jnp.einsum(
        "rd,dc->rc",
        decode_hidden.reshape(pairs, -1),
        w_latent,
        preferred_element_type=jnp.float32,
    ).astype(jnp.bfloat16)
    keep = lax.dynamic_index_in_dim(partial_group, core, axis=1, keepdims=False)
    give = lax.dynamic_index_in_dim(partial_group, 1 - core, axis=1, keepdims=False)
    taken = swap_core(
        jnp.concatenate([give.reshape(prompt_count * half_tokens, row_width), partial_decode])
    ).astype(jnp.float32)
    sum_group = keep.astype(jnp.float32) + taken[: prompt_count * half_tokens].reshape(keep.shape)
    sum_decode = partial_decode.astype(jnp.float32) + taken[prompt_count * half_tokens :]
    sum_group = sum_group.astype(jnp.bfloat16)
    sum_decode = sum_decode.astype(jnp.bfloat16)

    def part_of(place):
        chosen = lax.dynamic_index_in_dim(sum_group, place & 3, axis=0, keepdims=False)
        return jnp.concatenate([chosen, sum_decode])

    latent = part_of(tp_place).astype(jnp.float32)
    for shift in range(1, 4):
        latent = latent + fetch_tp(part_of(tp_place - shift), shift).astype(jnp.float32)
    half_order = jnp.arange(half_tokens, dtype=jnp.int32)
    group_positions = (
        past_len[tp_place] + seq_place * group_local + core * half_tokens + half_order
    )
    pair_order = jnp.arange(pairs, dtype=jnp.int32)
    decode_positions = (
        past_len[0]
        + group_local * seq_count
        + (dec_len[:, None] + jnp.arange(2, dtype=jnp.int32)).reshape(-1)
    )
    positions = jnp.concatenate([group_positions, decode_positions])
    rows_own = make_rows(latent, kv_gain, positions)
    fresh = jnp.pad(rows_own[half_tokens:], ((0, 128 - pairs), (0, 0)))

    group_own = rows_own[:half_tokens]
    group_x = jnp.stack([group_own] + [fetch_x(group_own, shift) for shift in range(1, 4)])
    group_z = jnp.stack([group_x] + [fetch_z(group_x, shift) for shift in range(1, 4)])
    group_z = group_z.reshape(seq_count * half_tokens, row_width)
    group_near = jnp.stack([group_z] + [fetch_tp(group_z, shift) for shift in range(1, 4)])
    group_far = swap_core(group_near)
    ring = jnp.arange(4, dtype=jnp.int32)
    holder = ((z_place + ring) & 3)[:, None] * 4 + ((x_place + ring) & 3)[None, :]
    key_token = holder.reshape(seq_count, 1) * group_local + half_order[None, :]
    key_token = key_token.reshape(1, seq_count * half_tokens)
    key_token = jnp.concatenate(
        [key_token + core * half_tokens, key_token + (1 - core) * half_tokens], axis=0
    )

    is_used = slot_length > 0
    used_rank = jnp.cumsum(is_used.astype(jnp.int32)) - 1
    used = jnp.sum(is_used.astype(jnp.int32))
    slots = jnp.arange(slot_count, dtype=jnp.int32)
    wanted = jnp.minimum(slots, jnp.maximum(used - 1, 0))
    order = jnp.sum(
        jnp.where(is_used[None, :] & (used_rank[None, :] == wanted[:, None]), slots[None, :], 0),
        axis=1,
    )
    cache_latent, cache_lse = attend_cache(
        order, slot_length, used.reshape(1), arrived, jnp.swapaxes(decode_pool, 1, 2), lat, factor
    )
    cache_value = jnp.einsum(
        "nshc,hcv->nshv",
        cache_latent.reshape(slot_count, 2, head_local, lat),
        w_value,
        preferred_element_type=jnp.float32,
    ).astype(jnp.bfloat16)
    back = jnp.concatenate(
        [cache_value.reshape(slot_count, query_pairs, value_width), cache_lse], axis=-1
    )
    back = lax.all_to_all(
        back.reshape(seq_count, pair_limit * query_pairs, 2 * value_width),
        "seq",
        split_axis=0,
        concat_axis=0,
        tiled=True,
    ).reshape(slot_count, query_pairs, 2 * value_width)

    info = jnp.stack(
        [past_len[p] for p in range(prompt_count)]
        + [seq_place * group_local, (4 - tp_place) & 3, z_place, x_place, core]
    ).astype(jnp.int32)
    queries = group_query.reshape(prompt_count, group_local * head_local, row_width)
    first_latent, near_latent, near_lse = attend_first(
        info,
        queries,
        decode_query.reshape(request_local * query_pairs, row_width),
        past_first,
        group_near,
        group_far,
        key_token,
        fresh,
        lat,
        factor,
        head_local,
    )
    near = jnp.einsum(
        "rshc,hcv->rshv",
        near_latent.reshape(request_local, 2, head_local, lat),
        w_value,
        preferred_element_type=jnp.float32,
    )
    decode_out = merge_decode(
        destination,
        back,
        near.reshape(request_local, query_pairs, value_width),
        near_lse.reshape(request_local, query_pairs, 128),
    ).reshape(request_local, 2, head_local, value_width)

    later_latent = attend_later(
        info, queries, past_later, group_near, group_far, key_token, 1, lat, factor, head_local
    )
    prefill_latent = jnp.concatenate([first_latent, later_latent], axis=0)
    prefill_out = jnp.einsum(
        "pthc,hcv->pthv",
        prefill_latent.reshape(prompt_count, group_local, head_local, lat),
        w_value,
        preferred_element_type=jnp.float32,
    ).astype(jnp.bfloat16)
    return (prefill_out, decode_out)


def solution(mesh):
    in_specs = (
        P(None, "seq", ("tp", "grp")),
        P(None, "seq", ("tp", "grp"), None),
        P(None, "seq", None),
        P(),
        P("seq", None, ("tp", "grp")),
        P("seq", None, ("tp", "grp"), None),
        P("seq", None, None),
        P("seq", None),
        P("seq"),
        P(("tp", "grp"), None),
        P(),
        P(("tp", "grp"), None, None),
    )
    out_specs = (P(None, "seq", ("tp", "grp"), None), P("seq", None, ("tp", "grp"), None))
    return jax.shard_map(
        on_device, mesh=mesh, in_specs=in_specs, out_specs=out_specs, check_vma=False
    )
```

```python
import functools

import jax
import jax.numpy as jnp
from jax import lax
from jax.experimental import pallas as pl
from jax.experimental.pallas import tpu as pltpu
from jax.sharding import PartitionSpec as P

epsilon = 1e-06
negative = -1e30
log2_e = 1.4426950408889634
NT = (((1,), (1,)), ((), ()))
NN = (((1,), (0,)), ((), ()))
VMEM_BYTES = 56 * 2**20


def rotate(rope_part, positions):
    half_width = rope_part.shape[-1] // 2
    frequency = jnp.exp(-jnp.log(10000.0) * jnp.arange(half_width).astype(jnp.float32) / half_width)
    angles = positions.astype(jnp.float32)[..., None] * frequency
    cosine = jnp.cos(angles)
    sine_part = jnp.sin(angles)
    former = rope_part[..., :half_width]
    latter = rope_part[..., half_width:]
    return jnp.concatenate(
        [former * cosine - latter * sine_part, latter * cosine + former * sine_part], axis=-1
    )


def make_rows(latent, kv_gain, positions):
    lat_width = kv_gain.shape[0]
    latent_part = latent[..., :lat_width]
    spread = jnp.mean(latent_part * latent_part, axis=-1, keepdims=True)
    normed = latent_part * lax.rsqrt(spread + epsilon) * kv_gain
    return jnp.concatenate([normed, rotate(latent[..., lat_width:], positions)], axis=-1).astype(
        jnp.bfloat16
    )


def dot(left, right, dims):
    return lax.dot_general(left, right, dims, preferred_element_type=jnp.float32)


def key_scores(queries, keys, lat, dims):
    if dims is NT:
        return dot(queries[:, :lat], keys[:, :lat], NT) + dot(queries[:, lat:], keys[:, lat:], NT)
    return dot(queries[:, :lat], keys[:lat], NN) + dot(queries[:, lat:], keys[lat:], NN)


def lane_fold(op, total, block):
    for start in range(0, block.shape[1], 128):
        part = block[:, start : start + 128]
        total = part if total is None else op(total, part)
    return total


def attend_rows(shape, q_ref, out_ref, lse_ref, hold, past_keys, past_len, others, row_masks):
    tile, lat, factor, chunk, past_count = shape
    rows = q_ref.shape[0]
    for i in range(rows // tile):
        span = pl.ds(i * tile, tile)
        queries = q_ref[span, :]
        row = lax.broadcasted_iota(jnp.int32, (tile, 1), 0) + i * tile
        highest = None
        parts = []
        end = 0
        for j in range(past_count + len(others)):
            keys = functools.partial(past_keys, j) if j < past_count else others[j - past_count]
            block = keys()
            scores = key_scores(queries, block, lat, NT)
            if j >= past_count:
                mask = row_masks[j - past_count](row)
                if mask is not None:
                    scores = jnp.where(mask, scores, negative)
            elif (j + 1) * chunk > past_count * chunk // 2:
                place = lax.broadcasted_iota(jnp.int32, (1, chunk), 1) + j * chunk
                scores = jnp.where(place < past_len, scores, negative)
            place = slice(end, end + block.shape[0])
            end += block.shape[0]
            parts.append((place, keys))
            hold[i % 2, :, place] = scores
            highest = lane_fold(jnp.maximum, highest, scores)
        peak = jnp.max(highest, axis=1, keepdims=True)
        total = None
        summed = None
        for place, keys in parts:
            weights = jnp.exp2((hold[i % 2, :, place] - peak) * factor)
            total = lane_fold(jnp.add, total, weights)
            part = dot(weights.astype(jnp.bfloat16), keys()[:, :lat], NN)
            summed = part if summed is None else summed + part
        total = jnp.sum(total, axis=1, keepdims=True)
        out_ref[span, :] = (summed / total).astype(jnp.bfloat16)
        if lse_ref is not None:
            lse = peak * factor + jnp.log2(total)
            lse_ref[span, :] = jnp.broadcast_to(lse, (tile, lse_ref.shape[1]))


def pair_body(shape, head_local, first, info, q_ref, *rest):
    chunk, past_count = shape[3:]
    decode = first == 0
    if decode:
        dq_ref, fresh_ref = rest[:2]
        rest = rest[2:]
    piece_refs = rest[:8]
    if decode:
        out_ref, decode_ref, lse_ref = rest[8:11]
        rest = rest[11:]
    else:
        out_ref = rest[8]
        rest = rest[9:]
    hold, past, group, past_arrive, group_arrive = rest
    count, holders, piece_rows, width = past.shape
    group_rows = group.shape[2]
    step = holders // past_count
    z_place, x_place, core = info[5], info[6], info[7]
    copies = []
    for p in range(count):
        copies.append([])
        for c in range(2):
            side = core if c == 0 else 1 - core
            for s in range(4):
                for j in range(4):
                    dz = s + (j - s) * side
                    dx = j + (s - j) * side
                    holder = ((z_place + dz) & 3) * 4 + ((x_place + dx) & 3)
                    place = holder * 2 + side
                    number = c * 16 + s * 4 + j
                    piece = piece_refs[c * 4 + s]
                    copies[p].append(
                        pltpu.make_async_copy(
                            piece.at[j, p, pl.ds(0, piece_rows)],
                            past.at[p, place],
                            past_arrive.at[p, number],
                        )
                    )
                    copies[p].append(
                        pltpu.make_async_copy(
                            piece.at[j, p, pl.ds(piece_rows, group_rows)],
                            group.at[p, place],
                            group_arrive.at[p, number],
                        )
                    )
    for p in range(count):
        for copy in copies[p]:
            copy.start()

    def group_mask(row):
        place = lax.broadcasted_iota(jnp.int32, (1, holders * group_rows), 1)
        return place <= info[4] + row // head_local

    def fresh_mask(row):
        place = lax.broadcasted_iota(jnp.int32, (1, fresh_ref.shape[0]), 1)
        return (place >= row // (2 * head_local) * 2) & (place <= row // head_local)

    for p in range(count):
        for copy in copies[p]:
            copy.wait()

        def past_keys(j, p=p):
            return past[p, j * step : (j + 1) * step].reshape(chunk, width)

        def group_keys(p=p):
            return group[p].reshape(holders * group_rows, width)

        if decode and p == 0:
            attend_rows(
                shape,
                dq_ref,
                decode_ref,
                lse_ref,
                hold,
                past_keys,
                info[0],
                [group_keys, lambda: fresh_ref[...]],
                [lambda row: None, fresh_mask],
            )
        attend_rows(
            shape,
            q_ref.at[p],
            out_ref.at[p],
            None,
            hold,
            past_keys,
            info[first + p],
            [group_keys],
            [group_mask],
        )


def attend_pair(info, query, pieces, first, piece_rows, decode_query, fresh, lat, factor, head_local):
    decode = first == 0
    _, rows, width = query.shape
    count = pieces[0].shape[1]
    group_rows = pieces[0].shape[2] - piece_rows
    holders = 2 * 16
    keys = holders * (piece_rows + group_rows)
    tile = min(256, rows)
    chunk = 768
    shape = (tile, lat, factor, chunk, holders * piece_rows // chunk)
    in_specs = [pl.BlockSpec((count, rows, width), lambda p, _: (first // count, 0, 0))]
    operands = [query]
    out_specs = [pl.BlockSpec((count, rows, lat), lambda p, _: (0, 0, 0))]
    out_shape = [jax.ShapeDtypeStruct((count, rows, lat), jnp.bfloat16)]
    blocks = count
    most_keys = keys
    if decode:
        decode_rows = decode_query.shape[0]
        in_specs += [
            pl.BlockSpec(decode_query.shape, lambda p, _: (0, 0)),
            pl.BlockSpec(fresh.shape, lambda p, _: (0, 0)),
        ]
        operands += [decode_query, fresh]
        out_specs += [
            pl.BlockSpec((decode_rows, lat), lambda p, _: (0, 0)),
            pl.BlockSpec((decode_rows, 128), lambda p, _: (0, 0)),
        ]
        out_shape += [
            jax.ShapeDtypeStruct((decode_rows, lat), jnp.bfloat16),
            jax.ShapeDtypeStruct((decode_rows, 128), jnp.float32),
        ]
        blocks += 1
        most_keys += fresh.shape[0]
    in_specs += [pl.BlockSpec(memory_space=pl.ANY)] * len(pieces)
    return pl.pallas_call(
        functools.partial(pair_body, shape, head_local, first),
        grid_spec=pltpu.PrefetchScalarGridSpec(
            num_scalar_prefetch=1,
            grid=(1,),
            in_specs=in_specs,
            out_specs=out_specs,
            scratch_shapes=[
                pltpu.VMEM((2, tile, most_keys), jnp.float32),
                pltpu.VMEM((count, holders, piece_rows, width), jnp.bfloat16),
                pltpu.VMEM((count, holders, group_rows, width), jnp.bfloat16),
                pltpu.SemaphoreType.DMA((count, holders)),
                pltpu.SemaphoreType.DMA((count, holders)),
            ],
        ),
        out_shape=out_shape,
        compiler_params=pltpu.CompilerParams(vmem_limit_bytes=VMEM_BYTES),
        cost_estimate=pl.CostEstimate(
            flops=2 * blocks * rows * keys * (768 + lat),
            bytes_accessed=2 * (count * keys + 2 * blocks * rows) * width,
            transcendentals=blocks * rows * keys,
        ),
        name="attend_first" if decode else "attend_later",
    )(info, *operands, *pieces)


def dispatch_body(source, length, q_ref, out_ref):
    slots, rows, width = out_ref.shape
    lat_rope = q_ref.shape[2]
    lane = lax.broadcasted_iota(jnp.int32, (rows, width - lat_rope), 1)
    for slot in range(slots):
        out_ref[slot, :, :lat_rope] = q_ref[source[slot]]
        size = length[slot]
        tail = jnp.where(lane < 32, size >> 4, size & 15)
        out_ref[slot, :, lat_rope:] = tail.astype(jnp.float32).astype(jnp.bfloat16)


def dispatch_queries(source, length, query, width):
    slots = source.shape[0]
    _, rows, _ = query.shape
    smem = pl.BlockSpec(memory_space=pltpu.SMEM)
    vmem = pl.BlockSpec(memory_space=pltpu.VMEM)
    return pl.pallas_call(
        dispatch_body,
        in_specs=[smem, smem, vmem],
        out_specs=vmem,
        out_shape=jax.ShapeDtypeStruct((slots, rows, width), jnp.bfloat16),
        compiler_params=pltpu.CompilerParams(vmem_limit_bytes=VMEM_BYTES),
        name="dispatch_queries",
    )(source, length, query)


def cache_body(lat, factor, batch, order, length, used, q_ref, *rest):
    pool_refs = rest[:batch]
    out_ref, lse_ref = rest[batch:]
    step = pl.program_id(0)
    rows = q_ref.shape[1]
    width, cache_rows = pool_refs[0].shape

    @pl.when(step * batch < used[0])
    def _():
        place = lax.broadcasted_iota(jnp.int32, (1, cache_rows), 1)
        lane = lax.broadcasted_iota(jnp.int32, (rows, lse_ref.shape[2]), 1)
        slots = [order[step * batch + b] for b in range(batch)]
        scores = [
            key_scores(q_ref[slots[b], :, :width], pool_refs[b][...], lat, NN)
            for b in range(batch)
        ]
        for b in range(batch):
            masked = jnp.where(place < length[slots[b]], scores[b], negative)
            peak = jnp.max(masked, axis=1, keepdims=True)
            weights = jnp.exp2((masked - peak) * factor)
            total = jnp.sum(weights, axis=1, keepdims=True)
            summed = dot(weights.astype(jnp.bfloat16), pool_refs[b][:lat], NT)
            out_ref[slots[b]] = (summed / total).astype(jnp.bfloat16)
            lse = peak * factor + jnp.log2(total)
            high = lse.astype(jnp.bfloat16).astype(jnp.float32)
            middle = (lse - high).astype(jnp.bfloat16).astype(jnp.float32)
            low = lse - high - middle
            lse_ref[slots[b]] = jnp.where(
                lane == 0, high, jnp.where(lane == 1, middle, low)
            ).astype(jnp.bfloat16)


def attend_cache(order, length, used, query, pool, lat, factor):
    batch = 4
    slots, rows, padded = query.shape
    _, width, cache_rows = pool.shape
    whole = pl.BlockSpec((slots, rows, padded), lambda i, *_: (0, 0, 0))

    def pool_spec(b):
        return pl.BlockSpec(
            (None, width, cache_rows), lambda i, order, *_: (order[i * batch + b], 0, 0)
        )

    return pl.pallas_call(
        functools.partial(cache_body, lat, factor, batch),
        grid_spec=pltpu.PrefetchScalarGridSpec(
            num_scalar_prefetch=3,
            grid=(slots // batch,),
            in_specs=[whole] + [pool_spec(b) for b in range(batch)],
            out_specs=[
                pl.BlockSpec((slots, rows, lat), lambda i, *_: (0, 0, 0)),
                pl.BlockSpec((slots, rows, 128), lambda i, *_: (0, 0, 0)),
            ],
        ),
        out_shape=[
            jax.ShapeDtypeStruct((slots, rows, lat), jnp.bfloat16),
            jax.ShapeDtypeStruct((slots, rows, 128), jnp.bfloat16),
        ],
        compiler_params=pltpu.CompilerParams(vmem_limit_bytes=VMEM_BYTES),
        cost_estimate=pl.CostEstimate(
            flops=2 * slots * 128 * cache_rows * (width + lat),
            bytes_accessed=2 * slots * cache_rows * width,
            transcendentals=slots * rows * cache_rows,
        ),
        name="attend_cache",
    )(order, length, used, query, *([pool] * batch))


def merge_body(slot, back_ref, near_ref, near_lse_ref, out_ref):
    count = near_ref.shape[0]
    width = near_ref.shape[2]
    for r in range(count):
        back = back_ref[slot[r]].astype(jnp.float32)
        far = back[:, :width]
        far_lse = back[:, width : width + 1] + back[:, width + 1 : width + 2]
        far_lse = far_lse + back[:, width + 2 : width + 3]
        near_lse = near_lse_ref[r][:, :1]
        peak = jnp.maximum(far_lse, near_lse)
        far_part = jnp.exp2(far_lse - peak)
        near_part = jnp.exp2(near_lse - peak)
        mixed = far * far_part + near_ref[r] * near_part
        out_ref[r] = (mixed / (far_part + near_part)).astype(jnp.bfloat16)


def merge_decode(slot, back, near, near_lse):
    smem = pl.BlockSpec(memory_space=pltpu.SMEM)
    vmem = pl.BlockSpec(memory_space=pltpu.VMEM)
    return pl.pallas_call(
        merge_body,
        in_specs=[smem, vmem, vmem, vmem],
        out_specs=vmem,
        out_shape=jax.ShapeDtypeStruct(near.shape, jnp.bfloat16),
        compiler_params=pltpu.CompilerParams(vmem_limit_bytes=VMEM_BYTES),
        name="merge_decode",
    )(slot, back, near, near_lse)


def swap_core(value):
    return lax.ppermute(value, "grp", [(0, 1), (1, 0)])


def fetch_tp(value, shift):
    return lax.ppermute(value, "tp", [((i + shift) % 4, i) for i in range(4)])


def fetch_ring(value, shift, turn):
    moves = []
    for i in range(16):
        z, x = i // 4, i % 4
        for c in range(2):
            if (c + turn) % 2 == 0:
                origin = z * 4 + (x + shift) % 4
            else:
                origin = (z + shift) % 4 * 4 + x
            moves.append((origin * 2 + c, i * 2 + c))
    return lax.ppermute(value, ("seq", "grp"), moves)


def on_device(
    group_hidden,
    group_query,
    past_cache,
    past_len,
    decode_hidden,
    decode_query,
    decode_pool,
    owner,
    dec_len,
    w_latent,
    kv_gain,
    w_value,
):
    seq_count = lax.axis_size("seq")
    seq_place = lax.axis_index("seq")
    core = lax.axis_index("grp")
    z_place, x_place = seq_place >> 2, seq_place & 3
    prompt_count, group_local, head_local, row_width = group_query.shape
    past_local = past_cache.shape[1]
    request_local = decode_query.shape[0]
    lat = kv_gain.shape[0]
    value_width = w_value.shape[2]
    slot_count = decode_pool.shape[0]
    pair_limit = slot_count // seq_count
    query_pairs = 2 * head_local
    factor = (value_width + row_width - lat) ** (-0.5) * log2_e

    half = past_local // 2
    past_half = lax.dynamic_slice_in_dim(past_cache, core * half, half, axis=1)
    past_line = [past_half] + [fetch_ring(past_half, shift, 0) for shift in range(1, 4)]

    targets = owner[:, 0]
    request_order = jnp.arange(request_local, dtype=jnp.int32)
    earlier = (targets[:, None] == targets[None, :]) & (
        request_order[None, :] < request_order[:, None]
    )
    slot_rank = jnp.sum(earlier.astype(jnp.int32), axis=1)
    destination = targets * pair_limit + slot_rank
    matches = jnp.arange(slot_count, dtype=jnp.int32)[:, None] == destination[None, :]
    source = jnp.sum(jnp.where(matches, request_order[None, :], 0), axis=1)
    send_length = jnp.sum(jnp.where(matches, dec_len[None, :], 0), axis=1)
    send_query = dispatch_queries(
        source,
        send_length,
        decode_query.reshape(request_local, query_pairs, row_width),
        row_width + 64,
    )
    arrived = lax.all_to_all(
        send_query.reshape(seq_count, pair_limit * query_pairs, row_width + 64),
        "seq",
        split_axis=0,
        concat_axis=0,
        tiled=True,
    ).reshape(slot_count, query_pairs, row_width + 64)
    marks = arrived[:, 0, row_width:].astype(jnp.float32)
    slot_length = (marks[:, 0] * 16 + marks[:, 32]).astype(jnp.int32)

    half_tokens = group_local // 2
    pairs = 2 * request_local
    partial_group = jnp.einsum(
        "ptd,dc->ptc", group_hidden, w_latent, preferred_element_type=jnp.float32
    ).astype(jnp.bfloat16)
    partial_group = partial_group.reshape(prompt_count, 2, half_tokens, row_width)
    partial_decode = jnp.einsum(
        "rd,dc->rc",
        decode_hidden.reshape(pairs, -1),
        w_latent,
        preferred_element_type=jnp.float32,
    ).astype(jnp.bfloat16)
    group_part = prompt_count * half_tokens

    def both(chosen):
        part = lax.dynamic_index_in_dim(partial_group, chosen, axis=1, keepdims=False)
        return jnp.concatenate([part.reshape(group_part, row_width), partial_decode])

    pair_sum = both(core).astype(jnp.float32) + swap_core(both(1 - core)).astype(jnp.float32)
    pair_sum = pair_sum.astype(jnp.bfloat16)
    latent = pair_sum.astype(jnp.float32)
    for shift in range(1, 4):
        latent = latent + fetch_tp(pair_sum, shift).astype(jnp.float32)
    half_order = jnp.arange(half_tokens, dtype=jnp.int32)
    group_positions = (
        past_len[:, None] + seq_place * group_local + core * half_tokens + half_order[None, :]
    )
    decode_positions = (
        past_len[0]
        + group_local * seq_count
        + (dec_len[:, None] + jnp.arange(2, dtype=jnp.int32)).reshape(-1)
    )
    positions = jnp.concatenate([group_positions.reshape(-1), decode_positions])
    rows_own = make_rows(latent, kv_gain, positions)
    fresh = jnp.pad(rows_own[group_part:], ((0, 128 - pairs), (0, 0)))

    group_own = rows_own[:group_part].reshape(prompt_count, half_tokens, row_width)
    group_line = [group_own] + [fetch_ring(group_own, shift, 0) for shift in range(1, 4)]
    pieces = []
    for first in range(0, prompt_count, 2):
        line = jnp.stack(
            [
                jnp.concatenate([old[first : first + 2], new[first : first + 2]], axis=1)
                for old, new in zip(past_line, group_line)
            ]
        )
        lines = [line] + [fetch_ring(line, shift, 1) for shift in range(1, 4)]
        pieces.append(lines + [swap_core(piece) for piece in lines])

    is_used = slot_length > 0
    used_rank = jnp.cumsum(is_used.astype(jnp.int32)) - 1
    used = jnp.sum(is_used.astype(jnp.int32))
    slots = jnp.arange(slot_count, dtype=jnp.int32)
    wanted = jnp.minimum(slots, jnp.maximum(used - 1, 0))
    order = jnp.sum(
        jnp.where(is_used[None, :] & (used_rank[None, :] == wanted[:, None]), slots[None, :], 0),
        axis=1,
    )
    cache_latent, cache_lse = attend_cache(
        order, slot_length, used.reshape(1), arrived, jnp.swapaxes(decode_pool, 1, 2), lat, factor
    )
    cache_value = jnp.einsum(
        "nshc,hcv->nshv",
        cache_latent.reshape(slot_count, 2, head_local, lat),
        w_value,
        preferred_element_type=jnp.float32,
    ).astype(jnp.bfloat16)
    back = jnp.concatenate(
        [cache_value.reshape(slot_count, query_pairs, value_width), cache_lse], axis=-1
    )
    back = lax.all_to_all(
        back.reshape(seq_count, pair_limit * query_pairs, 2 * value_width),
        "seq",
        split_axis=0,
        concat_axis=0,
        tiled=True,
    ).reshape(slot_count, query_pairs, 2 * value_width)

    info = jnp.stack(
        [past_len[p] for p in range(prompt_count)]
        + [seq_place * group_local, z_place, x_place, core]
    ).astype(jnp.int32)
    queries = group_query.reshape(prompt_count, group_local * head_local, row_width)
    first_latent, near_latent, near_lse = attend_pair(
        info,
        queries,
        pieces[0],
        0,
        half,
        decode_query.reshape(request_local * query_pairs, row_width),
        fresh,
        lat,
        factor,
        head_local,
    )
    near = jnp.einsum(
        "rshc,hcv->rshv",
        near_latent.reshape(request_local, 2, head_local, lat),
        w_value,
        preferred_element_type=jnp.float32,
    )
    decode_out = merge_decode(
        destination,
        back,
        near.reshape(request_local, query_pairs, value_width),
        near_lse.reshape(request_local, query_pairs, 128),
    ).reshape(request_local, 2, head_local, value_width)

    (later_latent,) = attend_pair(
        info, queries, pieces[1], 2, half, None, None, lat, factor, head_local
    )
    prefill_latent = jnp.concatenate([first_latent, later_latent], axis=0)
    prefill_out = jnp.einsum(
        "pthc,hcv->pthv",
        prefill_latent.reshape(prompt_count, group_local, head_local, lat),
        w_value,
        preferred_element_type=jnp.float32,
    ).astype(jnp.bfloat16)
    return (prefill_out, decode_out)


def solution(mesh):
    in_specs = (
        P(None, "seq", ("tp", "grp")),
        P(None, "seq", ("tp", "grp"), None),
        P(None, "seq", None),
        P(),
        P("seq", None, ("tp", "grp")),
        P("seq", None, ("tp", "grp"), None),
        P("seq", None, None),
        P("seq", None),
        P("seq"),
        P(("tp", "grp"), None),
        P(),
        P(("tp", "grp"), None, None),
    )
    out_specs = (P(None, "seq", ("tp", "grp"), None), P("seq", None, ("tp", "grp"), None))
    return jax.shard_map(
        on_device, mesh=mesh, in_specs=in_specs, out_specs=out_specs, check_vma=False
    )
```

```python
import functools

import jax
import jax.numpy as jnp
from jax import lax
from jax.experimental import pallas as pl
from jax.experimental.pallas import tpu as pltpu
from jax.sharding import PartitionSpec as P

epsilon = 1e-06
negative = -1e30
log2_e = 1.4426950408889634
NT = (((1,), (1,)), ((), ()))
NN = (((1,), (0,)), ((), ()))
VMEM_BYTES = 56 * 2**20


def rotate(rope_part, positions):
    half_width = rope_part.shape[-1] // 2
    frequency = jnp.exp(-jnp.log(10000.0) * jnp.arange(half_width).astype(jnp.float32) / half_width)
    angles = positions.astype(jnp.float32)[..., None] * frequency
    cosine = jnp.cos(angles)
    sine_part = jnp.sin(angles)
    former = rope_part[..., :half_width]
    latter = rope_part[..., half_width:]
    return jnp.concatenate(
        [former * cosine - latter * sine_part, latter * cosine + former * sine_part], axis=-1
    )


def make_rows(latent, kv_gain, positions):
    lat_width = kv_gain.shape[0]
    latent_part = latent[..., :lat_width]
    spread = jnp.mean(latent_part * latent_part, axis=-1, keepdims=True)
    normed = latent_part * lax.rsqrt(spread + epsilon) * kv_gain
    return jnp.concatenate([normed, rotate(latent[..., lat_width:], positions)], axis=-1).astype(
        jnp.bfloat16
    )


def dot(left, right, dims):
    return lax.dot_general(left, right, dims, preferred_element_type=jnp.float32)


def key_scores(queries, keys, lat, dims):
    if dims is NT:
        return dot(queries[:, :lat], keys[:, :lat], NT) + dot(queries[:, lat:], keys[:, lat:], NT)
    return dot(queries[:, :lat], keys[:lat], NN) + dot(queries[:, lat:], keys[lat:], NN)


def lane_fold(op, total, block):
    for start in range(0, block.shape[1], 128):
        part = block[:, start : start + 128]
        total = part if total is None else op(total, part)
    return total


def attend_rows(shape, q_ref, out_ref, lse_ref, hold, past_keys, past_len, others, row_masks):
    tile, lat, factor, chunk, past_count = shape
    rows = q_ref.shape[0]
    for i in range(rows // tile):
        span = pl.ds(i * tile, tile)
        queries = q_ref[span, :]
        row = lax.broadcasted_iota(jnp.int32, (tile, 1), 0) + i * tile
        highest = None
        parts = []
        end = 0
        for j in range(past_count + len(others)):
            keys = functools.partial(past_keys, j) if j < past_count else others[j - past_count]
            block = keys()
            scores = key_scores(queries, block, lat, NT)
            if j >= past_count:
                mask = row_masks[j - past_count](row)
                if mask is not None:
                    scores = jnp.where(mask, scores, negative)
            elif (j + 1) * chunk > past_count * chunk // 2:
                place = lax.broadcasted_iota(jnp.int32, (1, chunk), 1) + j * chunk
                scores = jnp.where(place < past_len, scores, negative)
            place = slice(end, end + block.shape[0])
            end += block.shape[0]
            parts.append((place, keys))
            hold[i % 2, :, place] = scores
            highest = lane_fold(jnp.maximum, highest, scores)
        peak = jnp.max(highest, axis=1, keepdims=True)
        total = None
        summed = None
        for place, keys in parts:
            weights = jnp.exp2((hold[i % 2, :, place] - peak) * factor)
            total = lane_fold(jnp.add, total, weights)
            part = dot(weights.astype(jnp.bfloat16), keys()[:, :lat], NN)
            summed = part if summed is None else summed + part
        total = jnp.sum(total, axis=1, keepdims=True)
        out_ref[span, :] = (summed / total).astype(jnp.bfloat16)
        if lse_ref is not None:
            lse = peak * factor + jnp.log2(total)
            lse_ref[span, :] = jnp.broadcast_to(lse, (tile, lse_ref.shape[1]))


def pair_body(shape, head_local, first, lines, info, q_ref, *rest):
    chunk, past_count = shape[3:]
    decode = first == 0
    if decode:
        dq_ref, fresh_ref = rest[:2]
        rest = rest[2:]
    piece_refs = rest[:8]
    rest = rest[8:]
    if not lines:
        whole_ref = rest[0]
        rest = rest[1:]
    out_ref = rest[0]
    rest = rest[1:]
    if decode:
        decode_ref, lse_ref = rest[:2]
        rest = rest[2:]
    hold, past, group, past_arrive, group_arrive = rest
    count, holders, piece_blocks, group_rows, width = past.shape
    step = holders // past_count
    z_place, x_place, core = info[5], info[6], info[7]
    copies = []
    for p in range(count):
        copies.append([])
        if not lines:
            copies[p].append(
                pltpu.make_async_copy(whole_ref.at[:, p], past.at[p], past_arrive.at[p, 0])
            )
        for c in range(2):
            side = core if c == 0 else 1 - core
            for s in range(4):
                for j in range(4):
                    dz = s + (j - s) * side
                    dx = j + (s - j) * side
                    holder = ((z_place + dz) & 3) * 4 + ((x_place + dx) & 3)
                    place = holder * 2 + side
                    number = c * 16 + s * 4 + j
                    piece = piece_refs[c * 4 + s]
                    if lines:
                        copies[p].append(
                            pltpu.make_async_copy(
                                piece.at[j, pl.ds(p * piece_blocks, piece_blocks)],
                                past.at[p, place],
                                past_arrive.at[p, number],
                            )
                        )
                    copies[p].append(
                        pltpu.make_async_copy(
                            piece.at[j, 2 * piece_blocks + first + p],
                            group.at[p, place],
                            group_arrive.at[p, number],
                        )
                    )
    for p in range(count):
        for copy in copies[p]:
            copy.start()

    def group_mask(row):
        place = lax.broadcasted_iota(jnp.int32, (1, holders * group_rows), 1)
        return place <= info[4] + row // head_local

    def fresh_mask(row):
        place = lax.broadcasted_iota(jnp.int32, (1, fresh_ref.shape[0]), 1)
        return (place >= row // (2 * head_local) * 2) & (place <= row // head_local)

    for p in range(count):
        for copy in copies[p]:
            copy.wait()

        def past_keys(j, p=p):
            return past[p, j * step : (j + 1) * step].reshape(chunk, width)

        def group_keys(p=p):
            return group[p].reshape(holders * group_rows, width)

        if decode and p == 0:
            attend_rows(
                shape,
                dq_ref,
                decode_ref,
                lse_ref,
                hold,
                past_keys,
                info[0],
                [group_keys, lambda: fresh_ref[...]],
                [lambda row: None, fresh_mask],
            )
        attend_rows(
            shape,
            q_ref.at[p],
            out_ref.at[p],
            None,
            hold,
            past_keys,
            info[first + p],
            [group_keys],
            [group_mask],
        )


def attend_pair(
    info, query, pieces, whole, first, piece_rows, decode_query, fresh, lat, factor, head_local
):
    decode = first == 0
    _, rows, width = query.shape
    count = 2
    group_rows = pieces[0].shape[2]
    holders = 2 * 16
    keys = holders * (piece_rows + group_rows)
    tile = min(256, rows)
    chunk = 768
    shape = (tile, lat, factor, chunk, holders * piece_rows // chunk)
    in_specs = [pl.BlockSpec((count, rows, width), lambda p, _: (first // count, 0, 0))]
    operands = [query]
    out_specs = [pl.BlockSpec((count, rows, lat), lambda p, _: (0, 0, 0))]
    out_shape = [jax.ShapeDtypeStruct((count, rows, lat), jnp.bfloat16)]
    blocks = count
    most_keys = keys
    if decode:
        decode_rows = decode_query.shape[0]
        in_specs += [
            pl.BlockSpec(decode_query.shape, lambda p, _: (0, 0)),
            pl.BlockSpec(fresh.shape, lambda p, _: (0, 0)),
        ]
        operands += [decode_query, fresh]
        out_specs += [
            pl.BlockSpec((decode_rows, lat), lambda p, _: (0, 0)),
            pl.BlockSpec((decode_rows, 128), lambda p, _: (0, 0)),
        ]
        out_shape += [
            jax.ShapeDtypeStruct((decode_rows, lat), jnp.bfloat16),
            jax.ShapeDtypeStruct((decode_rows, 128), jnp.float32),
        ]
        blocks += 1
        most_keys += fresh.shape[0]
    far = list(pieces) + ([] if whole is None else [whole])
    in_specs += [pl.BlockSpec(memory_space=pl.ANY)] * len(far)
    return pl.pallas_call(
        functools.partial(pair_body, shape, head_local, first, whole is None),
        grid_spec=pltpu.PrefetchScalarGridSpec(
            num_scalar_prefetch=1,
            grid=(1,),
            in_specs=in_specs,
            out_specs=out_specs,
            scratch_shapes=[
                pltpu.VMEM((2, tile, most_keys), jnp.float32),
                pltpu.VMEM(
                    (count, holders, piece_rows // group_rows, group_rows, width), jnp.bfloat16
                ),
                pltpu.VMEM((count, holders, group_rows, width), jnp.bfloat16),
                pltpu.SemaphoreType.DMA((count, holders)),
                pltpu.SemaphoreType.DMA((count, holders)),
            ],
        ),
        out_shape=out_shape,
        compiler_params=pltpu.CompilerParams(vmem_limit_bytes=VMEM_BYTES),
        cost_estimate=pl.CostEstimate(
            flops=2 * blocks * rows * keys * (768 + lat),
            bytes_accessed=2 * (count * keys + 2 * blocks * rows) * width,
            transcendentals=blocks * rows * keys,
        ),
        name="attend_first" if decode else "attend_later",
    )(info, *operands, *far)


def dispatch_body(source, length, q_ref, out_ref):
    slots, rows, width = out_ref.shape
    lat_rope = q_ref.shape[2]
    lane = lax.broadcasted_iota(jnp.int32, (rows, width - lat_rope), 1)
    for slot in range(slots):
        out_ref[slot, :, :lat_rope] = q_ref[source[slot]]
        size = length[slot]
        tail = jnp.where(lane < 32, size >> 4, size & 15)
        out_ref[slot, :, lat_rope:] = tail.astype(jnp.float32).astype(jnp.bfloat16)


def dispatch_queries(source, length, query, width):
    slots = source.shape[0]
    _, rows, _ = query.shape
    smem = pl.BlockSpec(memory_space=pltpu.SMEM)
    vmem = pl.BlockSpec(memory_space=pltpu.VMEM)
    return pl.pallas_call(
        dispatch_body,
        in_specs=[smem, smem, vmem],
        out_specs=vmem,
        out_shape=jax.ShapeDtypeStruct((slots, rows, width), jnp.bfloat16),
        compiler_params=pltpu.CompilerParams(vmem_limit_bytes=VMEM_BYTES),
        name="dispatch_queries",
    )(source, length, query)


def cache_body(lat, factor, batch, order, length, used, q_ref, *rest):
    pool_refs = rest[:batch]
    out_ref, lse_ref = rest[batch:]
    step = pl.program_id(0)
    rows = q_ref.shape[1]
    width, cache_rows = pool_refs[0].shape

    @pl.when(step * batch < used[0])
    def _():
        place = lax.broadcasted_iota(jnp.int32, (1, cache_rows), 1)
        lane = lax.broadcasted_iota(jnp.int32, (rows, lse_ref.shape[2]), 1)
        slots = [order[step * batch + b] for b in range(batch)]
        scores = [
            key_scores(q_ref[slots[b], :, :width], pool_refs[b][...], lat, NN)
            for b in range(batch)
        ]
        for b in range(batch):
            masked = jnp.where(place < length[slots[b]], scores[b], negative)
            peak = jnp.max(masked, axis=1, keepdims=True)
            weights = jnp.exp2((masked - peak) * factor)
            total = jnp.sum(weights, axis=1, keepdims=True)
            summed = dot(weights.astype(jnp.bfloat16), pool_refs[b][:lat], NT)
            out_ref[slots[b]] = (summed / total).astype(jnp.bfloat16)
            lse = peak * factor + jnp.log2(total)
            high = lse.astype(jnp.bfloat16).astype(jnp.float32)
            middle = (lse - high).astype(jnp.bfloat16).astype(jnp.float32)
            low = lse - high - middle
            lse_ref[slots[b]] = jnp.where(
                lane == 0, high, jnp.where(lane == 1, middle, low)
            ).astype(jnp.bfloat16)


def attend_cache(order, length, used, query, pool, lat, factor):
    batch = 4
    slots, rows, padded = query.shape
    _, width, cache_rows = pool.shape
    whole = pl.BlockSpec((slots, rows, padded), lambda i, *_: (0, 0, 0))

    def pool_spec(b):
        return pl.BlockSpec(
            (None, width, cache_rows), lambda i, order, *_: (order[i * batch + b], 0, 0)
        )

    return pl.pallas_call(
        functools.partial(cache_body, lat, factor, batch),
        grid_spec=pltpu.PrefetchScalarGridSpec(
            num_scalar_prefetch=3,
            grid=(slots // batch,),
            in_specs=[whole] + [pool_spec(b) for b in range(batch)],
            out_specs=[
                pl.BlockSpec((slots, rows, lat), lambda i, *_: (0, 0, 0)),
                pl.BlockSpec((slots, rows, 128), lambda i, *_: (0, 0, 0)),
            ],
        ),
        out_shape=[
            jax.ShapeDtypeStruct((slots, rows, lat), jnp.bfloat16),
            jax.ShapeDtypeStruct((slots, rows, 128), jnp.bfloat16),
        ],
        compiler_params=pltpu.CompilerParams(vmem_limit_bytes=VMEM_BYTES),
        cost_estimate=pl.CostEstimate(
            flops=2 * slots * 128 * cache_rows * (width + lat),
            bytes_accessed=2 * slots * cache_rows * width,
            transcendentals=slots * rows * cache_rows,
        ),
        name="attend_cache",
    )(order, length, used, query, *([pool] * batch))


def merge_body(slot, back_ref, near_ref, near_lse_ref, out_ref):
    count = near_ref.shape[0]
    width = near_ref.shape[2]
    for r in range(count):
        back = back_ref[slot[r]].astype(jnp.float32)
        far = back[:, :width]
        far_lse = back[:, width : width + 1] + back[:, width + 1 : width + 2]
        far_lse = far_lse + back[:, width + 2 : width + 3]
        near_lse = near_lse_ref[r][:, :1]
        peak = jnp.maximum(far_lse, near_lse)
        far_part = jnp.exp2(far_lse - peak)
        near_part = jnp.exp2(near_lse - peak)
        mixed = far * far_part + near_ref[r] * near_part
        out_ref[r] = (mixed / (far_part + near_part)).astype(jnp.bfloat16)


def merge_decode(slot, back, near, near_lse):
    smem = pl.BlockSpec(memory_space=pltpu.SMEM)
    vmem = pl.BlockSpec(memory_space=pltpu.VMEM)
    return pl.pallas_call(
        merge_body,
        in_specs=[smem, vmem, vmem, vmem],
        out_specs=vmem,
        out_shape=jax.ShapeDtypeStruct(near.shape, jnp.bfloat16),
        compiler_params=pltpu.CompilerParams(vmem_limit_bytes=VMEM_BYTES),
        name="merge_decode",
    )(slot, back, near, near_lse)


def swap_core(value):
    return lax.ppermute(value, "grp", [(0, 1), (1, 0)])


def fetch_tp(value, shift):
    return lax.ppermute(value, "tp", [((i + shift) % 4, i) for i in range(4)])


def fetch_ring(value, shift, turn):
    moves = []
    for i in range(16):
        z, x = i // 4, i % 4
        for c in range(2):
            if (c + turn) % 2 == 0:
                origin = z * 4 + (x + shift) % 4
            else:
                origin = (z + shift) % 4 * 4 + x
            moves.append((origin * 2 + c, i * 2 + c))
    return lax.ppermute(value, ("seq", "grp"), moves)


def on_device(
    group_hidden,
    group_query,
    past_cache,
    past_len,
    decode_hidden,
    decode_query,
    decode_pool,
    owner,
    dec_len,
    w_latent,
    kv_gain,
    w_value,
):
    seq_count = lax.axis_size("seq")
    seq_place = lax.axis_index("seq")
    core = lax.axis_index("grp")
    z_place, x_place = seq_place >> 2, seq_place & 3
    prompt_count, group_local, head_local, row_width = group_query.shape
    past_local = past_cache.shape[1]
    request_local = decode_query.shape[0]
    lat = kv_gain.shape[0]
    value_width = w_value.shape[2]
    slot_count = decode_pool.shape[0]
    pair_limit = slot_count // seq_count
    query_pairs = 2 * head_local
    factor = (value_width + row_width - lat) ** (-0.5) * log2_e

    half = past_local // 2
    past_far = lax.dynamic_slice(past_cache, (2, core * half, 0), (2, half, row_width))
    past_far = lax.all_gather(past_far, ("seq", "grp"), axis=0, tiled=False)
    past_far = past_far.reshape(2 * seq_count, 2, -1, group_local // 2, row_width)
    past_near = lax.dynamic_slice(past_cache, (0, core * half, 0), (2, half, row_width))
    past_near = past_near.reshape(2 * half, row_width)

    half_tokens = group_local // 2
    pairs = 2 * request_local
    partial_group = jnp.einsum(
        "ptd,dc->ptc", group_hidden, w_latent, preferred_element_type=jnp.float32
    ).astype(jnp.bfloat16)
    partial_group = partial_group.reshape(prompt_count, 2, half_tokens, row_width)
    partial_decode = jnp.einsum(
        "rd,dc->rc",
        decode_hidden.reshape(pairs, -1),
        w_latent,
        preferred_element_type=jnp.float32,
    ).astype(jnp.bfloat16)
    group_part = prompt_count * half_tokens

    def both(chosen):
        part = lax.dynamic_index_in_dim(partial_group, chosen, axis=1, keepdims=False)
        return jnp.concatenate([part.reshape(group_part, row_width), partial_decode])

    pair_sum = both(core).astype(jnp.float32) + swap_core(both(1 - core)).astype(jnp.float32)
    pair_sum = pair_sum.astype(jnp.bfloat16)
    past_near, pair_sum = lax.optimization_barrier((past_near, pair_sum))
    latent = pair_sum.astype(jnp.float32)
    for shift in range(1, 4):
        latent = latent + fetch_tp(pair_sum, shift).astype(jnp.float32)
    past_line = [past_near] + [fetch_ring(past_near, shift, 0) for shift in range(1, 4)]
    half_order = jnp.arange(half_tokens, dtype=jnp.int32)
    group_positions = (
        past_len[:, None] + seq_place * group_local + core * half_tokens + half_order[None, :]
    )
    decode_positions = (
        past_len[0]
        + group_local * seq_count
        + (dec_len[:, None] + jnp.arange(2, dtype=jnp.int32)).reshape(-1)
    )
    positions = jnp.concatenate([group_positions.reshape(-1), decode_positions])
    rows_own = make_rows(latent, kv_gain, positions)
    fresh = jnp.pad(rows_own[group_part:], ((0, 128 - pairs), (0, 0)))

    group_own = rows_own[:group_part]
    group_line = [group_own] + [fetch_ring(group_own, shift, 0) for shift in range(1, 4)]
    line = jnp.stack([jnp.concatenate([old, new]) for old, new in zip(past_line, group_line)])
    line = line.reshape(4, -1, half_tokens, row_width)
    line, decode_query = lax.optimization_barrier((line, decode_query))
    lines = [line] + [fetch_ring(line, shift, 1) for shift in range(1, 4)]
    lines = lines + [swap_core(piece) for piece in lines]

    targets = owner[:, 0]
    request_order = jnp.arange(request_local, dtype=jnp.int32)
    earlier = (targets[:, None] == targets[None, :]) & (
        request_order[None, :] < request_order[:, None]
    )
    slot_rank = jnp.sum(earlier.astype(jnp.int32), axis=1)
    destination = targets * pair_limit + slot_rank
    matches = jnp.arange(slot_count, dtype=jnp.int32)[:, None] == destination[None, :]
    source = jnp.sum(jnp.where(matches, request_order[None, :], 0), axis=1)
    send_length = jnp.sum(jnp.where(matches, dec_len[None, :], 0), axis=1)
    send_query = dispatch_queries(
        source,
        send_length,
        decode_query.reshape(request_local, query_pairs, row_width),
        row_width + 64,
    )
    arrived = lax.all_to_all(
        send_query.reshape(seq_count, pair_limit * query_pairs, row_width + 64),
        "seq",
        split_axis=0,
        concat_axis=0,
        tiled=True,
    ).reshape(slot_count, query_pairs, row_width + 64)
    marks = arrived[:, 0, row_width:].astype(jnp.float32)
    slot_length = (marks[:, 0] * 16 + marks[:, 32]).astype(jnp.int32)

    is_used = slot_length > 0
    used_rank = jnp.cumsum(is_used.astype(jnp.int32)) - 1
    used = jnp.sum(is_used.astype(jnp.int32))
    slots = jnp.arange(slot_count, dtype=jnp.int32)
    wanted = jnp.minimum(slots, jnp.maximum(used - 1, 0))
    order = jnp.sum(
        jnp.where(is_used[None, :] & (used_rank[None, :] == wanted[:, None]), slots[None, :], 0),
        axis=1,
    )
    cache_latent, cache_lse = attend_cache(
        order, slot_length, used.reshape(1), arrived, jnp.swapaxes(decode_pool, 1, 2), lat, factor
    )
    cache_value = jnp.einsum(
        "nshc,hcv->nshv",
        cache_latent.reshape(slot_count, 2, head_local, lat),
        w_value,
        preferred_element_type=jnp.float32,
    ).astype(jnp.bfloat16)
    back = jnp.concatenate(
        [cache_value.reshape(slot_count, query_pairs, value_width), cache_lse], axis=-1
    )
    back = lax.all_to_all(
        back.reshape(seq_count, pair_limit * query_pairs, 2 * value_width),
        "seq",
        split_axis=0,
        concat_axis=0,
        tiled=True,
    ).reshape(slot_count, query_pairs, 2 * value_width)

    info = jnp.stack(
        [past_len[p] for p in range(prompt_count)]
        + [seq_place * group_local, z_place, x_place, core]
    ).astype(jnp.int32)
    queries = group_query.reshape(prompt_count, group_local * head_local, row_width)
    first_latent, near_latent, near_lse = attend_pair(
        info,
        queries,
        lines,
        None,
        0,
        half,
        decode_query.reshape(request_local * query_pairs, row_width),
        fresh,
        lat,
        factor,
        head_local,
    )
    near = jnp.einsum(
        "rshc,hcv->rshv",
        near_latent.reshape(request_local, 2, head_local, lat),
        w_value,
        preferred_element_type=jnp.float32,
    )
    decode_out = merge_decode(
        destination,
        back,
        near.reshape(request_local, query_pairs, value_width),
        near_lse.reshape(request_local, query_pairs, 128),
    ).reshape(request_local, 2, head_local, value_width)

    (later_latent,) = attend_pair(
        info, queries, lines, past_far, 2, half, None, None, lat, factor, head_local
    )
    prefill_latent = jnp.concatenate([first_latent, later_latent], axis=0)
    prefill_out = jnp.einsum(
        "pthc,hcv->pthv",
        prefill_latent.reshape(prompt_count, group_local, head_local, lat),
        w_value,
        preferred_element_type=jnp.float32,
    ).astype(jnp.bfloat16)
    return (prefill_out, decode_out)


def solution(mesh):
    in_specs = (
        P(None, "seq", ("tp", "grp")),
        P(None, "seq", ("tp", "grp"), None),
        P(None, "seq", None),
        P(),
        P("seq", None, ("tp", "grp")),
        P("seq", None, ("tp", "grp"), None),
        P("seq", None, None),
        P("seq", None),
        P("seq"),
        P(("tp", "grp"), None),
        P(),
        P(("tp", "grp"), None, None),
    )
    out_specs = (P(None, "seq", ("tp", "grp"), None), P("seq", None, ("tp", "grp"), None))
    return jax.shard_map(
        on_device, mesh=mesh, in_specs=in_specs, out_specs=out_specs, check_vma=False
    )
```

```python
import functools

import jax
import jax.numpy as jnp
from jax import lax
from jax.experimental import pallas as pl
from jax.experimental.pallas import tpu as pltpu
from jax.sharding import PartitionSpec as P

epsilon = 1e-06
negative = -1e30
log2_e = 1.4426950408889634
NT = (((1,), (1,)), ((), ()))
NN = (((1,), (0,)), ((), ()))
VMEM_BYTES = 56 * 2**20


def rotate(rope_part, positions):
    half_width = rope_part.shape[-1] // 2
    frequency = jnp.exp(-jnp.log(10000.0) * jnp.arange(half_width).astype(jnp.float32) / half_width)
    angles = positions.astype(jnp.float32)[..., None] * frequency
    cosine = jnp.cos(angles)
    sine_part = jnp.sin(angles)
    former = rope_part[..., :half_width]
    latter = rope_part[..., half_width:]
    return jnp.concatenate(
        [former * cosine - latter * sine_part, latter * cosine + former * sine_part], axis=-1
    )


def make_rows(latent, kv_gain, positions):
    lat_width = kv_gain.shape[0]
    latent_part = latent[..., :lat_width]
    spread = jnp.mean(latent_part * latent_part, axis=-1, keepdims=True)
    normed = latent_part * lax.rsqrt(spread + epsilon) * kv_gain
    return jnp.concatenate([normed, rotate(latent[..., lat_width:], positions)], axis=-1).astype(
        jnp.bfloat16
    )


def dot(left, right, dims):
    return lax.dot_general(left, right, dims, preferred_element_type=jnp.float32)


def key_scores(queries, keys, lat, dims):
    if dims is NT:
        return dot(queries[:, :lat], keys[:, :lat], NT) + dot(queries[:, lat:], keys[:, lat:], NT)
    return dot(queries[:, :lat], keys[:lat], NN) + dot(queries[:, lat:], keys[lat:], NN)


def lane_fold(op, total, block):
    for start in range(0, block.shape[1], 128):
        part = block[:, start : start + 128]
        total = part if total is None else op(total, part)
    return total


def attend_tiles(config, count, load, store, hold, keys, masks):
    lat, factor = config
    for i in range(count):
        queries = load(i)
        row = lax.broadcasted_iota(jnp.int32, (queries.shape[0], 1), 0)
        highest = None
        parts = []
        end = 0
        for block, mask in zip(keys, masks):
            values = block(i == 0)
            scores = key_scores(queries, values, lat, NT)
            allowed = mask(i, row)
            if allowed is not None:
                scores = jnp.where(allowed, scores, negative)
            place = slice(end, end + values.shape[0])
            end += values.shape[0]
            parts.append((place, block))
            hold[i % 2, :, place] = scores
            highest = lane_fold(jnp.maximum, highest, scores)
        peak = jnp.max(highest, axis=1, keepdims=True)
        total = None
        summed = None
        for place, block in parts:
            weights = jnp.exp2((hold[i % 2, :, place] - peak) * factor)
            total = lane_fold(jnp.add, total, weights)
            part = dot(weights.astype(jnp.bfloat16), block(False)[:, :lat], NN)
            summed = part if summed is None else summed + part
        total = jnp.sum(total, axis=1, keepdims=True)
        store(i, summed / total, peak * factor + jnp.log2(total))


def past_blocks(past_ref, kind, past, arrive, chunk):
    holders, piece_rows, width = past.shape
    step = chunk // piece_rows
    copies = []
    for j in range(holders // step):
        span = pl.ds(j * step, step)
        copies.append(
            pltpu.make_async_copy(past_ref.at[span, kind], past.at[span], arrive.at[j])
        )
        copies[j].start()

    def keys(j):
        def block(first):
            if first:
                copies[j].wait()
            return past[j * step : (j + 1) * step].reshape(chunk, width)

        return block

    return [keys(j) for j in range(len(copies))]


def past_masks(past_len, chunk, count):
    def mask(j):
        def allowed(i, row):
            if 2 * (j + 1) <= count:
                return None
            return lax.broadcasted_iota(jnp.int32, (1, chunk), 1) + j * chunk < past_len

        return allowed

    return [mask(j) for j in range(count)]


def whole_block(ref):
    return lambda first: ref[...].reshape(-1, ref.shape[-1])


def prefill_body(config, chunk, head_local, part, info, q_ref, near_ref, far_ref, token_ref, *rest):
    past_ref, out_ref, hold, past, arrive = rest
    senders, rows, width = q_ref.shape
    tile = hold.shape[1]
    each = tile // rows
    keys = past_blocks(past_ref, 0, past, arrive, chunk)
    masks = past_masks(info[0], chunk, len(keys))

    def group_mask(c):
        def allowed(i, row):
            token = info[2] + part * (rows // head_local) + (row & (rows - 1)) // head_local
            return token_ref[c : c + 1, :] <= token

        return allowed

    def load(i):
        return q_ref[i * each : (i + 1) * each].reshape(tile, width)

    def store(i, value, _):
        out_ref[i * each : (i + 1) * each] = value.astype(jnp.bfloat16).reshape(
            each, rows, value.shape[1]
        )

    attend_tiles(
        config,
        senders // each,
        load,
        store,
        hold,
        keys + [whole_block(near_ref), whole_block(far_ref)],
        masks + [group_mask(0), group_mask(1)],
    )


def attend_prefill(info, query, past, near, far, token, part, parts, lat, factor, head_local):
    senders, all_rows, width = query.shape
    rows = all_rows // parts
    holders, _, piece_rows, _ = past.shape
    lines, _, half_tokens, _ = near.shape
    keys = holders * piece_rows + 2 * lines * half_tokens
    tile = 2 * rows
    chunk = 768
    group_spec = pl.BlockSpec((lines, None, half_tokens, width), lambda i, _: (0, 0, 0, 0))
    return pl.pallas_call(
        functools.partial(prefill_body, (lat, factor), chunk, head_local, part),
        grid_spec=pltpu.PrefetchScalarGridSpec(
            num_scalar_prefetch=1,
            grid=(1,),
            in_specs=[
                pl.BlockSpec((senders, rows, width), lambda i, _: (0, part, 0)),
                group_spec,
                group_spec,
                pl.BlockSpec(token.shape, lambda i, _: (0, 0)),
                pl.BlockSpec(memory_space=pl.ANY),
            ],
            out_specs=pl.BlockSpec((senders, rows, lat), lambda i, _: (0, 0, 0)),
            scratch_shapes=[
                pltpu.VMEM((2, tile, keys), jnp.float32),
                pltpu.VMEM((holders, piece_rows, width), jnp.bfloat16),
                pltpu.SemaphoreType.DMA((holders * piece_rows // chunk,)),
            ],
        ),
        out_shape=jax.ShapeDtypeStruct((senders, rows, lat), jnp.bfloat16),
        compiler_params=pltpu.CompilerParams(vmem_limit_bytes=VMEM_BYTES),
        cost_estimate=pl.CostEstimate(
            flops=2 * senders * rows * keys * (768 + lat),
            bytes_accessed=2 * (keys + 2 * senders * rows) * width,
            transcendentals=senders * rows * keys,
        ),
        name="attend_prefill",
    )(info, query, near, far, token, past)


def decode_body(config, chunk, head_local, info, q_ref, near_ref, far_ref, fresh_ref, *rest):
    past_ref, out_ref, lse_ref, hold, past, arrive = rest
    tile = hold.shape[1]
    keys = past_blocks(past_ref, 1, past, arrive, chunk)
    masks = past_masks(info[1], chunk, len(keys))

    def fresh_mask(i, row):
        place = lax.broadcasted_iota(jnp.int32, (1, fresh_ref.shape[0]), 1)
        row = row + i * tile
        return (place >= row // (2 * head_local) * 2) & (place <= row // head_local)

    def store(i, value, lse):
        span = pl.ds(i * tile, tile)
        out_ref[span, :] = value.astype(jnp.bfloat16)
        lse_ref[span, :] = jnp.broadcast_to(lse, (tile, lse_ref.shape[1]))

    attend_tiles(
        config,
        q_ref.shape[0] // tile,
        lambda i: q_ref[i * tile : (i + 1) * tile, :],
        store,
        hold,
        keys + [whole_block(near_ref), whole_block(far_ref), whole_block(fresh_ref)],
        masks + [lambda i, row: None, lambda i, row: None, fresh_mask],
    )


def attend_decode(info, query, past, near, far, fresh, lat, factor, head_local):
    rows, width = query.shape
    holders, _, piece_rows, _ = past.shape
    lines, _, half_tokens, _ = near.shape
    keys = holders * piece_rows + 2 * lines * half_tokens + fresh.shape[0]
    tile = min(256, rows)
    chunk = 768
    group_spec = pl.BlockSpec((lines, None, half_tokens, width), lambda i, _: (0, 1, 0, 0))
    return pl.pallas_call(
        functools.partial(decode_body, (lat, factor), chunk, head_local),
        grid_spec=pltpu.PrefetchScalarGridSpec(
            num_scalar_prefetch=1,
            grid=(1,),
            in_specs=[
                pl.BlockSpec((rows, width), lambda i, _: (0, 0)),
                group_spec,
                group_spec,
                pl.BlockSpec(fresh.shape, lambda i, _: (0, 0)),
                pl.BlockSpec(memory_space=pl.ANY),
            ],
            out_specs=[
                pl.BlockSpec((rows, lat), lambda i, _: (0, 0)),
                pl.BlockSpec((rows, 128), lambda i, _: (0, 0)),
            ],
            scratch_shapes=[
                pltpu.VMEM((2, tile, keys), jnp.float32),
                pltpu.VMEM((holders, piece_rows, width), jnp.bfloat16),
                pltpu.SemaphoreType.DMA((holders * piece_rows // chunk,)),
            ],
        ),
        out_shape=[
            jax.ShapeDtypeStruct((rows, lat), jnp.bfloat16),
            jax.ShapeDtypeStruct((rows, 128), jnp.float32),
        ],
        compiler_params=pltpu.CompilerParams(vmem_limit_bytes=VMEM_BYTES),
        cost_estimate=pl.CostEstimate(
            flops=2 * rows * keys * (768 + lat),
            bytes_accessed=2 * (keys + 2 * rows) * width,
            transcendentals=rows * keys,
        ),
        name="attend_decode",
    )(info, query, near, far, fresh, past)


def dispatch_body(source, length, q_ref, out_ref):
    slots, rows, width = out_ref.shape
    lat_rope = q_ref.shape[2]
    lane = lax.broadcasted_iota(jnp.int32, (rows, width - lat_rope), 1)
    for slot in range(slots):
        out_ref[slot, :, :lat_rope] = q_ref[source[slot]]
        size = length[slot]
        tail = jnp.where(lane < 32, size >> 4, size & 15)
        out_ref[slot, :, lat_rope:] = tail.astype(jnp.float32).astype(jnp.bfloat16)


def dispatch_queries(source, length, query, width):
    slots = source.shape[0]
    _, rows, _ = query.shape
    smem = pl.BlockSpec(memory_space=pltpu.SMEM)
    vmem = pl.BlockSpec(memory_space=pltpu.VMEM)
    return pl.pallas_call(
        dispatch_body,
        in_specs=[smem, smem, vmem],
        out_specs=vmem,
        out_shape=jax.ShapeDtypeStruct((slots, rows, width), jnp.bfloat16),
        compiler_params=pltpu.CompilerParams(vmem_limit_bytes=VMEM_BYTES),
        name="dispatch_queries",
    )(source, length, query)


def cache_body(lat, factor, batch, order, length, used, q_ref, *rest):
    pool_refs = rest[:batch]
    out_ref, lse_ref = rest[batch:]
    step = pl.program_id(0)
    rows = q_ref.shape[1]
    width, cache_rows = pool_refs[0].shape

    @pl.when(step * batch < used[0])
    def _():
        place = lax.broadcasted_iota(jnp.int32, (1, cache_rows), 1)
        lane = lax.broadcasted_iota(jnp.int32, (rows, lse_ref.shape[2]), 1)
        slots = [order[step * batch + b] for b in range(batch)]
        scores = [
            key_scores(q_ref[slots[b], :, :width], pool_refs[b][...], lat, NN)
            for b in range(batch)
        ]
        for b in range(batch):
            masked = jnp.where(place < length[slots[b]], scores[b], negative)
            peak = jnp.max(masked, axis=1, keepdims=True)
            weights = jnp.exp2((masked - peak) * factor)
            total = jnp.sum(weights, axis=1, keepdims=True)
            summed = dot(weights.astype(jnp.bfloat16), pool_refs[b][:lat], NT)
            out_ref[slots[b]] = (summed / total).astype(jnp.bfloat16)
            lse = peak * factor + jnp.log2(total)
            high = lse.astype(jnp.bfloat16).astype(jnp.float32)
            middle = (lse - high).astype(jnp.bfloat16).astype(jnp.float32)
            low = lse - high - middle
            lse_ref[slots[b]] = jnp.where(
                lane == 0, high, jnp.where(lane == 1, middle, low)
            ).astype(jnp.bfloat16)


def attend_cache(order, length, used, query, pool, lat, factor):
    batch = 4
    slots, rows, padded = query.shape
    _, width, cache_rows = pool.shape
    whole = pl.BlockSpec((slots, rows, padded), lambda i, *_: (0, 0, 0))

    def pool_spec(b):
        return pl.BlockSpec(
            (None, width, cache_rows), lambda i, order, *_: (order[i * batch + b], 0, 0)
        )

    return pl.pallas_call(
        functools.partial(cache_body, lat, factor, batch),
        grid_spec=pltpu.PrefetchScalarGridSpec(
            num_scalar_prefetch=3,
            grid=(slots // batch,),
            in_specs=[whole] + [pool_spec(b) for b in range(batch)],
            out_specs=[
                pl.BlockSpec((slots, rows, lat), lambda i, *_: (0, 0, 0)),
                pl.BlockSpec((slots, rows, 128), lambda i, *_: (0, 0, 0)),
            ],
        ),
        out_shape=[
            jax.ShapeDtypeStruct((slots, rows, lat), jnp.bfloat16),
            jax.ShapeDtypeStruct((slots, rows, 128), jnp.bfloat16),
        ],
        compiler_params=pltpu.CompilerParams(vmem_limit_bytes=VMEM_BYTES),
        cost_estimate=pl.CostEstimate(
            flops=2 * slots * 128 * cache_rows * (width + lat),
            bytes_accessed=2 * slots * cache_rows * width,
            transcendentals=slots * rows * cache_rows,
        ),
        name="attend_cache",
    )(order, length, used, query, *([pool] * batch))


def merge_body(slot, back_ref, near_ref, near_lse_ref, out_ref):
    count = near_ref.shape[0]
    width = near_ref.shape[2]
    for r in range(count):
        back = back_ref[slot[r]].astype(jnp.float32)
        far = back[:, :width]
        far_lse = back[:, width : width + 1] + back[:, width + 1 : width + 2]
        far_lse = far_lse + back[:, width + 2 : width + 3]
        near_lse = near_lse_ref[r][:, :1]
        peak = jnp.maximum(far_lse, near_lse)
        far_part = jnp.exp2(far_lse - peak)
        near_part = jnp.exp2(near_lse - peak)
        mixed = far * far_part + near_ref[r] * near_part
        out_ref[r] = (mixed / (far_part + near_part)).astype(jnp.bfloat16)


def merge_decode(slot, back, near, near_lse):
    smem = pl.BlockSpec(memory_space=pltpu.SMEM)
    vmem = pl.BlockSpec(memory_space=pltpu.VMEM)
    return pl.pallas_call(
        merge_body,
        in_specs=[smem, vmem, vmem, vmem],
        out_specs=vmem,
        out_shape=jax.ShapeDtypeStruct(near.shape, jnp.bfloat16),
        compiler_params=pltpu.CompilerParams(vmem_limit_bytes=VMEM_BYTES),
        name="merge_decode",
    )(slot, back, near, near_lse)


def swap_core(value):
    return lax.ppermute(value, "grp", [(0, 1), (1, 0)])


def fetch_tp(value, shift):
    return lax.ppermute(value, "tp", [((i + shift) % 4, i) for i in range(4)])


def fetch_ring(value, shift, turn):
    moves = []
    for i in range(16):
        z, x = i // 4, i % 4
        for c in range(2):
            if (c + turn) % 2 == 0:
                origin = z * 4 + (x + shift) % 4
            else:
                origin = (z + shift) % 4 * 4 + x
            moves.append((origin * 2 + c, i * 2 + c))
    return lax.ppermute(value, ("seq", "grp"), moves)


def on_device(
    group_hidden,
    group_query,
    past_cache,
    past_len,
    decode_hidden,
    decode_query,
    decode_pool,
    owner,
    dec_len,
    w_latent,
    kv_gain,
    w_value,
):
    seq_count = lax.axis_size("seq")
    seq_place = lax.axis_index("seq")
    tp_place = lax.axis_index("tp")
    core = lax.axis_index("grp")
    z_place, x_place = seq_place >> 2, seq_place & 3
    prompt_count, group_local, head_local, row_width = group_query.shape
    past_local = past_cache.shape[1]
    request_local = decode_query.shape[0]
    lat = kv_gain.shape[0]
    value_width = w_value.shape[2]
    slot_count = decode_pool.shape[0]
    pair_limit = slot_count // seq_count
    query_pairs = 2 * head_local
    factor = (value_width + row_width - lat) ** (-0.5) * log2_e

    queries = lax.all_to_all(group_query, "tp", split_axis=0, concat_axis=0, tiled=True)
    queries = queries.reshape(prompt_count, group_local * head_local, row_width)

    half = past_local // 2
    past_own = lax.dynamic_slice(past_cache, (tp_place, core * half, 0), (1, half, row_width))
    past_zero = lax.dynamic_slice(past_cache, (0, core * half, 0), (1, half, row_width))
    past_all = lax.all_gather(
        jnp.concatenate([past_own, past_zero]), ("seq", "grp"), axis=0, tiled=False
    )

    half_tokens = group_local // 2
    pairs = 2 * request_local
    partial_group = jnp.einsum(
        "ptd,dc->ptc", group_hidden, w_latent, preferred_element_type=jnp.float32
    ).astype(jnp.bfloat16)
    partial_group = partial_group.reshape(prompt_count, 2, half_tokens, row_width)
    partial_decode = jnp.einsum(
        "rd,dc->rc",
        decode_hidden.reshape(pairs, -1),
        w_latent,
        preferred_element_type=jnp.float32,
    ).astype(jnp.bfloat16)
    group_part = prompt_count * half_tokens

    def both(chosen):
        part = lax.dynamic_index_in_dim(partial_group, chosen, axis=1, keepdims=False)
        return jnp.concatenate([part.reshape(group_part, row_width), partial_decode])

    pair_sum = both(core).astype(jnp.float32) + swap_core(both(1 - core)).astype(jnp.float32)
    pair_sum = pair_sum.astype(jnp.bfloat16)

    def part_of(place):
        chosen = lax.dynamic_slice_in_dim(
            pair_sum, (place & 3) * half_tokens, half_tokens, axis=0
        )
        return jnp.concatenate([chosen, pair_sum[:half_tokens], pair_sum[group_part:]])

    latent = part_of(tp_place).astype(jnp.float32)
    for shift in range(1, 4):
        latent = latent + fetch_tp(part_of(tp_place - shift), shift).astype(jnp.float32)
    half_order = jnp.arange(half_tokens, dtype=jnp.int32)
    token = seq_place * group_local + core * half_tokens + half_order
    decode_positions = (
        past_len[0]
        + group_local * seq_count
        + (dec_len[:, None] + jnp.arange(2, dtype=jnp.int32)).reshape(-1)
    )
    positions = jnp.concatenate(
        [past_len[tp_place] + token, past_len[0] + token, decode_positions]
    )
    rows_own = make_rows(latent, kv_gain, positions)
    fresh = jnp.pad(rows_own[2 * half_tokens :], ((0, 128 - pairs), (0, 0)))

    group_own = rows_own[: 2 * half_tokens].reshape(2, half_tokens, row_width)
    group_line = [group_own] + [fetch_ring(group_own, shift, 0) for shift in range(1, 4)]
    group_line = jnp.stack(group_line)
    decode_query, group_line = lax.optimization_barrier((decode_query, group_line))
    group_lines = [group_line] + [fetch_ring(group_line, shift, 1) for shift in range(1, 4)]
    group_near = jnp.concatenate(group_lines)
    group_far = swap_core(group_near)
    outer = jnp.arange(4, dtype=jnp.int32)[:, None]
    inner = jnp.arange(4, dtype=jnp.int32)[None, :]

    def tokens_of(side):
        z_from = (z_place + outer + (inner - outer) * side) & 3
        x_from = (x_place + inner + (outer - inner) * side) & 3
        start = (z_from * 4 + x_from) * group_local + side * half_tokens
        return (start.reshape(seq_count, 1) + half_order[None, :]).reshape(1, -1)

    key_token = jnp.concatenate([tokens_of(core), tokens_of(1 - core)])

    targets = owner[:, 0]
    request_order = jnp.arange(request_local, dtype=jnp.int32)
    earlier = (targets[:, None] == targets[None, :]) & (
        request_order[None, :] < request_order[:, None]
    )
    slot_rank = jnp.sum(earlier.astype(jnp.int32), axis=1)
    destination = targets * pair_limit + slot_rank
    matches = jnp.arange(slot_count, dtype=jnp.int32)[:, None] == destination[None, :]
    source = jnp.sum(jnp.where(matches, request_order[None, :], 0), axis=1)
    send_length = jnp.sum(jnp.where(matches, dec_len[None, :], 0), axis=1)
    send_query = dispatch_queries(
        source,
        send_length,
        decode_query.reshape(request_local, query_pairs, row_width),
        row_width + 64,
    )
    arrived = lax.all_to_all(
        send_query.reshape(seq_count, pair_limit * query_pairs, row_width + 64),
        "seq",
        split_axis=0,
        concat_axis=0,
        tiled=True,
    ).reshape(slot_count, query_pairs, row_width + 64)
    marks = arrived[:, 0, row_width:].astype(jnp.float32)
    slot_length = (marks[:, 0] * 16 + marks[:, 32]).astype(jnp.int32)

    is_used = slot_length > 0
    used_rank = jnp.cumsum(is_used.astype(jnp.int32)) - 1
    used = jnp.sum(is_used.astype(jnp.int32))
    slots = jnp.arange(slot_count, dtype=jnp.int32)
    wanted = jnp.minimum(slots, jnp.maximum(used - 1, 0))
    order = jnp.sum(
        jnp.where(is_used[None, :] & (used_rank[None, :] == wanted[:, None]), slots[None, :], 0),
        axis=1,
    )
    cache_latent, cache_lse = attend_cache(
        order, slot_length, used.reshape(1), arrived, jnp.swapaxes(decode_pool, 1, 2), lat, factor
    )
    cache_value = jnp.einsum(
        "nshc,hcv->nshv",
        cache_latent.reshape(slot_count, 2, head_local, lat),
        w_value,
        preferred_element_type=jnp.float32,
    ).astype(jnp.bfloat16)
    back = jnp.concatenate(
        [cache_value.reshape(slot_count, query_pairs, value_width), cache_lse], axis=-1
    )
    back = lax.all_to_all(
        back.reshape(seq_count, pair_limit * query_pairs, 2 * value_width),
        "seq",
        split_axis=0,
        concat_axis=0,
        tiled=True,
    ).reshape(slot_count, query_pairs, 2 * value_width)

    info = jnp.stack([past_len[tp_place], past_len[0], seq_place * group_local]).astype(jnp.int32)
    near_latent, near_lse = attend_decode(
        info,
        decode_query.reshape(request_local * query_pairs, row_width),
        past_all,
        group_near,
        group_far,
        fresh,
        lat,
        factor,
        head_local,
    )
    near = jnp.einsum(
        "rshc,hcv->rshv",
        near_latent.reshape(request_local, 2, head_local, lat),
        w_value,
        preferred_element_type=jnp.float32,
    )
    decode_out = merge_decode(
        destination,
        back,
        near.reshape(request_local, query_pairs, value_width),
        near_lse.reshape(request_local, query_pairs, 128),
    ).reshape(request_local, 2, head_local, value_width)

    parts = 2
    values = []
    for part in range(parts):
        prefill_latent = attend_prefill(
            info,
            queries,
            past_all,
            group_near,
            group_far,
            key_token,
            part,
            parts,
            lat,
            factor,
            head_local,
        )
        prefill_latent = lax.all_to_all(
            prefill_latent, "tp", split_axis=0, concat_axis=0, tiled=True
        )
        values.append(
            jnp.einsum(
                "pthc,hcv->pthv",
                prefill_latent.reshape(prompt_count, group_local // parts, head_local, lat),
                w_value,
                preferred_element_type=jnp.float32,
            ).astype(jnp.bfloat16)
        )
    prefill_out = jnp.concatenate(values, axis=1)
    return (prefill_out, decode_out)


def solution(mesh):
    in_specs = (
        P(None, "seq", ("tp", "grp")),
        P(None, "seq", ("tp", "grp"), None),
        P(None, "seq", None),
        P(),
        P("seq", None, ("tp", "grp")),
        P("seq", None, ("tp", "grp"), None),
        P("seq", None, None),
        P("seq", None),
        P("seq"),
        P(("tp", "grp"), None),
        P(),
        P(("tp", "grp"), None, None),
    )
    out_specs = (P(None, "seq", ("tp", "grp"), None), P("seq", None, ("tp", "grp"), None))
    return jax.shard_map(
        on_device, mesh=mesh, in_specs=in_specs, out_specs=out_specs, check_vma=False
    )
```

```python
import functools

import jax
import jax.numpy as jnp
from jax import lax
from jax.experimental import pallas as pl
from jax.experimental.pallas import tpu as pltpu
from jax.sharding import PartitionSpec as P

epsilon = 1e-06
negative = -1e30
log2_e = 1.4426950408889634
NT = (((1,), (1,)), ((), ()))
NN = (((1,), (0,)), ((), ()))
VMEM_BYTES = 56 * 2**20


def rotate(rope_part, positions):
    half_width = rope_part.shape[-1] // 2
    frequency = jnp.exp(-jnp.log(10000.0) * jnp.arange(half_width).astype(jnp.float32) / half_width)
    angles = positions.astype(jnp.float32)[..., None] * frequency
    cosine = jnp.cos(angles)
    sine_part = jnp.sin(angles)
    former = rope_part[..., :half_width]
    latter = rope_part[..., half_width:]
    return jnp.concatenate(
        [former * cosine - latter * sine_part, latter * cosine + former * sine_part], axis=-1
    )


def make_rows(latent, kv_gain, positions):
    lat_width = kv_gain.shape[0]
    latent_part = latent[..., :lat_width]
    spread = jnp.mean(latent_part * latent_part, axis=-1, keepdims=True)
    normed = latent_part * lax.rsqrt(spread + epsilon) * kv_gain
    return jnp.concatenate([normed, rotate(latent[..., lat_width:], positions)], axis=-1).astype(
        jnp.bfloat16
    )


def dot(left, right, dims):
    return lax.dot_general(left, right, dims, preferred_element_type=jnp.float32)


def key_scores(queries, keys, lat, dims):
    if dims is NT:
        return dot(queries[:, :lat], keys[:, :lat], NT) + dot(queries[:, lat:], keys[:, lat:], NT)
    return dot(queries[:, :lat], keys[:lat], NN) + dot(queries[:, lat:], keys[lat:], NN)


def lane_fold(op, total, block):
    for start in range(0, block.shape[1], 128):
        part = block[:, start : start + 128]
        total = part if total is None else op(total, part)
    return total


def attend_tiles(config, count, load, store, hold, peaks, keys, masks):
    lat, factor = config

    def score(i, slot, first):
        queries = load(i)
        row = lax.broadcasted_iota(jnp.int32, (queries.shape[0], 1), 0)
        highest = None
        end = 0
        for block, mask in zip(keys, masks):
            values = block(first)
            scores = key_scores(queries, values, lat, NT)
            allowed = mask(i, row)
            if allowed is not None:
                scores = jnp.where(allowed, scores, negative)
            hold[slot, :, end : end + values.shape[0]] = scores
            end += values.shape[0]
            highest = lane_fold(jnp.maximum, highest, scores)
        peaks[slot] = highest

    def collect(i, slot):
        peak = jnp.max(peaks[slot], axis=1, keepdims=True)
        total = None
        summed = None
        end = 0
        for block in keys:
            values = block(False)
            weights = jnp.exp2((hold[slot, :, end : end + values.shape[0]] - peak) * factor)
            end += values.shape[0]
            total = lane_fold(jnp.add, total, weights)
            part = dot(weights.astype(jnp.bfloat16), values[:, :lat], NN)
            summed = part if summed is None else summed + part
        total = jnp.sum(total, axis=1, keepdims=True)
        store(i, summed / total, peak * factor + jnp.log2(total))

    score(0, 0, True)

    def step(i, carry):
        collect(i, i & 1)
        score(i + 1, 1 - (i & 1), False)
        return carry

    lax.fori_loop(0, count - 1, step, 0)
    collect(count - 1, (count - 1) & 1)


def past_blocks(past_ref, kind, past, arrive, chunk):
    holders, piece_rows, width = past.shape
    step = chunk // piece_rows
    copies = []
    for j in range(holders // step):
        span = pl.ds(j * step, step)
        copies.append(
            pltpu.make_async_copy(past_ref.at[span, kind], past.at[span], arrive.at[j])
        )
        copies[j].start()

    def keys(j):
        def block(first):
            if first:
                copies[j].wait()
            return past[j * step : (j + 1) * step].reshape(chunk, width)

        return block

    return [keys(j) for j in range(len(copies))]


def past_masks(past_len, chunk, count):
    def mask(j):
        def allowed(i, row):
            if 2 * (j + 1) <= count:
                return None
            return lax.broadcasted_iota(jnp.int32, (1, chunk), 1) + j * chunk < past_len

        return allowed

    return [mask(j) for j in range(count)]


def whole_block(ref):
    return lambda first: ref[...].reshape(-1, ref.shape[-1])


def prefill_body(config, chunk, head_local, part, info, q_ref, near_ref, far_ref, token_ref, *rest):
    past_ref, out_ref, hold, peaks, past, arrive = rest
    senders, rows, width = q_ref.shape
    tile = hold.shape[1]
    each = tile // rows
    keys = past_blocks(past_ref, 0, past, arrive, chunk)
    masks = past_masks(info[0], chunk, len(keys))

    def group_mask(c):
        def allowed(i, row):
            token = info[2] + part * (rows // head_local) + (row & (rows - 1)) // head_local
            return token_ref[c : c + 1, :] <= token

        return allowed

    def load(i):
        return q_ref[pl.ds(i * each, each)].reshape(tile, width)

    def store(i, value, _):
        out_ref[pl.ds(i * each, each)] = value.astype(jnp.bfloat16).reshape(
            each, rows, value.shape[1]
        )

    attend_tiles(
        config,
        senders // each,
        load,
        store,
        hold,
        peaks,
        keys + [whole_block(near_ref), whole_block(far_ref)],
        masks + [group_mask(0), group_mask(1)],
    )


def attend_prefill(info, query, past, near, far, token, part, parts, lat, factor, head_local):
    senders, all_rows, width = query.shape
    rows = all_rows // parts
    holders, _, piece_rows, _ = past.shape
    lines, _, half_tokens, _ = near.shape
    keys = holders * piece_rows + 2 * lines * half_tokens
    tile = 2 * rows
    chunk = 768
    group_spec = pl.BlockSpec((lines, None, half_tokens, width), lambda i, _: (0, 0, 0, 0))
    return pl.pallas_call(
        functools.partial(prefill_body, (lat, factor), chunk, head_local, part),
        grid_spec=pltpu.PrefetchScalarGridSpec(
            num_scalar_prefetch=1,
            grid=(1,),
            in_specs=[
                pl.BlockSpec((senders, rows, width), lambda i, _: (0, part, 0)),
                group_spec,
                group_spec,
                pl.BlockSpec(token.shape, lambda i, _: (0, 0)),
                pl.BlockSpec(memory_space=pl.ANY),
            ],
            out_specs=pl.BlockSpec((senders, rows, lat), lambda i, _: (0, 0, 0)),
            scratch_shapes=[
                pltpu.VMEM((2, tile, keys), jnp.float32),
                pltpu.VMEM((2, tile, 128), jnp.float32),
                pltpu.VMEM((holders, piece_rows, width), jnp.bfloat16),
                pltpu.SemaphoreType.DMA((holders * piece_rows // chunk,)),
            ],
        ),
        out_shape=jax.ShapeDtypeStruct((senders, rows, lat), jnp.bfloat16),
        compiler_params=pltpu.CompilerParams(vmem_limit_bytes=VMEM_BYTES),
        cost_estimate=pl.CostEstimate(
            flops=2 * senders * rows * keys * (768 + lat),
            bytes_accessed=2 * (keys + 2 * senders * rows) * width,
            transcendentals=senders * rows * keys,
        ),
        name="attend_prefill",
    )(info, query, near, far, token, past)


def decode_body(config, chunk, head_local, info, q_ref, near_ref, far_ref, fresh_ref, *rest):
    past_ref, out_ref, lse_ref, hold, peaks, past, arrive = rest
    tile = hold.shape[1]
    keys = past_blocks(past_ref, 1, past, arrive, chunk)
    masks = past_masks(info[1], chunk, len(keys))

    def fresh_mask(i, row):
        place = lax.broadcasted_iota(jnp.int32, (1, fresh_ref.shape[0]), 1)
        row = row + i * tile
        return (place >= row // (2 * head_local) * 2) & (place <= row // head_local)

    def store(i, value, lse):
        span = pl.ds(pl.multiple_of(i * tile, tile), tile)
        out_ref[span, :] = value.astype(jnp.bfloat16)
        lse_ref[span, :] = jnp.broadcast_to(lse, (tile, lse_ref.shape[1]))

    attend_tiles(
        config,
        q_ref.shape[0] // tile,
        lambda i: q_ref[pl.ds(pl.multiple_of(i * tile, tile), tile), :],
        store,
        hold,
        peaks,
        keys + [whole_block(near_ref), whole_block(far_ref), whole_block(fresh_ref)],
        masks + [lambda i, row: None, lambda i, row: None, fresh_mask],
    )


def attend_decode(info, query, past, near, far, fresh, lat, factor, head_local):
    rows, width = query.shape
    holders, _, piece_rows, _ = past.shape
    lines, _, half_tokens, _ = near.shape
    keys = holders * piece_rows + 2 * lines * half_tokens + fresh.shape[0]
    tile = min(256, rows)
    chunk = 768
    group_spec = pl.BlockSpec((lines, None, half_tokens, width), lambda i, _: (0, 1, 0, 0))
    return pl.pallas_call(
        functools.partial(decode_body, (lat, factor), chunk, head_local),
        grid_spec=pltpu.PrefetchScalarGridSpec(
            num_scalar_prefetch=1,
            grid=(1,),
            in_specs=[
                pl.BlockSpec((rows, width), lambda i, _: (0, 0)),
                group_spec,
                group_spec,
                pl.BlockSpec(fresh.shape, lambda i, _: (0, 0)),
                pl.BlockSpec(memory_space=pl.ANY),
            ],
            out_specs=[
                pl.BlockSpec((rows, lat), lambda i, _: (0, 0)),
                pl.BlockSpec((rows, 128), lambda i, _: (0, 0)),
            ],
            scratch_shapes=[
                pltpu.VMEM((2, tile, keys), jnp.float32),
                pltpu.VMEM((2, tile, 128), jnp.float32),
                pltpu.VMEM((holders, piece_rows, width), jnp.bfloat16),
                pltpu.SemaphoreType.DMA((holders * piece_rows // chunk,)),
            ],
        ),
        out_shape=[
            jax.ShapeDtypeStruct((rows, lat), jnp.bfloat16),
            jax.ShapeDtypeStruct((rows, 128), jnp.float32),
        ],
        compiler_params=pltpu.CompilerParams(vmem_limit_bytes=VMEM_BYTES),
        cost_estimate=pl.CostEstimate(
            flops=2 * rows * keys * (768 + lat),
            bytes_accessed=2 * (keys + 2 * rows) * width,
            transcendentals=rows * keys,
        ),
        name="attend_decode",
    )(info, query, near, far, fresh, past)


def dispatch_body(source, length, q_ref, out_ref):
    slots, rows, width = out_ref.shape
    lat_rope = q_ref.shape[2]
    lane = lax.broadcasted_iota(jnp.int32, (rows, width - lat_rope), 1)
    for slot in range(slots):
        out_ref[slot, :, :lat_rope] = q_ref[source[slot]]
        size = length[slot]
        tail = jnp.where(lane < 32, size >> 4, size & 15)
        out_ref[slot, :, lat_rope:] = tail.astype(jnp.float32).astype(jnp.bfloat16)


def dispatch_queries(source, length, query, width):
    slots = source.shape[0]
    _, rows, _ = query.shape
    smem = pl.BlockSpec(memory_space=pltpu.SMEM)
    vmem = pl.BlockSpec(memory_space=pltpu.VMEM)
    return pl.pallas_call(
        dispatch_body,
        in_specs=[smem, smem, vmem],
        out_specs=vmem,
        out_shape=jax.ShapeDtypeStruct((slots, rows, width), jnp.bfloat16),
        compiler_params=pltpu.CompilerParams(vmem_limit_bytes=VMEM_BYTES),
        name="dispatch_queries",
    )(source, length, query)


def cache_body(lat, factor, batch, order, length, used, q_ref, *rest):
    pool_refs = rest[:batch]
    out_ref, lse_ref = rest[batch:]
    step = pl.program_id(0)
    rows = q_ref.shape[1]
    width, cache_rows = pool_refs[0].shape

    @pl.when(step * batch < used[0])
    def _():
        place = lax.broadcasted_iota(jnp.int32, (1, cache_rows), 1)
        lane = lax.broadcasted_iota(jnp.int32, (rows, lse_ref.shape[2]), 1)
        slots = [order[step * batch + b] for b in range(batch)]
        scores = [
            key_scores(q_ref[slots[b], :, :width], pool_refs[b][...], lat, NN)
            for b in range(batch)
        ]
        for b in range(batch):
            masked = jnp.where(place < length[slots[b]], scores[b], negative)
            peak = jnp.max(masked, axis=1, keepdims=True)
            weights = jnp.exp2((masked - peak) * factor)
            total = jnp.sum(weights, axis=1, keepdims=True)
            summed = dot(weights.astype(jnp.bfloat16), pool_refs[b][:lat], NT)
            out_ref[slots[b]] = (summed / total).astype(jnp.bfloat16)
            lse = peak * factor + jnp.log2(total)
            high = lse.astype(jnp.bfloat16).astype(jnp.float32)
            middle = (lse - high).astype(jnp.bfloat16).astype(jnp.float32)
            low = lse - high - middle
            lse_ref[slots[b]] = jnp.where(
                lane == 0, high, jnp.where(lane == 1, middle, low)
            ).astype(jnp.bfloat16)


def attend_cache(order, length, used, query, pool, lat, factor):
    batch = 4
    slots, rows, padded = query.shape
    _, width, cache_rows = pool.shape
    whole = pl.BlockSpec((slots, rows, padded), lambda i, *_: (0, 0, 0))

    def pool_spec(b):
        return pl.BlockSpec(
            (None, width, cache_rows), lambda i, order, *_: (order[i * batch + b], 0, 0)
        )

    return pl.pallas_call(
        functools.partial(cache_body, lat, factor, batch),
        grid_spec=pltpu.PrefetchScalarGridSpec(
            num_scalar_prefetch=3,
            grid=(slots // batch,),
            in_specs=[whole] + [pool_spec(b) for b in range(batch)],
            out_specs=[
                pl.BlockSpec((slots, rows, lat), lambda i, *_: (0, 0, 0)),
                pl.BlockSpec((slots, rows, 128), lambda i, *_: (0, 0, 0)),
            ],
        ),
        out_shape=[
            jax.ShapeDtypeStruct((slots, rows, lat), jnp.bfloat16),
            jax.ShapeDtypeStruct((slots, rows, 128), jnp.bfloat16),
        ],
        compiler_params=pltpu.CompilerParams(vmem_limit_bytes=VMEM_BYTES),
        cost_estimate=pl.CostEstimate(
            flops=2 * slots * 128 * cache_rows * (width + lat),
            bytes_accessed=2 * slots * cache_rows * width,
            transcendentals=slots * rows * cache_rows,
        ),
        name="attend_cache",
    )(order, length, used, query, *([pool] * batch))


def merge_body(slot, back_ref, near_ref, near_lse_ref, out_ref):
    count = near_ref.shape[0]
    width = near_ref.shape[2]
    for r in range(count):
        back = back_ref[slot[r]].astype(jnp.float32)
        far = back[:, :width]
        far_lse = back[:, width : width + 1] + back[:, width + 1 : width + 2]
        far_lse = far_lse + back[:, width + 2 : width + 3]
        near_lse = near_lse_ref[r][:, :1]
        peak = jnp.maximum(far_lse, near_lse)
        far_part = jnp.exp2(far_lse - peak)
        near_part = jnp.exp2(near_lse - peak)
        mixed = far * far_part + near_ref[r] * near_part
        out_ref[r] = (mixed / (far_part + near_part)).astype(jnp.bfloat16)


def merge_decode(slot, back, near, near_lse):
    smem = pl.BlockSpec(memory_space=pltpu.SMEM)
    vmem = pl.BlockSpec(memory_space=pltpu.VMEM)
    return pl.pallas_call(
        merge_body,
        in_specs=[smem, vmem, vmem, vmem],
        out_specs=vmem,
        out_shape=jax.ShapeDtypeStruct(near.shape, jnp.bfloat16),
        compiler_params=pltpu.CompilerParams(vmem_limit_bytes=VMEM_BYTES),
        name="merge_decode",
    )(slot, back, near, near_lse)


def swap_core(value):
    return lax.ppermute(value, "grp", [(0, 1), (1, 0)])


def fetch_tp(value, shift):
    return lax.ppermute(value, "tp", [((i + shift) % 4, i) for i in range(4)])


def fetch_ring(value, shift, turn):
    moves = []
    for i in range(16):
        z, x = i // 4, i % 4
        for c in range(2):
            if (c + turn) % 2 == 0:
                origin = z * 4 + (x + shift) % 4
            else:
                origin = (z + shift) % 4 * 4 + x
            moves.append((origin * 2 + c, i * 2 + c))
    return lax.ppermute(value, ("seq", "grp"), moves)


def on_device(
    group_hidden,
    group_query,
    past_cache,
    past_len,
    decode_hidden,
    decode_query,
    decode_pool,
    owner,
    dec_len,
    w_latent,
    kv_gain,
    w_value,
):
    seq_count = lax.axis_size("seq")
    seq_place = lax.axis_index("seq")
    tp_place = lax.axis_index("tp")
    core = lax.axis_index("grp")
    z_place, x_place = seq_place >> 2, seq_place & 3
    prompt_count, group_local, head_local, row_width = group_query.shape
    past_local = past_cache.shape[1]
    request_local = decode_query.shape[0]
    lat = kv_gain.shape[0]
    value_width = w_value.shape[2]
    slot_count = decode_pool.shape[0]
    pair_limit = slot_count // seq_count
    query_pairs = 2 * head_local
    factor = (value_width + row_width - lat) ** (-0.5) * log2_e

    half = past_local // 2
    past_own = lax.dynamic_slice(past_cache, (tp_place, core * half, 0), (1, half, row_width))
    past_zero = lax.dynamic_slice(past_cache, (0, core * half, 0), (1, half, row_width))
    past_all = lax.all_gather(
        jnp.concatenate([past_own, past_zero]), ("seq", "grp"), axis=0, tiled=False
    )

    half_tokens = group_local // 2
    pairs = 2 * request_local
    partial_group = jnp.einsum(
        "ptd,dc->ptc", group_hidden, w_latent, preferred_element_type=jnp.float32
    ).astype(jnp.bfloat16)
    partial_group = partial_group.reshape(prompt_count, 2, half_tokens, row_width)
    partial_decode = jnp.einsum(
        "rd,dc->rc",
        decode_hidden.reshape(pairs, -1),
        w_latent,
        preferred_element_type=jnp.float32,
    ).astype(jnp.bfloat16)
    group_part = prompt_count * half_tokens

    def both(chosen):
        part = lax.dynamic_index_in_dim(partial_group, chosen, axis=1, keepdims=False)
        return jnp.concatenate([part.reshape(group_part, row_width), partial_decode])

    pair_sum = both(core).astype(jnp.float32) + swap_core(both(1 - core)).astype(jnp.float32)
    pair_sum = pair_sum.astype(jnp.bfloat16)

    def part_of(place):
        chosen = lax.dynamic_slice_in_dim(
            pair_sum, (place & 3) * half_tokens, half_tokens, axis=0
        )
        return jnp.concatenate([chosen, pair_sum[:half_tokens], pair_sum[group_part:]])

    latent = part_of(tp_place).astype(jnp.float32)
    for shift in range(1, 4):
        latent = latent + fetch_tp(part_of(tp_place - shift), shift).astype(jnp.float32)
    half_order = jnp.arange(half_tokens, dtype=jnp.int32)
    token = seq_place * group_local + core * half_tokens + half_order
    decode_positions = (
        past_len[0]
        + group_local * seq_count
        + (dec_len[:, None] + jnp.arange(2, dtype=jnp.int32)).reshape(-1)
    )
    positions = jnp.concatenate(
        [past_len[tp_place] + token, past_len[0] + token, decode_positions]
    )
    rows_own = make_rows(latent, kv_gain, positions)
    fresh = jnp.pad(rows_own[2 * half_tokens :], ((0, 128 - pairs), (0, 0)))

    group_own = rows_own[: 2 * half_tokens].reshape(2, half_tokens, row_width)
    group_line = [group_own] + [fetch_ring(group_own, shift, 0) for shift in range(1, 4)]
    group_line = jnp.stack(group_line)
    group_lines = [group_line] + [fetch_ring(group_line, shift, 1) for shift in range(1, 4)]
    group_near = jnp.concatenate(group_lines)
    group_far = swap_core(group_near)
    outer = jnp.arange(4, dtype=jnp.int32)[:, None]
    inner = jnp.arange(4, dtype=jnp.int32)[None, :]

    def tokens_of(side):
        z_from = (z_place + outer + (inner - outer) * side) & 3
        x_from = (x_place + inner + (outer - inner) * side) & 3
        start = (z_from * 4 + x_from) * group_local + side * half_tokens
        return (start.reshape(seq_count, 1) + half_order[None, :]).reshape(1, -1)

    key_token = jnp.concatenate([tokens_of(core), tokens_of(1 - core)])

    targets = owner[:, 0]
    request_order = jnp.arange(request_local, dtype=jnp.int32)
    earlier = (targets[:, None] == targets[None, :]) & (
        request_order[None, :] < request_order[:, None]
    )
    slot_rank = jnp.sum(earlier.astype(jnp.int32), axis=1)
    destination = targets * pair_limit + slot_rank
    matches = jnp.arange(slot_count, dtype=jnp.int32)[:, None] == destination[None, :]
    source = jnp.sum(jnp.where(matches, request_order[None, :], 0), axis=1)
    send_length = jnp.sum(jnp.where(matches, dec_len[None, :], 0), axis=1)
    send_query = dispatch_queries(
        source,
        send_length,
        decode_query.reshape(request_local, query_pairs, row_width),
        row_width + 64,
    )
    arrived = lax.all_to_all(
        send_query.reshape(seq_count, pair_limit * query_pairs, row_width + 64),
        "seq",
        split_axis=0,
        concat_axis=0,
        tiled=True,
    ).reshape(slot_count, query_pairs, row_width + 64)
    arrived, group_query, _ = lax.optimization_barrier((arrived, group_query, group_line))
    queries = lax.all_to_all(group_query, "tp", split_axis=0, concat_axis=0, tiled=True)
    queries = queries.reshape(prompt_count, group_local * head_local, row_width)

    marks = arrived[:, 0, row_width:].astype(jnp.float32)
    slot_length = (marks[:, 0] * 16 + marks[:, 32]).astype(jnp.int32)

    is_used = slot_length > 0
    used_rank = jnp.cumsum(is_used.astype(jnp.int32)) - 1
    used = jnp.sum(is_used.astype(jnp.int32))
    slots = jnp.arange(slot_count, dtype=jnp.int32)
    wanted = jnp.minimum(slots, jnp.maximum(used - 1, 0))
    order = jnp.sum(
        jnp.where(is_used[None, :] & (used_rank[None, :] == wanted[:, None]), slots[None, :], 0),
        axis=1,
    )
    cache_latent, cache_lse = attend_cache(
        order, slot_length, used.reshape(1), arrived, jnp.swapaxes(decode_pool, 1, 2), lat, factor
    )
    cache_value = jnp.einsum(
        "nshc,hcv->nshv",
        cache_latent.reshape(slot_count, 2, head_local, lat),
        w_value,
        preferred_element_type=jnp.float32,
    ).astype(jnp.bfloat16)
    back = jnp.concatenate(
        [cache_value.reshape(slot_count, query_pairs, value_width), cache_lse], axis=-1
    )
    back = lax.all_to_all(
        back.reshape(seq_count, pair_limit * query_pairs, 2 * value_width),
        "seq",
        split_axis=0,
        concat_axis=0,
        tiled=True,
    ).reshape(slot_count, query_pairs, 2 * value_width)

    info = jnp.stack([past_len[tp_place], past_len[0], seq_place * group_local]).astype(jnp.int32)
    parts = 2
    sums = [
        attend_prefill(
            info,
            queries,
            past_all,
            group_near,
            group_far,
            key_token,
            part,
            parts,
            lat,
            factor,
            head_local,
        )
        for part in range(parts)
    ]
    sums[-1], decode_query = lax.optimization_barrier((sums[-1], decode_query))
    values = []
    for value in sums:
        value = lax.all_to_all(value, "tp", split_axis=0, concat_axis=0, tiled=True)
        values.append(
            jnp.einsum(
                "pthc,hcv->pthv",
                value.reshape(prompt_count, group_local // parts, head_local, lat),
                w_value,
                preferred_element_type=jnp.float32,
            ).astype(jnp.bfloat16)
        )
    prefill_out = jnp.concatenate(values, axis=1)
    near_latent, near_lse = attend_decode(
        info,
        decode_query.reshape(request_local * query_pairs, row_width),
        past_all,
        group_near,
        group_far,
        fresh,
        lat,
        factor,
        head_local,
    )
    near = jnp.einsum(
        "rshc,hcv->rshv",
        near_latent.reshape(request_local, 2, head_local, lat),
        w_value,
        preferred_element_type=jnp.float32,
    )
    decode_out = merge_decode(
        destination,
        back,
        near.reshape(request_local, query_pairs, value_width),
        near_lse.reshape(request_local, query_pairs, 128),
    ).reshape(request_local, 2, head_local, value_width)

    return (prefill_out, decode_out)


def solution(mesh):
    in_specs = (
        P(None, "seq", ("tp", "grp")),
        P(None, "seq", ("tp", "grp"), None),
        P(None, "seq", None),
        P(),
        P("seq", None, ("tp", "grp")),
        P("seq", None, ("tp", "grp"), None),
        P("seq", None, None),
        P("seq", None),
        P("seq"),
        P(("tp", "grp"), None),
        P(),
        P(("tp", "grp"), None, None),
    )
    out_specs = (P(None, "seq", ("tp", "grp"), None), P("seq", None, ("tp", "grp"), None))
    return jax.shard_map(
        on_device, mesh=mesh, in_specs=in_specs, out_specs=out_specs, check_vma=False
    )
```

```python
import functools

import jax
import jax.numpy as jnp
from jax import lax
from jax.experimental import pallas as pl
from jax.experimental.pallas import tpu as pltpu
from jax.sharding import PartitionSpec as P

epsilon = 1e-06
negative = -1e30
log2_e = 1.4426950408889634
NT = (((1,), (1,)), ((), ()))
NN = (((1,), (0,)), ((), ()))
VMEM_BYTES = 56 * 2**20


def rotate(rope_part, positions):
    half_width = rope_part.shape[-1] // 2
    frequency = jnp.exp(-jnp.log(10000.0) * jnp.arange(half_width).astype(jnp.float32) / half_width)
    angles = positions.astype(jnp.float32)[..., None] * frequency
    cosine = jnp.cos(angles)
    sine_part = jnp.sin(angles)
    former = rope_part[..., :half_width]
    latter = rope_part[..., half_width:]
    return jnp.concatenate(
        [former * cosine - latter * sine_part, latter * cosine + former * sine_part], axis=-1
    )


def make_rows(latent, kv_gain, positions):
    lat_width = kv_gain.shape[0]
    latent_part = latent[..., :lat_width]
    spread = jnp.mean(latent_part * latent_part, axis=-1, keepdims=True)
    normed = latent_part * lax.rsqrt(spread + epsilon) * kv_gain
    return jnp.concatenate([normed, rotate(latent[..., lat_width:], positions)], axis=-1).astype(
        jnp.bfloat16
    )


def dot(left, right, dims):
    return lax.dot_general(left, right, dims, preferred_element_type=jnp.float32)


def key_scores(queries, keys, lat, dims):
    if dims is NT:
        return dot(queries[:, :lat], keys[:, :lat], NT) + dot(queries[:, lat:], keys[:, lat:], NT)
    return dot(queries[:, :lat], keys[:lat], NN) + dot(queries[:, lat:], keys[lat:], NN)


def lane_fold(op, total, block):
    for start in range(0, block.shape[1], 128):
        part = block[:, start : start + 128]
        total = part if total is None else op(total, part)
    return total


def attend_tiles(config, count, load, store, hold, keys, masks):
    lat, factor = config
    for i in range(count):
        queries = load(i)
        row = lax.broadcasted_iota(jnp.int32, (queries.shape[0], 1), 0) + i * queries.shape[0]
        highest = None
        end = 0
        for block, mask in zip(keys, masks):
            values = block()
            scores = key_scores(queries, values, lat, NT)
            allowed = mask(row)
            if allowed is not None:
                scores = jnp.where(allowed, scores, negative)
            hold[i % 2, :, end : end + values.shape[0]] = scores
            end += values.shape[0]
            highest = lane_fold(jnp.maximum, highest, scores)
        peak = jnp.max(highest, axis=1, keepdims=True)
        total = None
        summed = None
        end = 0
        for block in keys:
            values = block()
            weights = jnp.exp2((hold[i % 2, :, end : end + values.shape[0]] - peak) * factor)
            end += values.shape[0]
            total = lane_fold(jnp.add, total, weights)
            part = dot(weights.astype(jnp.bfloat16), values[:, :lat], NN)
            summed = part if summed is None else summed + part
        total = jnp.sum(total, axis=1, keepdims=True)
        store(i, summed / total, peak * factor + jnp.log2(total))


def attend_body(config, chunk, head_local, info, q_ref, dq_ref, past_ref, near_ref, far_ref, *rest):
    fresh_ref, out_ref, decode_ref, lse_ref, hold = rest
    step = pl.program_id(0)
    tile = hold.shape[1]
    seq_count, _, piece_rows, width = past_ref.shape
    lines, half_tokens, _ = near_ref.shape
    held = chunk // (2 * piece_rows)
    past_count = seq_count // held
    past_len = info[jnp.maximum(step - 1, 0)]
    z_place, x_place, core = info[5], info[6], info[7]

    def past_keys(j):
        return lambda: past_ref[j * held : (j + 1) * held].reshape(chunk, width)

    def past_mask(j):
        def allowed(row):
            if 2 * (j + 1) <= past_count:
                return None
            return lax.broadcasted_iota(jnp.int32, (1, chunk), 1) + j * chunk < past_len

        return allowed

    def group_mask(side):
        def allowed(row):
            place = lax.broadcasted_iota(jnp.int32, (1, lines * half_tokens), 1)
            outer = place // (4 * half_tokens)
            inner = (place // half_tokens) & 3
            z_from = (z_place + outer + (inner - outer) * side) & 3
            x_from = (x_place + inner + (outer - inner) * side) & 3
            key_token = (z_from * 4 + x_from) * (2 * half_tokens) + side * half_tokens
            key_token = key_token + (place & (half_tokens - 1))
            return key_token <= info[4] + row // head_local

        return allowed

    def fresh_mask(row):
        place = lax.broadcasted_iota(jnp.int32, (1, fresh_ref.shape[0]), 1)
        return (place >= row // (2 * head_local) * 2) & (place <= row // head_local)

    keys = [past_keys(j) for j in range(past_count)]
    keys += [
        lambda: near_ref[...].reshape(lines * half_tokens, width),
        lambda: far_ref[...].reshape(lines * half_tokens, width),
    ]
    masks = [past_mask(j) for j in range(past_count)]

    @pl.when(step == 0)
    def _():
        def store(i, value, lse):
            decode_ref[i * tile : (i + 1) * tile, :] = value.astype(jnp.bfloat16)
            lse_ref[i * tile : (i + 1) * tile, :] = jnp.broadcast_to(lse, (tile, lse_ref.shape[1]))

        attend_tiles(
            config,
            dq_ref.shape[0] // tile,
            lambda i: dq_ref[i * tile : (i + 1) * tile, :],
            store,
            hold,
            keys + [lambda: fresh_ref[...]],
            masks + [lambda row: None, lambda row: None, fresh_mask],
        )

    @pl.when(step > 0)
    def _():
        def store(i, value, lse):
            out_ref[i * tile : (i + 1) * tile, :] = value.astype(jnp.bfloat16)

        attend_tiles(
            config,
            q_ref.shape[0] // tile,
            lambda i: q_ref[i * tile : (i + 1) * tile, :],
            store,
            hold,
            keys,
            masks + [group_mask(core), group_mask(1 - core)],
        )


def attend_all(info, query, decode_query, past, near, far, fresh, lat, factor, head_local):
    prompts, rows, width = query.shape
    decode_rows = decode_query.shape[0]
    seq_count, _, halves, piece_rows, _ = past.shape
    lines, _, half_tokens, _ = near.shape
    keys = seq_count * halves * piece_rows + 2 * lines * half_tokens + fresh.shape[0]
    tile = 256
    chunk = 768

    def prompt(i):
        return jnp.maximum(i - 1, 0)

    group_spec = pl.BlockSpec(
        (lines, None, half_tokens, width), lambda i, _: (0, prompt(i), 0, 0)
    )
    return pl.pallas_call(
        functools.partial(attend_body, (lat, factor), chunk, head_local),
        grid_spec=pltpu.PrefetchScalarGridSpec(
            num_scalar_prefetch=1,
            grid=(prompts + 1,),
            in_specs=[
                pl.BlockSpec((None, rows, width), lambda i, _: (prompt(i), 0, 0)),
                pl.BlockSpec((decode_rows, width), lambda i, _: (0, 0)),
                pl.BlockSpec(
                    (seq_count, None, halves, piece_rows, width),
                    lambda i, _: (0, prompt(i), 0, 0, 0),
                ),
                group_spec,
                group_spec,
                pl.BlockSpec(fresh.shape, lambda i, _: (0, 0)),
            ],
            out_specs=[
                pl.BlockSpec((None, rows, lat), lambda i, _: (prompt(i), 0, 0)),
                pl.BlockSpec((decode_rows, lat), lambda i, _: (0, 0)),
                pl.BlockSpec((decode_rows, 128), lambda i, _: (0, 0)),
            ],
            scratch_shapes=[pltpu.VMEM((2, tile, keys), jnp.float32)],
        ),
        out_shape=[
            jax.ShapeDtypeStruct((prompts, rows, lat), jnp.bfloat16),
            jax.ShapeDtypeStruct((decode_rows, lat), jnp.bfloat16),
            jax.ShapeDtypeStruct((decode_rows, 128), jnp.float32),
        ],
        compiler_params=pltpu.CompilerParams(vmem_limit_bytes=VMEM_BYTES),
        cost_estimate=pl.CostEstimate(
            flops=2 * (prompts * rows + decode_rows) * keys * (768 + lat),
            bytes_accessed=2 * prompts * (keys + 2 * rows) * width,
            transcendentals=(prompts * rows + decode_rows) * keys,
        ),
        name="attend_all",
    )(info, query, decode_query, past, near, far, fresh)


def dispatch_body(source, length, q_ref, out_ref):
    slots, rows, width = out_ref.shape
    lat_rope = q_ref.shape[2]
    lane = lax.broadcasted_iota(jnp.int32, (rows, width - lat_rope), 1)
    for slot in range(slots):
        out_ref[slot, :, :lat_rope] = q_ref[source[slot]]
        size = length[slot]
        tail = jnp.where(lane < 32, size >> 4, size & 15)
        out_ref[slot, :, lat_rope:] = tail.astype(jnp.float32).astype(jnp.bfloat16)


def dispatch_queries(source, length, query, width):
    slots = source.shape[0]
    _, rows, _ = query.shape
    smem = pl.BlockSpec(memory_space=pltpu.SMEM)
    vmem = pl.BlockSpec(memory_space=pltpu.VMEM)
    return pl.pallas_call(
        dispatch_body,
        in_specs=[smem, smem, vmem],
        out_specs=vmem,
        out_shape=jax.ShapeDtypeStruct((slots, rows, width), jnp.bfloat16),
        compiler_params=pltpu.CompilerParams(vmem_limit_bytes=VMEM_BYTES),
        name="dispatch_queries",
    )(source, length, query)


def cache_body(lat, factor, batch, order, length, used, q_ref, *rest):
    pool_refs = rest[:batch]
    out_ref, lse_ref = rest[batch:]
    step = pl.program_id(0)
    rows = q_ref.shape[1]
    width, cache_rows = pool_refs[0].shape

    @pl.when(step * batch < used[0])
    def _():
        place = lax.broadcasted_iota(jnp.int32, (1, cache_rows), 1)
        lane = lax.broadcasted_iota(jnp.int32, (rows, lse_ref.shape[2]), 1)
        slots = [order[step * batch + b] for b in range(batch)]
        scores = [
            key_scores(q_ref[slots[b], :, :width], pool_refs[b][...], lat, NN)
            for b in range(batch)
        ]
        for b in range(batch):
            masked = jnp.where(place < length[slots[b]], scores[b], negative)
            peak = jnp.max(masked, axis=1, keepdims=True)
            weights = jnp.exp2((masked - peak) * factor)
            total = jnp.sum(weights, axis=1, keepdims=True)
            summed = dot(weights.astype(jnp.bfloat16), pool_refs[b][:lat], NT)
            out_ref[slots[b]] = (summed / total).astype(jnp.bfloat16)
            lse = peak * factor + jnp.log2(total)
            high = lse.astype(jnp.bfloat16).astype(jnp.float32)
            middle = (lse - high).astype(jnp.bfloat16).astype(jnp.float32)
            low = lse - high - middle
            lse_ref[slots[b]] = jnp.where(
                lane == 0, high, jnp.where(lane == 1, middle, low)
            ).astype(jnp.bfloat16)


def attend_cache(order, length, used, query, pool, lat, factor):
    batch = 4
    slots, rows, padded = query.shape
    _, width, cache_rows = pool.shape
    whole = pl.BlockSpec((slots, rows, padded), lambda i, *_: (0, 0, 0))

    def pool_spec(b):
        return pl.BlockSpec(
            (None, width, cache_rows), lambda i, order, *_: (order[i * batch + b], 0, 0)
        )

    return pl.pallas_call(
        functools.partial(cache_body, lat, factor, batch),
        grid_spec=pltpu.PrefetchScalarGridSpec(
            num_scalar_prefetch=3,
            grid=(slots // batch,),
            in_specs=[whole] + [pool_spec(b) for b in range(batch)],
            out_specs=[
                pl.BlockSpec((slots, rows, lat), lambda i, *_: (0, 0, 0)),
                pl.BlockSpec((slots, rows, 128), lambda i, *_: (0, 0, 0)),
            ],
        ),
        out_shape=[
            jax.ShapeDtypeStruct((slots, rows, lat), jnp.bfloat16),
            jax.ShapeDtypeStruct((slots, rows, 128), jnp.bfloat16),
        ],
        compiler_params=pltpu.CompilerParams(vmem_limit_bytes=VMEM_BYTES),
        cost_estimate=pl.CostEstimate(
            flops=2 * slots * 128 * cache_rows * (width + lat),
            bytes_accessed=2 * slots * cache_rows * width,
            transcendentals=slots * rows * cache_rows,
        ),
        name="attend_cache",
    )(order, length, used, query, *([pool] * batch))


def merge_body(slot, back_ref, near_ref, near_lse_ref, out_ref):
    count = near_ref.shape[0]
    width = near_ref.shape[2]
    for r in range(count):
        back = back_ref[slot[r]].astype(jnp.float32)
        far = back[:, :width]
        far_lse = back[:, width : width + 1] + back[:, width + 1 : width + 2]
        far_lse = far_lse + back[:, width + 2 : width + 3]
        near_lse = near_lse_ref[r][:, :1]
        peak = jnp.maximum(far_lse, near_lse)
        far_part = jnp.exp2(far_lse - peak)
        near_part = jnp.exp2(near_lse - peak)
        mixed = far * far_part + near_ref[r] * near_part
        out_ref[r] = (mixed / (far_part + near_part)).astype(jnp.bfloat16)


def merge_decode(slot, back, near, near_lse):
    smem = pl.BlockSpec(memory_space=pltpu.SMEM)
    vmem = pl.BlockSpec(memory_space=pltpu.VMEM)
    return pl.pallas_call(
        merge_body,
        in_specs=[smem, vmem, vmem, vmem],
        out_specs=vmem,
        out_shape=jax.ShapeDtypeStruct(near.shape, jnp.bfloat16),
        compiler_params=pltpu.CompilerParams(vmem_limit_bytes=VMEM_BYTES),
        name="merge_decode",
    )(slot, back, near, near_lse)


def swap_core(value):
    return lax.ppermute(value, "grp", [(0, 1), (1, 0)])


def fetch_tp(value, shift):
    return lax.ppermute(value, "tp", [((i + shift) % 4, i) for i in range(4)])


def fetch_ring(value, shift, turn):
    moves = []
    for i in range(16):
        z, x = i // 4, i % 4
        for c in range(2):
            if (c + turn) % 2 == 0:
                origin = z * 4 + (x + shift) % 4
            else:
                origin = (z + shift) % 4 * 4 + x
            moves.append((origin * 2 + c, i * 2 + c))
    return lax.ppermute(value, ("seq", "grp"), moves)


def on_device(
    group_hidden,
    group_query,
    past_cache,
    past_len,
    decode_hidden,
    decode_query,
    decode_pool,
    owner,
    dec_len,
    w_latent,
    kv_gain,
    w_value,
):
    seq_count = lax.axis_size("seq")
    seq_place = lax.axis_index("seq")
    tp_place = lax.axis_index("tp")
    core = lax.axis_index("grp")
    z_place, x_place = seq_place >> 2, seq_place & 3
    prompt_count, group_local, head_local, row_width = group_query.shape
    past_local = past_cache.shape[1]
    request_local = decode_query.shape[0]
    lat = kv_gain.shape[0]
    value_width = w_value.shape[2]
    slot_count = decode_pool.shape[0]
    pair_limit = slot_count // seq_count
    query_pairs = 2 * head_local
    factor = (value_width + row_width - lat) ** (-0.5) * log2_e

    half = past_local // 2
    past_part = lax.dynamic_slice(past_cache, (tp_place, core * half, 0), (1, half, row_width))
    past_all = lax.all_gather(
        past_part.reshape(half, row_width), ("seq", "tp", "grp"), axis=0, tiled=False
    ).reshape(seq_count, prompt_count, 2, half, row_width)

    half_tokens = group_local // 2
    pairs = 2 * request_local
    partial_group = jnp.einsum(
        "ptd,dc->ptc", group_hidden, w_latent, preferred_element_type=jnp.float32
    ).astype(jnp.bfloat16)
    partial_group = partial_group.reshape(prompt_count, 2, half_tokens, row_width)
    partial_decode = jnp.einsum(
        "rd,dc->rc",
        decode_hidden.reshape(pairs, -1),
        w_latent,
        preferred_element_type=jnp.float32,
    ).astype(jnp.bfloat16)
    group_part = prompt_count * half_tokens

    def both(chosen):
        part = lax.dynamic_index_in_dim(partial_group, chosen, axis=1, keepdims=False)
        return jnp.concatenate([part.reshape(group_part, row_width), partial_decode])

    pair_sum = both(core).astype(jnp.float32) + swap_core(both(1 - core)).astype(jnp.float32)
    pair_sum = pair_sum.astype(jnp.bfloat16)

    latent = pair_sum.astype(jnp.float32)
    for shift in range(1, 4):
        latent = latent + fetch_tp(pair_sum, shift).astype(jnp.float32)
    half_order = jnp.arange(half_tokens, dtype=jnp.int32)
    group_positions = (
        past_len[:, None] + seq_place * group_local + core * half_tokens + half_order[None, :]
    )
    decode_positions = (
        past_len[0]
        + group_local * seq_count
        + (dec_len[:, None] + jnp.arange(2, dtype=jnp.int32)).reshape(-1)
    )
    positions = jnp.concatenate([group_positions.reshape(-1), decode_positions])
    rows_own = make_rows(latent, kv_gain, positions)
    fresh = jnp.pad(rows_own[group_part:], ((0, 128 - pairs), (0, 0)))

    group_own = rows_own[:group_part].reshape(prompt_count, half_tokens, row_width)
    group_line = [group_own] + [fetch_ring(group_own, shift, 0) for shift in range(1, 4)]
    group_line = jnp.stack(group_line)
    group_lines = [group_line] + [fetch_ring(group_line, shift, 1) for shift in range(1, 4)]
    group_near = jnp.concatenate(group_lines)
    group_far = swap_core(group_near)

    targets = owner[:, 0]
    request_order = jnp.arange(request_local, dtype=jnp.int32)
    earlier = (targets[:, None] == targets[None, :]) & (
        request_order[None, :] < request_order[:, None]
    )
    slot_rank = jnp.sum(earlier.astype(jnp.int32), axis=1)
    destination = targets * pair_limit + slot_rank
    matches = jnp.arange(slot_count, dtype=jnp.int32)[:, None] == destination[None, :]
    source = jnp.sum(jnp.where(matches, request_order[None, :], 0), axis=1)
    send_length = jnp.sum(jnp.where(matches, dec_len[None, :], 0), axis=1)
    send_query = dispatch_queries(
        source,
        send_length,
        decode_query.reshape(request_local, query_pairs, row_width),
        row_width + 64,
    )
    arrived = lax.all_to_all(
        send_query.reshape(seq_count, pair_limit * query_pairs, row_width + 64),
        "seq",
        split_axis=0,
        concat_axis=0,
        tiled=True,
    ).reshape(slot_count, query_pairs, row_width + 64)
    marks = arrived[:, 0, row_width:].astype(jnp.float32)
    slot_length = (marks[:, 0] * 16 + marks[:, 32]).astype(jnp.int32)

    is_used = slot_length > 0
    used_rank = jnp.cumsum(is_used.astype(jnp.int32)) - 1
    used = jnp.sum(is_used.astype(jnp.int32))
    slots = jnp.arange(slot_count, dtype=jnp.int32)
    wanted = jnp.minimum(slots, jnp.maximum(used - 1, 0))
    order = jnp.sum(
        jnp.where(is_used[None, :] & (used_rank[None, :] == wanted[:, None]), slots[None, :], 0),
        axis=1,
    )
    cache_latent, cache_lse = attend_cache(
        order, slot_length, used.reshape(1), arrived, jnp.swapaxes(decode_pool, 1, 2), lat, factor
    )
    cache_value = jnp.einsum(
        "nshc,hcv->nshv",
        cache_latent.reshape(slot_count, 2, head_local, lat),
        w_value,
        preferred_element_type=jnp.float32,
    ).astype(jnp.bfloat16)
    back = jnp.concatenate(
        [cache_value.reshape(slot_count, query_pairs, value_width), cache_lse], axis=-1
    )
    back = lax.all_to_all(
        back.reshape(seq_count, pair_limit * query_pairs, 2 * value_width),
        "seq",
        split_axis=0,
        concat_axis=0,
        tiled=True,
    ).reshape(slot_count, query_pairs, 2 * value_width)

    info = jnp.stack(
        [past_len[p] for p in range(prompt_count)]
        + [seq_place * group_local, z_place, x_place, core]
    ).astype(jnp.int32)
    group_query, _ = lax.optimization_barrier((group_query, cache_value))
    prefill_latent, near_latent, near_lse = attend_all(
        info,
        group_query.reshape(prompt_count, group_local * head_local, row_width),
        decode_query.reshape(request_local * query_pairs, row_width),
        past_all,
        group_near,
        group_far,
        fresh,
        lat,
        factor,
        head_local,
    )
    near = jnp.einsum(
        "rshc,hcv->rshv",
        near_latent.reshape(request_local, 2, head_local, lat),
        w_value,
        preferred_element_type=jnp.float32,
    )
    decode_out = merge_decode(
        destination,
        back,
        near.reshape(request_local, query_pairs, value_width),
        near_lse.reshape(request_local, query_pairs, 128),
    ).reshape(request_local, 2, head_local, value_width)

    prefill_out = jnp.einsum(
        "pthc,hcv->pthv",
        prefill_latent.reshape(prompt_count, group_local, head_local, lat),
        w_value,
        preferred_element_type=jnp.float32,
    ).astype(jnp.bfloat16)
    return (prefill_out, decode_out)


def solution(mesh):
    in_specs = (
        P(None, "seq", ("tp", "grp")),
        P(None, "seq", ("tp", "grp"), None),
        P(None, "seq", None),
        P(),
        P("seq", None, ("tp", "grp")),
        P("seq", None, ("tp", "grp"), None),
        P("seq", None, None),
        P("seq", None),
        P("seq"),
        P(("tp", "grp"), None),
        P(),
        P(("tp", "grp"), None, None),
    )
    out_specs = (P(None, "seq", ("tp", "grp"), None), P("seq", None, ("tp", "grp"), None))
    return jax.shard_map(
        on_device, mesh=mesh, in_specs=in_specs, out_specs=out_specs, check_vma=False
    )
```

```python
import functools

import jax
import jax.numpy as jnp
from jax import lax
from jax.experimental import pallas as pl
from jax.experimental.pallas import tpu as pltpu
from jax.sharding import PartitionSpec as P

epsilon = 1e-06
negative = -1e30
log2_e = 1.4426950408889634
NT = (((1,), (1,)), ((), ()))
NN = (((1,), (0,)), ((), ()))
VMEM_BYTES = 56 * 2**20


def rotate(rope_part, positions):
    half_width = rope_part.shape[-1] // 2
    frequency = jnp.exp(-jnp.log(10000.0) * jnp.arange(half_width).astype(jnp.float32) / half_width)
    angles = positions.astype(jnp.float32)[..., None] * frequency
    cosine = jnp.cos(angles)
    sine_part = jnp.sin(angles)
    former = rope_part[..., :half_width]
    latter = rope_part[..., half_width:]
    return jnp.concatenate(
        [former * cosine - latter * sine_part, latter * cosine + former * sine_part], axis=-1
    )


def make_rows(latent, kv_gain, positions):
    lat_width = kv_gain.shape[0]
    latent_part = latent[..., :lat_width]
    spread = jnp.mean(latent_part * latent_part, axis=-1, keepdims=True)
    normed = latent_part * lax.rsqrt(spread + epsilon) * kv_gain
    return jnp.concatenate([normed, rotate(latent[..., lat_width:], positions)], axis=-1).astype(
        jnp.bfloat16
    )


def dot(left, right, dims):
    return lax.dot_general(left, right, dims, preferred_element_type=jnp.float32)


def key_scores(queries, keys, lat, dims):
    if dims is NT:
        return dot(queries[:, :lat], keys[:, :lat], NT) + dot(queries[:, lat:], keys[:, lat:], NT)
    return dot(queries[:, :lat], keys[:lat], NN) + dot(queries[:, lat:], keys[lat:], NN)


def lane_fold(op, total, block):
    for start in range(0, block.shape[1], 128):
        part = block[:, start : start + 128]
        total = part if total is None else op(total, part)
    return total


def attend_tiles(config, count, load, store, hold, keys, masks):
    lat, factor = config
    for i in range(count):
        queries = load(i)
        row = lax.broadcasted_iota(jnp.int32, (queries.shape[0], 1), 0) + i * queries.shape[0]
        highest = None
        end = 0
        for block, mask in zip(keys, masks):
            values = block()
            scores = key_scores(queries, values, lat, NT)
            allowed = mask(row)
            if allowed is not None:
                scores = jnp.where(allowed, scores, negative)
            hold[i % 2, :, end : end + values.shape[0]] = scores
            end += values.shape[0]
            highest = lane_fold(jnp.maximum, highest, scores)
        peak = jnp.max(highest, axis=1, keepdims=True)
        total = None
        summed = None
        end = 0
        for block in keys:
            values = block()
            weights = jnp.exp2((hold[i % 2, :, end : end + values.shape[0]] - peak) * factor)
            end += values.shape[0]
            total = lane_fold(jnp.add, total, weights)
            part = dot(weights.astype(jnp.bfloat16), values[:, :lat], NN)
            summed = part if summed is None else summed + part
        total = jnp.sum(total, axis=1, keepdims=True)
        store(i, summed / total, peak * factor + jnp.log2(total))


def attend_body(config, chunk, head_local, info, q_ref, dq_ref, near_ref, far_ref, fresh_ref, *rest):
    pieces = rest[:8]
    out_ref, decode_ref, lse_ref, hold, past, arrive = rest[8:]
    step = pl.program_id(0)
    prompts = pl.num_programs(0) - 1
    tile = hold.shape[1]
    _, holders, piece_rows, width = past.shape
    lines, half_tokens, _ = near_ref.shape
    held = chunk // piece_rows
    past_count = holders // held
    prompt = jnp.maximum(step - 1, 0)
    slot = prompt & 1
    past_len = info[prompt]
    z_place, x_place, core = info[5], info[6], info[7]

    def copies(p):
        made = []
        for c in range(2):
            side = core if c == 0 else 1 - core
            for s in range(4):
                for j in range(4):
                    dz = s + (j - s) * side
                    dx = j + (s - j) * side
                    holder = ((z_place + dz) & 3) * 4 + ((x_place + dx) & 3)
                    made.append(
                        pltpu.make_async_copy(
                            pieces[c * 4 + s].at[j, p],
                            past.at[p & 1, holder * 2 + side],
                            arrive.at[p & 1, c * 16 + s * 4 + j],
                        )
                    )
        return made

    @pl.when(step == 0)
    def _():
        for copy in copies(0):
            copy.start()

    @pl.when((step > 0) & (step < prompts))
    def _():
        for copy in copies(step):
            copy.start()

    @pl.when(step != 1)
    def _():
        for copy in copies(prompt):
            copy.wait()

    def past_keys(j):
        return lambda: past[slot, j * held : (j + 1) * held].reshape(chunk, width)

    def past_mask(j):
        def allowed(row):
            if 2 * (j + 1) <= past_count:
                return None
            return lax.broadcasted_iota(jnp.int32, (1, chunk), 1) + j * chunk < past_len

        return allowed

    def group_mask(side):
        def allowed(row):
            place = lax.broadcasted_iota(jnp.int32, (1, lines * half_tokens), 1)
            outer = place // (4 * half_tokens)
            inner = (place // half_tokens) & 3
            z_from = (z_place + outer + (inner - outer) * side) & 3
            x_from = (x_place + inner + (outer - inner) * side) & 3
            key_token = (z_from * 4 + x_from) * (2 * half_tokens) + side * half_tokens
            key_token = key_token + (place & (half_tokens - 1))
            return key_token <= info[4] + row // head_local

        return allowed

    def fresh_mask(row):
        place = lax.broadcasted_iota(jnp.int32, (1, fresh_ref.shape[0]), 1)
        return (place >= row // (2 * head_local) * 2) & (place <= row // head_local)

    keys = [past_keys(j) for j in range(past_count)]
    keys += [
        lambda: near_ref[...].reshape(lines * half_tokens, width),
        lambda: far_ref[...].reshape(lines * half_tokens, width),
    ]
    masks = [past_mask(j) for j in range(past_count)]

    @pl.when(step == 0)
    def _():
        def store(i, value, lse):
            decode_ref[i * tile : (i + 1) * tile, :] = value.astype(jnp.bfloat16)
            lse_ref[i * tile : (i + 1) * tile, :] = jnp.broadcast_to(lse, (tile, lse_ref.shape[1]))

        attend_tiles(
            config,
            dq_ref.shape[0] // tile,
            lambda i: dq_ref[i * tile : (i + 1) * tile, :],
            store,
            hold,
            keys + [lambda: fresh_ref[...]],
            masks + [lambda row: None, lambda row: None, fresh_mask],
        )

    @pl.when(step > 0)
    def _():
        def store(i, value, lse):
            out_ref[i * tile : (i + 1) * tile, :] = value.astype(jnp.bfloat16)

        attend_tiles(
            config,
            q_ref.shape[0] // tile,
            lambda i: q_ref[i * tile : (i + 1) * tile, :],
            store,
            hold,
            keys,
            masks + [group_mask(core), group_mask(1 - core)],
        )


def attend_all(info, query, decode_query, pieces, near, far, fresh, lat, factor, head_local):
    prompts, rows, width = query.shape
    decode_rows = decode_query.shape[0]
    piece_rows = pieces[0].shape[2]
    holders = 4 * len(pieces)
    lines, _, half_tokens, _ = near.shape
    keys = holders * piece_rows + 2 * lines * half_tokens + fresh.shape[0]
    tile = 256
    chunk = 768

    def prompt(i):
        return jnp.maximum(i - 1, 0)

    group_spec = pl.BlockSpec(
        (lines, None, half_tokens, width), lambda i, _: (0, prompt(i), 0, 0)
    )
    return pl.pallas_call(
        functools.partial(attend_body, (lat, factor), chunk, head_local),
        grid_spec=pltpu.PrefetchScalarGridSpec(
            num_scalar_prefetch=1,
            grid=(prompts + 1,),
            in_specs=[
                pl.BlockSpec((None, rows, width), lambda i, _: (prompt(i), 0, 0)),
                pl.BlockSpec((decode_rows, width), lambda i, _: (0, 0)),
                group_spec,
                group_spec,
                pl.BlockSpec(fresh.shape, lambda i, _: (0, 0)),
            ]
            + [pl.BlockSpec(memory_space=pl.ANY)] * len(pieces),
            out_specs=[
                pl.BlockSpec((None, rows, lat), lambda i, _: (prompt(i), 0, 0)),
                pl.BlockSpec((decode_rows, lat), lambda i, _: (0, 0)),
                pl.BlockSpec((decode_rows, 128), lambda i, _: (0, 0)),
            ],
            scratch_shapes=[
                pltpu.VMEM((2, tile, keys), jnp.float32),
                pltpu.VMEM((2, holders, piece_rows, width), jnp.bfloat16),
                pltpu.SemaphoreType.DMA((2, holders)),
            ],
        ),
        out_shape=[
            jax.ShapeDtypeStruct((prompts, rows, lat), jnp.bfloat16),
            jax.ShapeDtypeStruct((decode_rows, lat), jnp.bfloat16),
            jax.ShapeDtypeStruct((decode_rows, 128), jnp.float32),
        ],
        compiler_params=pltpu.CompilerParams(vmem_limit_bytes=VMEM_BYTES),
        cost_estimate=pl.CostEstimate(
            flops=2 * (prompts * rows + decode_rows) * keys * (768 + lat),
            bytes_accessed=2 * prompts * (keys + 2 * rows) * width,
            transcendentals=(prompts * rows + decode_rows) * keys,
        ),
        name="attend_all",
    )(info, query, decode_query, near, far, fresh, *pieces)


def dispatch_body(source, length, q_ref, out_ref):
    slots, rows, width = out_ref.shape
    lat_rope = q_ref.shape[2]
    lane = lax.broadcasted_iota(jnp.int32, (rows, width - lat_rope), 1)
    for slot in range(slots):
        out_ref[slot, :, :lat_rope] = q_ref[source[slot]]
        size = length[slot]
        tail = jnp.where(lane < 32, size >> 4, size & 15)
        out_ref[slot, :, lat_rope:] = tail.astype(jnp.float32).astype(jnp.bfloat16)


def dispatch_queries(source, length, query, width):
    slots = source.shape[0]
    _, rows, _ = query.shape
    smem = pl.BlockSpec(memory_space=pltpu.SMEM)
    vmem = pl.BlockSpec(memory_space=pltpu.VMEM)
    return pl.pallas_call(
        dispatch_body,
        in_specs=[smem, smem, vmem],
        out_specs=vmem,
        out_shape=jax.ShapeDtypeStruct((slots, rows, width), jnp.bfloat16),
        compiler_params=pltpu.CompilerParams(vmem_limit_bytes=VMEM_BYTES),
        name="dispatch_queries",
    )(source, length, query)


def cache_body(lat, factor, batch, order, length, used, q_ref, *rest):
    pool_refs = rest[:batch]
    out_ref, lse_ref = rest[batch:]
    step = pl.program_id(0)
    rows = q_ref.shape[1]
    width, cache_rows = pool_refs[0].shape

    @pl.when(step * batch < used[0])
    def _():
        place = lax.broadcasted_iota(jnp.int32, (1, cache_rows), 1)
        lane = lax.broadcasted_iota(jnp.int32, (rows, lse_ref.shape[2]), 1)
        slots = [order[step * batch + b] for b in range(batch)]
        scores = [
            key_scores(q_ref[slots[b], :, :width], pool_refs[b][...], lat, NN)
            for b in range(batch)
        ]
        for b in range(batch):
            masked = jnp.where(place < length[slots[b]], scores[b], negative)
            peak = jnp.max(masked, axis=1, keepdims=True)
            weights = jnp.exp2((masked - peak) * factor)
            total = jnp.sum(weights, axis=1, keepdims=True)
            summed = dot(weights.astype(jnp.bfloat16), pool_refs[b][:lat], NT)
            out_ref[slots[b]] = (summed / total).astype(jnp.bfloat16)
            lse = peak * factor + jnp.log2(total)
            high = lse.astype(jnp.bfloat16).astype(jnp.float32)
            middle = (lse - high).astype(jnp.bfloat16).astype(jnp.float32)
            low = lse - high - middle
            lse_ref[slots[b]] = jnp.where(
                lane == 0, high, jnp.where(lane == 1, middle, low)
            ).astype(jnp.bfloat16)


def attend_cache(order, length, used, query, pool, lat, factor):
    batch = 4
    slots, rows, padded = query.shape
    _, width, cache_rows = pool.shape
    whole = pl.BlockSpec((slots, rows, padded), lambda i, *_: (0, 0, 0))

    def pool_spec(b):
        return pl.BlockSpec(
            (None, width, cache_rows), lambda i, order, *_: (order[i * batch + b], 0, 0)
        )

    return pl.pallas_call(
        functools.partial(cache_body, lat, factor, batch),
        grid_spec=pltpu.PrefetchScalarGridSpec(
            num_scalar_prefetch=3,
            grid=(slots // batch,),
            in_specs=[whole] + [pool_spec(b) for b in range(batch)],
            out_specs=[
                pl.BlockSpec((slots, rows, lat), lambda i, *_: (0, 0, 0)),
                pl.BlockSpec((slots, rows, 128), lambda i, *_: (0, 0, 0)),
            ],
        ),
        out_shape=[
            jax.ShapeDtypeStruct((slots, rows, lat), jnp.bfloat16),
            jax.ShapeDtypeStruct((slots, rows, 128), jnp.bfloat16),
        ],
        compiler_params=pltpu.CompilerParams(vmem_limit_bytes=VMEM_BYTES),
        cost_estimate=pl.CostEstimate(
            flops=2 * slots * 128 * cache_rows * (width + lat),
            bytes_accessed=2 * slots * cache_rows * width,
            transcendentals=slots * rows * cache_rows,
        ),
        name="attend_cache",
    )(order, length, used, query, *([pool] * batch))


def merge_body(slot, back_ref, near_ref, near_lse_ref, out_ref):
    count = near_ref.shape[0]
    width = near_ref.shape[2]
    for r in range(count):
        back = back_ref[slot[r]].astype(jnp.float32)
        far = back[:, :width]
        far_lse = back[:, width : width + 1] + back[:, width + 1 : width + 2]
        far_lse = far_lse + back[:, width + 2 : width + 3]
        near_lse = near_lse_ref[r][:, :1]
        peak = jnp.maximum(far_lse, near_lse)
        far_part = jnp.exp2(far_lse - peak)
        near_part = jnp.exp2(near_lse - peak)
        mixed = far * far_part + near_ref[r] * near_part
        out_ref[r] = (mixed / (far_part + near_part)).astype(jnp.bfloat16)


def merge_decode(slot, back, near, near_lse):
    smem = pl.BlockSpec(memory_space=pltpu.SMEM)
    vmem = pl.BlockSpec(memory_space=pltpu.VMEM)
    return pl.pallas_call(
        merge_body,
        in_specs=[smem, vmem, vmem, vmem],
        out_specs=vmem,
        out_shape=jax.ShapeDtypeStruct(near.shape, jnp.bfloat16),
        compiler_params=pltpu.CompilerParams(vmem_limit_bytes=VMEM_BYTES),
        name="merge_decode",
    )(slot, back, near, near_lse)


def swap_core(value):
    return lax.ppermute(value, "grp", [(0, 1), (1, 0)])


def fetch_tp(value, shift):
    return lax.ppermute(value, "tp", [((i + shift) % 4, i) for i in range(4)])


def fetch_ring(value, shift, turn):
    moves = []
    for i in range(16):
        z, x = i // 4, i % 4
        for c in range(2):
            if (c + turn) % 2 == 0:
                origin = z * 4 + (x + shift) % 4
            else:
                origin = (z + shift) % 4 * 4 + x
            moves.append((origin * 2 + c, i * 2 + c))
    return lax.ppermute(value, ("seq", "grp"), moves)


def on_device(
    group_hidden,
    group_query,
    past_cache,
    past_len,
    decode_hidden,
    decode_query,
    decode_pool,
    owner,
    dec_len,
    w_latent,
    kv_gain,
    w_value,
):
    seq_count = lax.axis_size("seq")
    seq_place = lax.axis_index("seq")
    core = lax.axis_index("grp")
    z_place, x_place = seq_place >> 2, seq_place & 3
    prompt_count, group_local, head_local, row_width = group_query.shape
    past_local = past_cache.shape[1]
    request_local = decode_query.shape[0]
    lat = kv_gain.shape[0]
    value_width = w_value.shape[2]
    slot_count = decode_pool.shape[0]
    pair_limit = slot_count // seq_count
    query_pairs = 2 * head_local
    factor = (value_width + row_width - lat) ** (-0.5) * log2_e

    half = past_local // 2
    past_half = lax.dynamic_slice_in_dim(past_cache, core * half, half, axis=1)
    past_line = [past_half] + [fetch_ring(past_half, shift, 0) for shift in range(1, 4)]
    past_line = jnp.stack(past_line)
    past_lines = [past_line] + [fetch_ring(past_line, shift, 1) for shift in range(1, 4)]
    past_lines = past_lines + [swap_core(piece) for piece in past_lines]

    half_tokens = group_local // 2
    pairs = 2 * request_local
    partial_group = jnp.einsum(
        "ptd,dc->ptc", group_hidden, w_latent, preferred_element_type=jnp.float32
    ).astype(jnp.bfloat16)
    partial_group = partial_group.reshape(prompt_count, 2, half_tokens, row_width)
    partial_decode = jnp.einsum(
        "rd,dc->rc",
        decode_hidden.reshape(pairs, -1),
        w_latent,
        preferred_element_type=jnp.float32,
    ).astype(jnp.bfloat16)
    group_part = prompt_count * half_tokens

    def both(chosen):
        part = lax.dynamic_index_in_dim(partial_group, chosen, axis=1, keepdims=False)
        return jnp.concatenate([part.reshape(group_part, row_width), partial_decode])

    pair_sum = both(core).astype(jnp.float32) + swap_core(both(1 - core)).astype(jnp.float32)
    pair_sum = pair_sum.astype(jnp.bfloat16)

    pair_sum, decode_query, _ = lax.optimization_barrier((pair_sum, decode_query, past_line))
    latent = pair_sum.astype(jnp.float32)
    for shift in range(1, 4):
        latent = latent + fetch_tp(pair_sum, shift).astype(jnp.float32)
    half_order = jnp.arange(half_tokens, dtype=jnp.int32)
    group_positions = (
        past_len[:, None] + seq_place * group_local + core * half_tokens + half_order[None, :]
    )
    decode_positions = (
        past_len[0]
        + group_local * seq_count
        + (dec_len[:, None] + jnp.arange(2, dtype=jnp.int32)).reshape(-1)
    )
    positions = jnp.concatenate([group_positions.reshape(-1), decode_positions])
    rows_own = make_rows(latent, kv_gain, positions)
    fresh = jnp.pad(rows_own[group_part:], ((0, 128 - pairs), (0, 0)))

    group_own = rows_own[:group_part].reshape(prompt_count, half_tokens, row_width)
    group_line = [group_own] + [fetch_ring(group_own, shift, 0) for shift in range(1, 4)]
    group_line = jnp.stack(group_line)
    group_lines = [group_line] + [fetch_ring(group_line, shift, 1) for shift in range(1, 4)]
    group_near = jnp.concatenate(group_lines)
    group_far = swap_core(group_near)

    targets = owner[:, 0]
    request_order = jnp.arange(request_local, dtype=jnp.int32)
    earlier = (targets[:, None] == targets[None, :]) & (
        request_order[None, :] < request_order[:, None]
    )
    slot_rank = jnp.sum(earlier.astype(jnp.int32), axis=1)
    destination = targets * pair_limit + slot_rank
    matches = jnp.arange(slot_count, dtype=jnp.int32)[:, None] == destination[None, :]
    source = jnp.sum(jnp.where(matches, request_order[None, :], 0), axis=1)
    send_length = jnp.sum(jnp.where(matches, dec_len[None, :], 0), axis=1)
    send_query = dispatch_queries(
        source,
        send_length,
        decode_query.reshape(request_local, query_pairs, row_width),
        row_width + 64,
    )
    arrived = lax.all_to_all(
        send_query.reshape(seq_count, pair_limit * query_pairs, row_width + 64),
        "seq",
        split_axis=0,
        concat_axis=0,
        tiled=True,
    ).reshape(slot_count, query_pairs, row_width + 64)
    marks = arrived[:, 0, row_width:].astype(jnp.float32)
    slot_length = (marks[:, 0] * 16 + marks[:, 32]).astype(jnp.int32)

    is_used = slot_length > 0
    used_rank = jnp.cumsum(is_used.astype(jnp.int32)) - 1
    used = jnp.sum(is_used.astype(jnp.int32))
    slots = jnp.arange(slot_count, dtype=jnp.int32)
    wanted = jnp.minimum(slots, jnp.maximum(used - 1, 0))
    order = jnp.sum(
        jnp.where(is_used[None, :] & (used_rank[None, :] == wanted[:, None]), slots[None, :], 0),
        axis=1,
    )
    cache_latent, cache_lse = attend_cache(
        order, slot_length, used.reshape(1), arrived, jnp.swapaxes(decode_pool, 1, 2), lat, factor
    )
    cache_value = jnp.einsum(
        "nshc,hcv->nshv",
        cache_latent.reshape(slot_count, 2, head_local, lat),
        w_value,
        preferred_element_type=jnp.float32,
    ).astype(jnp.bfloat16)
    back = jnp.concatenate(
        [cache_value.reshape(slot_count, query_pairs, value_width), cache_lse], axis=-1
    )
    back = lax.all_to_all(
        back.reshape(seq_count, pair_limit * query_pairs, 2 * value_width),
        "seq",
        split_axis=0,
        concat_axis=0,
        tiled=True,
    ).reshape(slot_count, query_pairs, 2 * value_width)

    info = jnp.stack(
        [past_len[p] for p in range(prompt_count)]
        + [seq_place * group_local, z_place, x_place, core]
    ).astype(jnp.int32)
    group_query, _ = lax.optimization_barrier((group_query, cache_value))
    prefill_latent, near_latent, near_lse = attend_all(
        info,
        group_query.reshape(prompt_count, group_local * head_local, row_width),
        decode_query.reshape(request_local * query_pairs, row_width),
        past_lines,
        group_near,
        group_far,
        fresh,
        lat,
        factor,
        head_local,
    )
    near = jnp.einsum(
        "rshc,hcv->rshv",
        near_latent.reshape(request_local, 2, head_local, lat),
        w_value,
        preferred_element_type=jnp.float32,
    )
    decode_out = merge_decode(
        destination,
        back,
        near.reshape(request_local, query_pairs, value_width),
        near_lse.reshape(request_local, query_pairs, 128),
    ).reshape(request_local, 2, head_local, value_width)

    prefill_out = jnp.einsum(
        "pthc,hcv->pthv",
        prefill_latent.reshape(prompt_count, group_local, head_local, lat),
        w_value,
        preferred_element_type=jnp.float32,
    ).astype(jnp.bfloat16)
    return (prefill_out, decode_out)


def solution(mesh):
    in_specs = (
        P(None, "seq", ("tp", "grp")),
        P(None, "seq", ("tp", "grp"), None),
        P(None, "seq", None),
        P(),
        P("seq", None, ("tp", "grp")),
        P("seq", None, ("tp", "grp"), None),
        P("seq", None, None),
        P("seq", None),
        P("seq"),
        P(("tp", "grp"), None),
        P(),
        P(("tp", "grp"), None, None),
    )
    out_specs = (P(None, "seq", ("tp", "grp"), None), P("seq", None, ("tp", "grp"), None))
    return jax.shard_map(
        on_device, mesh=mesh, in_specs=in_specs, out_specs=out_specs, check_vma=False
    )
```

```python
import functools

import jax
import jax.numpy as jnp
from jax import lax
from jax.experimental import pallas as pl
from jax.experimental.pallas import tpu as pltpu
from jax.sharding import PartitionSpec as P

epsilon = 1e-06
negative = -1e30
log2_e = 1.4426950408889634
NT = (((1,), (1,)), ((), ()))
NN = (((1,), (0,)), ((), ()))
VMEM_BYTES = 56 * 2**20


def rotate(rope_part, positions):
    half_width = rope_part.shape[-1] // 2
    frequency = jnp.exp(-jnp.log(10000.0) * jnp.arange(half_width).astype(jnp.float32) / half_width)
    angles = positions.astype(jnp.float32)[..., None] * frequency
    cosine = jnp.cos(angles)
    sine_part = jnp.sin(angles)
    former = rope_part[..., :half_width]
    latter = rope_part[..., half_width:]
    return jnp.concatenate(
        [former * cosine - latter * sine_part, latter * cosine + former * sine_part], axis=-1
    )


def make_rows(latent, kv_gain, positions):
    lat_width = kv_gain.shape[0]
    latent_part = latent[..., :lat_width]
    spread = jnp.mean(latent_part * latent_part, axis=-1, keepdims=True)
    normed = latent_part * lax.rsqrt(spread + epsilon) * kv_gain
    return jnp.concatenate([normed, rotate(latent[..., lat_width:], positions)], axis=-1).astype(
        jnp.bfloat16
    )


def dot(left, right, dims):
    return lax.dot_general(left, right, dims, preferred_element_type=jnp.float32)


def key_scores(queries, keys, lat, dims):
    if dims is NT:
        return dot(queries[:, :lat], keys[:, :lat], NT) + dot(queries[:, lat:], keys[:, lat:], NT)
    return dot(queries[:, :lat], keys[:lat], NN) + dot(queries[:, lat:], keys[lat:], NN)


def lane_fold(op, total, block):
    for start in range(0, block.shape[1], 128):
        part = block[:, start : start + 128]
        total = part if total is None else op(total, part)
    return total


def attend_tiles(config, count, load, store, hold, keys, masks):
    lat, factor = config
    for i in range(count):
        queries = load(i)
        row = lax.broadcasted_iota(jnp.int32, (queries.shape[0], 1), 0) + i * queries.shape[0]
        highest = None
        end = 0
        for block, mask in zip(keys, masks):
            values = block()
            scores = key_scores(queries, values, lat, NT)
            allowed = mask(row)
            if allowed is not None:
                scores = jnp.where(allowed, scores, negative)
            hold[i % 2, :, end : end + values.shape[0]] = scores
            end += values.shape[0]
            highest = lane_fold(jnp.maximum, highest, scores)
        peak = jnp.max(highest, axis=1, keepdims=True)
        total = None
        summed = None
        end = 0
        for block in keys:
            values = block()
            weights = jnp.exp2((hold[i % 2, :, end : end + values.shape[0]] - peak) * factor)
            end += values.shape[0]
            total = lane_fold(jnp.add, total, weights)
            part = dot(weights.astype(jnp.bfloat16), values[:, :lat], NN)
            summed = part if summed is None else summed + part
        total = jnp.sum(total, axis=1, keepdims=True)
        store(i, summed / total, peak * factor + jnp.log2(total))


def first_body(config, chunk, head_local, info, q_ref, dq_ref, near_ref, far_ref, fresh_ref, *rest):
    pieces = rest[:8]
    out_ref, decode_ref, lse_ref, hold, past, arrive = rest[8:]
    step = pl.program_id(0)
    prompts = pl.num_programs(0) - 1
    tile = hold.shape[1]
    _, holders, piece_rows, width = past.shape
    lines, half_tokens, _ = near_ref.shape
    held = chunk // piece_rows
    past_count = holders // held
    prompt = jnp.maximum(step - 1, 0)
    slot = prompt & 1
    past_len = info[prompt]
    z_place, x_place, core = info[5], info[6], info[7]

    def copies(p):
        made = []
        for c in range(2):
            side = core if c == 0 else 1 - core
            for s in range(4):
                for j in range(4):
                    dz = s + (j - s) * side
                    dx = j + (s - j) * side
                    holder = ((z_place + dz) & 3) * 4 + ((x_place + dx) & 3)
                    made.append(
                        pltpu.make_async_copy(
                            pieces[c * 4 + s].at[j, p],
                            past.at[p & 1, holder * 2 + side],
                            arrive.at[p & 1, c * 16 + s * 4 + j],
                        )
                    )
        return made

    @pl.when(step == 0)
    def _():
        for copy in copies(0):
            copy.start()

    @pl.when((step > 0) & (step < prompts))
    def _():
        for copy in copies(step):
            copy.start()

    @pl.when(step != 1)
    def _():
        for copy in copies(prompt):
            copy.wait()

    def past_keys(j):
        return lambda: past[slot, j * held : (j + 1) * held].reshape(chunk, width)

    def past_mask(j):
        def allowed(row):
            if 2 * (j + 1) <= past_count:
                return None
            return lax.broadcasted_iota(jnp.int32, (1, chunk), 1) + j * chunk < past_len

        return allowed

    def group_mask(side):
        def allowed(row):
            place = lax.broadcasted_iota(jnp.int32, (1, lines * half_tokens), 1)
            outer = place // (4 * half_tokens)
            inner = (place // half_tokens) & 3
            z_from = (z_place + outer + (inner - outer) * side) & 3
            x_from = (x_place + inner + (outer - inner) * side) & 3
            key_token = (z_from * 4 + x_from) * (2 * half_tokens) + side * half_tokens
            key_token = key_token + (place & (half_tokens - 1))
            return key_token <= info[4] + row // head_local

        return allowed

    def fresh_mask(row):
        place = lax.broadcasted_iota(jnp.int32, (1, fresh_ref.shape[0]), 1)
        return (place >= row // (2 * head_local) * 2) & (place <= row // head_local)

    keys = [past_keys(j) for j in range(past_count)]
    keys += [
        lambda: near_ref[...].reshape(lines * half_tokens, width),
        lambda: far_ref[...].reshape(lines * half_tokens, width),
    ]
    masks = [past_mask(j) for j in range(past_count)]

    @pl.when(step == 0)
    def _():
        def store(i, value, lse):
            decode_ref[i * tile : (i + 1) * tile, :] = value.astype(jnp.bfloat16)
            lse_ref[i * tile : (i + 1) * tile, :] = jnp.broadcast_to(lse, (tile, lse_ref.shape[1]))

        attend_tiles(
            config,
            dq_ref.shape[0] // tile,
            lambda i: dq_ref[i * tile : (i + 1) * tile, :],
            store,
            hold,
            keys + [lambda: fresh_ref[...]],
            masks + [lambda row: None, lambda row: None, fresh_mask],
        )

    @pl.when(step > 0)
    def _():
        def store(i, value, lse):
            out_ref[i * tile : (i + 1) * tile, :] = value.astype(jnp.bfloat16)

        attend_tiles(
            config,
            q_ref.shape[0] // tile,
            lambda i: q_ref[i * tile : (i + 1) * tile, :],
            store,
            hold,
            keys,
            masks + [group_mask(core), group_mask(1 - core)],
        )


def attend_first(info, query, decode_query, pieces, near, far, fresh, lat, factor, head_local):
    _, rows, width = query.shape
    prompts = pieces[0].shape[1]
    decode_rows = decode_query.shape[0]
    piece_rows = pieces[0].shape[2]
    holders = 4 * len(pieces)
    lines, _, half_tokens, _ = near.shape
    keys = holders * piece_rows + 2 * lines * half_tokens + fresh.shape[0]
    tile = 256
    chunk = 768

    def prompt(i):
        return jnp.maximum(i - 1, 0)

    group_spec = pl.BlockSpec(
        (lines, None, half_tokens, width), lambda i, _: (0, prompt(i), 0, 0)
    )
    return pl.pallas_call(
        functools.partial(first_body, (lat, factor), chunk, head_local),
        grid_spec=pltpu.PrefetchScalarGridSpec(
            num_scalar_prefetch=1,
            grid=(prompts + 1,),
            in_specs=[
                pl.BlockSpec((None, rows, width), lambda i, _: (prompt(i), 0, 0)),
                pl.BlockSpec((decode_rows, width), lambda i, _: (0, 0)),
                group_spec,
                group_spec,
                pl.BlockSpec(fresh.shape, lambda i, _: (0, 0)),
            ]
            + [pl.BlockSpec(memory_space=pl.ANY)] * len(pieces),
            out_specs=[
                pl.BlockSpec((None, rows, lat), lambda i, _: (prompt(i), 0, 0)),
                pl.BlockSpec((decode_rows, lat), lambda i, _: (0, 0)),
                pl.BlockSpec((decode_rows, 128), lambda i, _: (0, 0)),
            ],
            scratch_shapes=[
                pltpu.VMEM((2, tile, keys), jnp.float32),
                pltpu.VMEM((2, holders, piece_rows, width), jnp.bfloat16),
                pltpu.SemaphoreType.DMA((2, holders)),
            ],
        ),
        out_shape=[
            jax.ShapeDtypeStruct((prompts, rows, lat), jnp.bfloat16),
            jax.ShapeDtypeStruct((decode_rows, lat), jnp.bfloat16),
            jax.ShapeDtypeStruct((decode_rows, 128), jnp.float32),
        ],
        compiler_params=pltpu.CompilerParams(vmem_limit_bytes=VMEM_BYTES),
        cost_estimate=pl.CostEstimate(
            flops=2 * (prompts * rows + decode_rows) * keys * (768 + lat),
            bytes_accessed=2 * prompts * (keys + 2 * rows) * width,
            transcendentals=(prompts * rows + decode_rows) * keys,
        ),
        name="attend_first",
    )(info, query, decode_query, near, far, fresh, *pieces)


def later_body(config, chunk, head_local, first, info, q_ref, past_ref, near_ref, far_ref, out_ref, hold):
    step = pl.program_id(0)
    tile = hold.shape[1]
    seq_count, _, piece_rows, width = past_ref.shape
    lines, half_tokens, _ = near_ref.shape
    held = chunk // (2 * piece_rows)
    past_count = seq_count // held
    past_len = info[step + first]
    z_place, x_place, core = info[5], info[6], info[7]

    def past_keys(j):
        return lambda: past_ref[j * held : (j + 1) * held].reshape(chunk, width)

    def past_mask(j):
        def allowed(row):
            if 2 * (j + 1) <= past_count:
                return None
            return lax.broadcasted_iota(jnp.int32, (1, chunk), 1) + j * chunk < past_len

        return allowed

    def group_mask(side):
        def allowed(row):
            place = lax.broadcasted_iota(jnp.int32, (1, lines * half_tokens), 1)
            outer = place // (4 * half_tokens)
            inner = (place // half_tokens) & 3
            z_from = (z_place + outer + (inner - outer) * side) & 3
            x_from = (x_place + inner + (outer - inner) * side) & 3
            key_token = (z_from * 4 + x_from) * (2 * half_tokens) + side * half_tokens
            key_token = key_token + (place & (half_tokens - 1))
            return key_token <= info[4] + row // head_local

        return allowed

    keys = [past_keys(j) for j in range(past_count)]
    keys += [
        lambda: near_ref[...].reshape(lines * half_tokens, width),
        lambda: far_ref[...].reshape(lines * half_tokens, width),
    ]
    masks = [past_mask(j) for j in range(past_count)]

    def store(i, value, lse):
        out_ref[i * tile : (i + 1) * tile, :] = value.astype(jnp.bfloat16)

    def run(count):
        attend_tiles(
            config,
            q_ref.shape[0] // tile,
            lambda i: q_ref[i * tile : (i + 1) * tile, :],
            store,
            hold,
            keys[:count] + keys[past_count:],
            masks[:count] + [group_mask(core), group_mask(1 - core)],
        )

    short = past_len <= (past_count - 1) * chunk

    @pl.when(short)
    def _():
        run(past_count - 1)

    @pl.when(jnp.logical_not(short))
    def _():
        run(past_count)


def attend_later(info, query, past, near, far, first, lat, factor, head_local):
    prompts, rows, width = query.shape
    count = prompts - first
    seq_count, _, halves, piece_rows, _ = past.shape
    lines, _, half_tokens, _ = near.shape
    keys = seq_count * halves * piece_rows + 2 * lines * half_tokens
    tile = 256
    chunk = 768
    group_spec = pl.BlockSpec((lines, None, half_tokens, width), lambda i, _: (0, i + first, 0, 0))
    return pl.pallas_call(
        functools.partial(later_body, (lat, factor), chunk, head_local, first),
        grid_spec=pltpu.PrefetchScalarGridSpec(
            num_scalar_prefetch=1,
            grid=(count,),
            in_specs=[
                pl.BlockSpec((None, rows, width), lambda i, _: (i + first, 0, 0)),
                pl.BlockSpec(
                    (seq_count, None, halves, piece_rows, width),
                    lambda i, _: (0, i + first, 0, 0, 0),
                ),
                group_spec,
                group_spec,
            ],
            out_specs=pl.BlockSpec((None, rows, lat), lambda i, _: (i, 0, 0)),
            scratch_shapes=[pltpu.VMEM((2, tile, keys), jnp.float32)],
        ),
        out_shape=jax.ShapeDtypeStruct((count, rows, lat), jnp.bfloat16),
        compiler_params=pltpu.CompilerParams(vmem_limit_bytes=VMEM_BYTES),
        cost_estimate=pl.CostEstimate(
            flops=2 * count * rows * keys * (768 + lat),
            bytes_accessed=2 * count * (keys + 2 * rows) * width,
            transcendentals=count * rows * keys,
        ),
        name="attend_later",
    )(info, query, past, near, far)


def dispatch_body(source, length, q_ref, out_ref):
    slots, rows, width = out_ref.shape
    lat_rope = q_ref.shape[2]
    lane = lax.broadcasted_iota(jnp.int32, (rows, width - lat_rope), 1)
    for slot in range(slots):
        out_ref[slot, :, :lat_rope] = q_ref[source[slot]]
        size = length[slot]
        tail = jnp.where(lane < 32, size >> 4, size & 15)
        out_ref[slot, :, lat_rope:] = tail.astype(jnp.float32).astype(jnp.bfloat16)


def dispatch_queries(source, length, query, width):
    slots = source.shape[0]
    _, rows, _ = query.shape
    smem = pl.BlockSpec(memory_space=pltpu.SMEM)
    vmem = pl.BlockSpec(memory_space=pltpu.VMEM)
    return pl.pallas_call(
        dispatch_body,
        in_specs=[smem, smem, vmem],
        out_specs=vmem,
        out_shape=jax.ShapeDtypeStruct((slots, rows, width), jnp.bfloat16),
        compiler_params=pltpu.CompilerParams(vmem_limit_bytes=VMEM_BYTES),
        name="dispatch_queries",
    )(source, length, query)


def cache_body(lat, factor, batch, order, length, used, q_ref, *rest):
    pool_refs = rest[:batch]
    out_ref, lse_ref = rest[batch:]
    step = pl.program_id(0)
    rows = q_ref.shape[1]
    width, cache_rows = pool_refs[0].shape

    @pl.when(step * batch < used[0])
    def _():
        place = lax.broadcasted_iota(jnp.int32, (1, cache_rows), 1)
        lane = lax.broadcasted_iota(jnp.int32, (rows, lse_ref.shape[2]), 1)
        slots = [order[step * batch + b] for b in range(batch)]
        scores = [
            key_scores(q_ref[slots[b], :, :width], pool_refs[b][...], lat, NN)
            for b in range(batch)
        ]
        for b in range(batch):
            masked = jnp.where(place < length[slots[b]], scores[b], negative)
            peak = jnp.max(masked, axis=1, keepdims=True)
            weights = jnp.exp2((masked - peak) * factor)
            total = jnp.sum(weights, axis=1, keepdims=True)
            summed = dot(weights.astype(jnp.bfloat16), pool_refs[b][:lat], NT)
            out_ref[slots[b]] = (summed / total).astype(jnp.bfloat16)
            lse = peak * factor + jnp.log2(total)
            high = lse.astype(jnp.bfloat16).astype(jnp.float32)
            middle = (lse - high).astype(jnp.bfloat16).astype(jnp.float32)
            low = lse - high - middle
            lse_ref[slots[b]] = jnp.where(
                lane == 0, high, jnp.where(lane == 1, middle, low)
            ).astype(jnp.bfloat16)


def attend_cache(order, length, used, query, pool, lat, factor):
    batch = 4
    slots, rows, padded = query.shape
    _, width, cache_rows = pool.shape
    whole = pl.BlockSpec((slots, rows, padded), lambda i, *_: (0, 0, 0))

    def pool_spec(b):
        return pl.BlockSpec(
            (None, width, cache_rows), lambda i, order, *_: (order[i * batch + b], 0, 0)
        )

    return pl.pallas_call(
        functools.partial(cache_body, lat, factor, batch),
        grid_spec=pltpu.PrefetchScalarGridSpec(
            num_scalar_prefetch=3,
            grid=(slots // batch,),
            in_specs=[whole] + [pool_spec(b) for b in range(batch)],
            out_specs=[
                pl.BlockSpec((slots, rows, lat), lambda i, *_: (0, 0, 0)),
                pl.BlockSpec((slots, rows, 128), lambda i, *_: (0, 0, 0)),
            ],
        ),
        out_shape=[
            jax.ShapeDtypeStruct((slots, rows, lat), jnp.bfloat16),
            jax.ShapeDtypeStruct((slots, rows, 128), jnp.bfloat16),
        ],
        compiler_params=pltpu.CompilerParams(vmem_limit_bytes=VMEM_BYTES),
        cost_estimate=pl.CostEstimate(
            flops=2 * slots * 128 * cache_rows * (width + lat),
            bytes_accessed=2 * slots * cache_rows * width,
            transcendentals=slots * rows * cache_rows,
        ),
        name="attend_cache",
    )(order, length, used, query, *([pool] * batch))


def merge_body(slot, back_ref, near_ref, near_lse_ref, out_ref):
    count = near_ref.shape[0]
    width = near_ref.shape[2]
    for r in range(count):
        back = back_ref[slot[r]].astype(jnp.float32)
        far = back[:, :width]
        far_lse = back[:, width : width + 1] + back[:, width + 1 : width + 2]
        far_lse = far_lse + back[:, width + 2 : width + 3]
        near_lse = near_lse_ref[r][:, :1]
        peak = jnp.maximum(far_lse, near_lse)
        far_part = jnp.exp2(far_lse - peak)
        near_part = jnp.exp2(near_lse - peak)
        mixed = far * far_part + near_ref[r] * near_part
        out_ref[r] = (mixed / (far_part + near_part)).astype(jnp.bfloat16)


def merge_decode(slot, back, near, near_lse):
    smem = pl.BlockSpec(memory_space=pltpu.SMEM)
    vmem = pl.BlockSpec(memory_space=pltpu.VMEM)
    return pl.pallas_call(
        merge_body,
        in_specs=[smem, vmem, vmem, vmem],
        out_specs=vmem,
        out_shape=jax.ShapeDtypeStruct(near.shape, jnp.bfloat16),
        compiler_params=pltpu.CompilerParams(vmem_limit_bytes=VMEM_BYTES),
        name="merge_decode",
    )(slot, back, near, near_lse)


def swap_core(value):
    return lax.ppermute(value, "grp", [(0, 1), (1, 0)])


def fetch_tp(value, shift):
    return lax.ppermute(value, "tp", [((i + shift) % 4, i) for i in range(4)])


def fetch_ring(value, shift, turn):
    moves = []
    for i in range(16):
        z, x = i // 4, i % 4
        for c in range(2):
            if (c + turn) % 2 == 0:
                origin = z * 4 + (x + shift) % 4
            else:
                origin = (z + shift) % 4 * 4 + x
            moves.append((origin * 2 + c, i * 2 + c))
    return lax.ppermute(value, ("seq", "grp"), moves)


def on_device(
    group_hidden,
    group_query,
    past_cache,
    past_len,
    decode_hidden,
    decode_query,
    decode_pool,
    owner,
    dec_len,
    w_latent,
    kv_gain,
    w_value,
):
    seq_count = lax.axis_size("seq")
    seq_place = lax.axis_index("seq")
    tp_place = lax.axis_index("tp")
    core = lax.axis_index("grp")
    z_place, x_place = seq_place >> 2, seq_place & 3
    prompt_count, group_local, head_local, row_width = group_query.shape
    past_local = past_cache.shape[1]
    request_local = decode_query.shape[0]
    lat = kv_gain.shape[0]
    value_width = w_value.shape[2]
    slot_count = decode_pool.shape[0]
    pair_limit = slot_count // seq_count
    query_pairs = 2 * head_local
    factor = (value_width + row_width - lat) ** (-0.5) * log2_e

    half = past_local // 2
    past_part = lax.dynamic_slice(past_cache, (tp_place, core * half, 0), (1, half, row_width))
    past_all = lax.all_gather(
        past_part.reshape(half, row_width), ("seq", "tp", "grp"), axis=0, tiled=False
    ).reshape(seq_count, prompt_count, 2, half, row_width)

    past_half = lax.dynamic_slice(past_cache, (0, core * half, 0), (1, half, row_width))
    past_line = [past_half] + [fetch_ring(past_half, shift, 0) for shift in range(1, 4)]
    past_line = jnp.stack(past_line)
    past_lines = [past_line] + [fetch_ring(past_line, shift, 1) for shift in range(1, 4)]
    past_lines = past_lines + [swap_core(piece) for piece in past_lines]

    half_tokens = group_local // 2
    pairs = 2 * request_local
    partial_group = jnp.einsum(
        "ptd,dc->ptc", group_hidden, w_latent, preferred_element_type=jnp.float32
    ).astype(jnp.bfloat16)
    partial_group = partial_group.reshape(prompt_count, 2, half_tokens, row_width)
    partial_decode = jnp.einsum(
        "rd,dc->rc",
        decode_hidden.reshape(pairs, -1),
        w_latent,
        preferred_element_type=jnp.float32,
    ).astype(jnp.bfloat16)
    group_part = prompt_count * half_tokens

    def both(chosen):
        part = lax.dynamic_index_in_dim(partial_group, chosen, axis=1, keepdims=False)
        return jnp.concatenate([part.reshape(group_part, row_width), partial_decode])

    pair_sum = both(core).astype(jnp.float32) + swap_core(both(1 - core)).astype(jnp.float32)
    pair_sum = pair_sum.astype(jnp.bfloat16)

    pair_sum, _ = lax.optimization_barrier((pair_sum, past_line))
    latent = pair_sum.astype(jnp.float32)
    for shift in range(1, 4):
        latent = latent + fetch_tp(pair_sum, shift).astype(jnp.float32)
    half_order = jnp.arange(half_tokens, dtype=jnp.int32)
    group_positions = (
        past_len[:, None] + seq_place * group_local + core * half_tokens + half_order[None, :]
    )
    decode_positions = (
        past_len[0]
        + group_local * seq_count
        + (dec_len[:, None] + jnp.arange(2, dtype=jnp.int32)).reshape(-1)
    )
    positions = jnp.concatenate([group_positions.reshape(-1), decode_positions])
    rows_own = make_rows(latent, kv_gain, positions)
    fresh = jnp.pad(rows_own[group_part:], ((0, 128 - pairs), (0, 0)))

    group_own = rows_own[:group_part].reshape(prompt_count, half_tokens, row_width)
    group_line = [group_own] + [fetch_ring(group_own, shift, 0) for shift in range(1, 4)]
    group_line = jnp.stack(group_line)
    group_lines = [group_line] + [fetch_ring(group_line, shift, 1) for shift in range(1, 4)]
    group_near = jnp.concatenate(group_lines)
    group_far = swap_core(group_near)

    targets = owner[:, 0]
    request_order = jnp.arange(request_local, dtype=jnp.int32)
    earlier = (targets[:, None] == targets[None, :]) & (
        request_order[None, :] < request_order[:, None]
    )
    slot_rank = jnp.sum(earlier.astype(jnp.int32), axis=1)
    destination = targets * pair_limit + slot_rank
    matches = jnp.arange(slot_count, dtype=jnp.int32)[:, None] == destination[None, :]
    source = jnp.sum(jnp.where(matches, request_order[None, :], 0), axis=1)
    send_length = jnp.sum(jnp.where(matches, dec_len[None, :], 0), axis=1)
    send_query = dispatch_queries(
        source,
        send_length,
        decode_query.reshape(request_local, query_pairs, row_width),
        row_width + 64,
    )
    arrived = lax.all_to_all(
        send_query.reshape(seq_count, pair_limit * query_pairs, row_width + 64),
        "seq",
        split_axis=0,
        concat_axis=0,
        tiled=True,
    ).reshape(slot_count, query_pairs, row_width + 64)
    marks = arrived[:, 0, row_width:].astype(jnp.float32)
    slot_length = (marks[:, 0] * 16 + marks[:, 32]).astype(jnp.int32)

    is_used = slot_length > 0
    used_rank = jnp.cumsum(is_used.astype(jnp.int32)) - 1
    used = jnp.sum(is_used.astype(jnp.int32))
    slots = jnp.arange(slot_count, dtype=jnp.int32)
    wanted = jnp.minimum(slots, jnp.maximum(used - 1, 0))
    order = jnp.sum(
        jnp.where(is_used[None, :] & (used_rank[None, :] == wanted[:, None]), slots[None, :], 0),
        axis=1,
    )
    cache_latent, cache_lse = attend_cache(
        order, slot_length, used.reshape(1), arrived, jnp.swapaxes(decode_pool, 1, 2), lat, factor
    )
    cache_value = jnp.einsum(
        "nshc,hcv->nshv",
        cache_latent.reshape(slot_count, 2, head_local, lat),
        w_value,
        preferred_element_type=jnp.float32,
    ).astype(jnp.bfloat16)
    back = jnp.concatenate(
        [cache_value.reshape(slot_count, query_pairs, value_width), cache_lse], axis=-1
    )
    back = lax.all_to_all(
        back.reshape(seq_count, pair_limit * query_pairs, 2 * value_width),
        "seq",
        split_axis=0,
        concat_axis=0,
        tiled=True,
    ).reshape(slot_count, query_pairs, 2 * value_width)

    info = jnp.stack(
        [past_len[p] for p in range(prompt_count)]
        + [seq_place * group_local, z_place, x_place, core]
    ).astype(jnp.int32)
    queries = group_query.reshape(prompt_count, group_local * head_local, row_width)
    decode_rows, _ = lax.optimization_barrier((decode_query, cache_value))
    first_latent, near_latent, near_lse = attend_first(
        info,
        queries,
        decode_rows.reshape(request_local * query_pairs, row_width),
        past_lines,
        group_near,
        group_far,
        fresh,
        lat,
        factor,
        head_local,
    )
    near = jnp.einsum(
        "rshc,hcv->rshv",
        near_latent.reshape(request_local, 2, head_local, lat),
        w_value,
        preferred_element_type=jnp.float32,
    )
    decode_out = merge_decode(
        destination,
        back,
        near.reshape(request_local, query_pairs, value_width),
        near_lse.reshape(request_local, query_pairs, 128),
    ).reshape(request_local, 2, head_local, value_width)

    queries, _ = lax.optimization_barrier((queries, decode_out))
    later_latent = attend_later(
        info, queries, past_all, group_near, group_far, 1, lat, factor, head_local
    )
    prefill_out = jnp.concatenate(
        [
            jnp.einsum(
                "pthc,hcv->pthv",
                value.reshape(-1, group_local, head_local, lat),
                w_value,
                preferred_element_type=jnp.float32,
            ).astype(jnp.bfloat16)
            for value in (first_latent, later_latent)
        ]
    )
    return (prefill_out, decode_out)


def solution(mesh):
    in_specs = (
        P(None, "seq", ("tp", "grp")),
        P(None, "seq", ("tp", "grp"), None),
        P(None, "seq", None),
        P(),
        P("seq", None, ("tp", "grp")),
        P("seq", None, ("tp", "grp"), None),
        P("seq", None, None),
        P("seq", None),
        P("seq"),
        P(("tp", "grp"), None),
        P(),
        P(("tp", "grp"), None, None),
    )
    out_specs = (P(None, "seq", ("tp", "grp"), None), P("seq", None, ("tp", "grp"), None))
    return jax.shard_map(
        on_device, mesh=mesh, in_specs=in_specs, out_specs=out_specs, check_vma=False
    )
```

```python
import functools

import jax
import jax.numpy as jnp
from jax import lax
from jax.experimental import pallas as pl
from jax.experimental.pallas import tpu as pltpu
from jax.sharding import PartitionSpec as P

epsilon = 1e-06
negative = -1e30
log2_e = 1.4426950408889634
NT = (((1,), (1,)), ((), ()))
NN = (((1,), (0,)), ((), ()))
VMEM_BYTES = 56 * 2**20


def rotate(rope_part, positions):
    half_width = rope_part.shape[-1] // 2
    frequency = jnp.exp(-jnp.log(10000.0) * jnp.arange(half_width).astype(jnp.float32) / half_width)
    angles = positions.astype(jnp.float32)[..., None] * frequency
    cosine = jnp.cos(angles)
    sine_part = jnp.sin(angles)
    former = rope_part[..., :half_width]
    latter = rope_part[..., half_width:]
    return jnp.concatenate(
        [former * cosine - latter * sine_part, latter * cosine + former * sine_part], axis=-1
    )


def make_rows(latent, kv_gain, positions):
    lat_width = kv_gain.shape[0]
    latent_part = latent[..., :lat_width]
    spread = jnp.mean(latent_part * latent_part, axis=-1, keepdims=True)
    normed = latent_part * lax.rsqrt(spread + epsilon) * kv_gain
    return jnp.concatenate([normed, rotate(latent[..., lat_width:], positions)], axis=-1).astype(
        jnp.bfloat16
    )


def dot(left, right, dims):
    return lax.dot_general(left, right, dims, preferred_element_type=jnp.float32)


def key_scores(queries, keys, lat, dims):
    if dims is NT:
        return dot(queries[:, :lat], keys[:, :lat], NT) + dot(queries[:, lat:], keys[:, lat:], NT)
    return dot(queries[:, :lat], keys[:lat], NN) + dot(queries[:, lat:], keys[lat:], NN)


def lane_fold(op, total, block):
    for start in range(0, block.shape[1], 128):
        part = block[:, start : start + 128]
        total = part if total is None else op(total, part)
    return total


def attend_tiles(config, count, load, store, hold, keys, masks):
    lat, factor = config
    for i in range(count):
        queries = load(i)
        row = lax.broadcasted_iota(jnp.int32, (queries.shape[0], 1), 0) + i * queries.shape[0]
        highest = None
        end = 0
        for block, mask in zip(keys, masks):
            values = block()
            scores = key_scores(queries, values, lat, NT)
            allowed = mask(row)
            if allowed is not None:
                scores = jnp.where(allowed, scores, negative)
            hold[i % 2, :, end : end + values.shape[0]] = scores
            end += values.shape[0]
            highest = lane_fold(jnp.maximum, highest, scores)
        peak = jnp.max(highest, axis=1, keepdims=True)
        total = None
        summed = None
        end = 0
        for block in keys:
            values = block()
            weights = jnp.exp2((hold[i % 2, :, end : end + values.shape[0]] - peak) * factor)
            end += values.shape[0]
            total = lane_fold(jnp.add, total, weights)
            part = dot(weights.astype(jnp.bfloat16), values[:, :lat], NN)
            summed = part if summed is None else summed + part
        total = jnp.sum(total, axis=1, keepdims=True)
        store(i, summed / total, peak * factor + jnp.log2(total))


def gather_group(piece_refs, group):
    for c in range(2):
        for s in range(4):
            group[c, s] = piece_refs[c * 4 + s][...].reshape(group.shape[2:])


def first_body(config, chunk, head_local, info, q_ref, dq_ref, fresh_ref, *rest):
    pieces = rest[:8]
    group_refs = rest[8:16]
    out_ref, decode_ref, lse_ref, hold, past, group, arrive = rest[16:]
    step = pl.program_id(0)
    tile = hold.shape[1]
    holders, piece_blocks, half_tokens, width = past.shape
    lines = 16
    held = chunk // (piece_blocks * half_tokens)
    past_count = holders // held
    past_len = info[0]
    z_place, x_place, core = info[5], info[6], info[7]

    @pl.when(step == 0)
    def _():
        copies = []
        for c in range(2):
            side = core if c == 0 else 1 - core
            for s in range(4):
                for j in range(4):
                    dz = s + (j - s) * side
                    dx = j + (s - j) * side
                    holder = ((z_place + dz) & 3) * 4 + ((x_place + dx) & 3)
                    copies.append(
                        pltpu.make_async_copy(
                            pieces[c * 4 + s].at[j, pl.ds(0, piece_blocks)],
                            past.at[holder * 2 + side],
                            arrive.at[c * 16 + s * 4 + j],
                        )
                    )
        for copy in copies:
            copy.start()
        gather_group(group_refs, group)
        for copy in copies:
            copy.wait()

    def past_keys(j):
        return lambda: past[j * held : (j + 1) * held].reshape(chunk, width)

    def past_mask(j):
        def allowed(row):
            if 2 * (j + 1) <= past_count:
                return None
            return lax.broadcasted_iota(jnp.int32, (1, chunk), 1) + j * chunk < past_len

        return allowed

    def group_mask(side):
        def allowed(row):
            place = lax.broadcasted_iota(jnp.int32, (1, lines * half_tokens), 1)
            outer = place // (4 * half_tokens)
            inner = (place // half_tokens) & 3
            z_from = (z_place + outer + (inner - outer) * side) & 3
            x_from = (x_place + inner + (outer - inner) * side) & 3
            key_token = (z_from * 4 + x_from) * (2 * half_tokens) + side * half_tokens
            key_token = key_token + (place & (half_tokens - 1))
            return key_token <= info[4] + row // head_local

        return allowed

    def fresh_mask(row):
        place = lax.broadcasted_iota(jnp.int32, (1, fresh_ref.shape[0]), 1)
        return (place >= row // (2 * head_local) * 2) & (place <= row // head_local)

    keys = [past_keys(j) for j in range(past_count)]
    keys += [
        lambda: group[0].reshape(lines * half_tokens, width),
        lambda: group[1].reshape(lines * half_tokens, width),
    ]
    masks = [past_mask(j) for j in range(past_count)]

    @pl.when(step == 0)
    def _():
        def store(i, value, lse):
            decode_ref[i * tile : (i + 1) * tile, :] = value.astype(jnp.bfloat16)
            lse_ref[i * tile : (i + 1) * tile, :] = jnp.broadcast_to(lse, (tile, lse_ref.shape[1]))

        attend_tiles(
            config,
            dq_ref.shape[0] // tile,
            lambda i: dq_ref[i * tile : (i + 1) * tile, :],
            store,
            hold,
            keys + [lambda: fresh_ref[...]],
            masks + [lambda row: None, lambda row: None, fresh_mask],
        )

    @pl.when(step > 0)
    def _():
        def store(i, value, lse):
            out_ref[i * tile : (i + 1) * tile, :] = value.astype(jnp.bfloat16)

        attend_tiles(
            config,
            q_ref.shape[0] // tile,
            lambda i: q_ref[i * tile : (i + 1) * tile, :],
            store,
            hold,
            keys,
            masks + [group_mask(core), group_mask(1 - core)],
        )


def group_specs(pieces, block):
    count, _, half_tokens, width = pieces[0].shape
    return [pl.BlockSpec((count, None, half_tokens, width), block) for _ in pieces]


def attend_first(info, query, decode_query, pieces, piece_blocks, fresh, lat, factor, head_local):
    _, rows, width = query.shape
    decode_rows = decode_query.shape[0]
    half_tokens = pieces[0].shape[2]
    holders = 4 * len(pieces)
    keys = holders * (piece_blocks + 1) * half_tokens + fresh.shape[0]
    tile = 256
    chunk = 768
    return pl.pallas_call(
        functools.partial(first_body, (lat, factor), chunk, head_local),
        grid_spec=pltpu.PrefetchScalarGridSpec(
            num_scalar_prefetch=1,
            grid=(2,),
            in_specs=[
                pl.BlockSpec((None, rows, width), lambda i, _: (0, 0, 0)),
                pl.BlockSpec((decode_rows, width), lambda i, _: (0, 0)),
                pl.BlockSpec(fresh.shape, lambda i, _: (0, 0)),
            ]
            + [pl.BlockSpec(memory_space=pl.ANY)] * len(pieces)
            + group_specs(pieces, lambda i, _: (0, piece_blocks, 0, 0)),
            out_specs=[
                pl.BlockSpec((None, rows, lat), lambda i, _: (0, 0, 0)),
                pl.BlockSpec((decode_rows, lat), lambda i, _: (0, 0)),
                pl.BlockSpec((decode_rows, 128), lambda i, _: (0, 0)),
            ],
            scratch_shapes=[
                pltpu.VMEM((2, tile, keys), jnp.float32),
                pltpu.VMEM((holders, piece_blocks, half_tokens, width), jnp.bfloat16),
                pltpu.VMEM((2, 4, 4 * half_tokens, width), jnp.bfloat16),
                pltpu.SemaphoreType.DMA((holders,)),
            ],
        ),
        out_shape=[
            jax.ShapeDtypeStruct((1, rows, lat), jnp.bfloat16),
            jax.ShapeDtypeStruct((decode_rows, lat), jnp.bfloat16),
            jax.ShapeDtypeStruct((decode_rows, 128), jnp.float32),
        ],
        compiler_params=pltpu.CompilerParams(vmem_limit_bytes=VMEM_BYTES),
        cost_estimate=pl.CostEstimate(
            flops=2 * (rows + decode_rows) * keys * (768 + lat),
            bytes_accessed=2 * (keys + 2 * rows + 2 * decode_rows) * width,
            transcendentals=(rows + decode_rows) * keys,
        ),
        name="attend_first",
    )(info, query, decode_query, fresh, *pieces, *pieces)


def later_body(config, chunk, head_local, first, info, q_ref, past_ref, *rest):
    group_refs = rest[:8]
    out_ref, hold, group = rest[8:]
    step = pl.program_id(0)
    tile = hold.shape[1]
    seq_count, _, piece_rows, width = past_ref.shape
    lines = 16
    half_tokens = group_refs[0].shape[1]
    gather_group(group_refs, group)
    held = chunk // (2 * piece_rows)
    past_count = seq_count // held
    past_len = info[step + first]
    z_place, x_place, core = info[5], info[6], info[7]

    def past_keys(j):
        return lambda: past_ref[j * held : (j + 1) * held].reshape(chunk, width)

    def past_mask(j):
        def allowed(row):
            if 2 * (j + 1) <= past_count:
                return None
            return lax.broadcasted_iota(jnp.int32, (1, chunk), 1) + j * chunk < past_len

        return allowed

    def group_mask(side):
        def allowed(row):
            place = lax.broadcasted_iota(jnp.int32, (1, lines * half_tokens), 1)
            outer = place // (4 * half_tokens)
            inner = (place // half_tokens) & 3
            z_from = (z_place + outer + (inner - outer) * side) & 3
            x_from = (x_place + inner + (outer - inner) * side) & 3
            key_token = (z_from * 4 + x_from) * (2 * half_tokens) + side * half_tokens
            key_token = key_token + (place & (half_tokens - 1))
            return key_token <= info[4] + row // head_local

        return allowed

    keys = [past_keys(j) for j in range(past_count)]
    keys += [
        lambda: group[0].reshape(lines * half_tokens, width),
        lambda: group[1].reshape(lines * half_tokens, width),
    ]
    masks = [past_mask(j) for j in range(past_count)]

    def store(i, value, lse):
        out_ref[i * tile : (i + 1) * tile, :] = value.astype(jnp.bfloat16)

    def run(count):
        attend_tiles(
            config,
            q_ref.shape[0] // tile,
            lambda i: q_ref[i * tile : (i + 1) * tile, :],
            store,
            hold,
            keys[:count] + keys[past_count:],
            masks[:count] + [group_mask(core), group_mask(1 - core)],
        )

    short = past_len <= (past_count - 1) * chunk

    @pl.when(short)
    def _():
        run(past_count - 1)

    @pl.when(jnp.logical_not(short))
    def _():
        run(past_count)


def attend_later(info, query, past, pieces, piece_blocks, first, lat, factor, head_local):
    prompts, rows, width = query.shape
    count = prompts - first
    seq_count, _, halves, piece_rows, _ = past.shape
    half_tokens = pieces[0].shape[2]
    keys = seq_count * halves * (piece_rows + half_tokens)
    tile = 256
    chunk = 768
    return pl.pallas_call(
        functools.partial(later_body, (lat, factor), chunk, head_local, first),
        grid_spec=pltpu.PrefetchScalarGridSpec(
            num_scalar_prefetch=1,
            grid=(count,),
            in_specs=[
                pl.BlockSpec((None, rows, width), lambda i, _: (i + first, 0, 0)),
                pl.BlockSpec(
                    (seq_count, None, halves, piece_rows, width),
                    lambda i, _: (0, i + first, 0, 0, 0),
                ),
            ]
            + group_specs(pieces, lambda i, _: (0, piece_blocks + i + first, 0, 0)),
            out_specs=pl.BlockSpec((None, rows, lat), lambda i, _: (i, 0, 0)),
            scratch_shapes=[
                pltpu.VMEM((2, tile, keys), jnp.float32),
                pltpu.VMEM((2, 4, 4 * half_tokens, width), jnp.bfloat16),
            ],
        ),
        out_shape=jax.ShapeDtypeStruct((count, rows, lat), jnp.bfloat16),
        compiler_params=pltpu.CompilerParams(vmem_limit_bytes=VMEM_BYTES),
        cost_estimate=pl.CostEstimate(
            flops=2 * count * rows * keys * (768 + lat),
            bytes_accessed=2 * count * (keys + 2 * rows) * width,
            transcendentals=count * rows * keys,
        ),
        name="attend_later",
    )(info, query, past, *pieces)


def dispatch_body(source, length, q_ref, out_ref):
    slots, rows, width = out_ref.shape
    lat_rope = q_ref.shape[2]
    lane = lax.broadcasted_iota(jnp.int32, (rows, width - lat_rope), 1)
    for slot in range(slots):
        out_ref[slot, :, :lat_rope] = q_ref[source[slot]]
        size = length[slot]
        tail = jnp.where(lane < 32, size >> 4, size & 15)
        out_ref[slot, :, lat_rope:] = tail.astype(jnp.float32).astype(jnp.bfloat16)


def dispatch_queries(source, length, query, width):
    slots = source.shape[0]
    _, rows, _ = query.shape
    smem = pl.BlockSpec(memory_space=pltpu.SMEM)
    vmem = pl.BlockSpec(memory_space=pltpu.VMEM)
    return pl.pallas_call(
        dispatch_body,
        in_specs=[smem, smem, vmem],
        out_specs=vmem,
        out_shape=jax.ShapeDtypeStruct((slots, rows, width), jnp.bfloat16),
        compiler_params=pltpu.CompilerParams(vmem_limit_bytes=VMEM_BYTES),
        name="dispatch_queries",
    )(source, length, query)


def cache_body(lat, factor, batch, order, length, used, q_ref, *rest):
    pool_refs = rest[:batch]
    out_ref, lse_ref = rest[batch:]
    step = pl.program_id(0)
    rows = q_ref.shape[1]
    width, cache_rows = pool_refs[0].shape

    @pl.when(step * batch < used[0])
    def _():
        place = lax.broadcasted_iota(jnp.int32, (1, cache_rows), 1)
        lane = lax.broadcasted_iota(jnp.int32, (rows, lse_ref.shape[2]), 1)
        slots = [order[step * batch + b] for b in range(batch)]
        scores = [
            key_scores(q_ref[slots[b], :, :width], pool_refs[b][...], lat, NN)
            for b in range(batch)
        ]
        for b in range(batch):
            masked = jnp.where(place < length[slots[b]], scores[b], negative)
            peak = jnp.max(masked, axis=1, keepdims=True)
            weights = jnp.exp2((masked - peak) * factor)
            total = jnp.sum(weights, axis=1, keepdims=True)
            summed = dot(weights.astype(jnp.bfloat16), pool_refs[b][:lat], NT)
            out_ref[slots[b]] = (summed / total).astype(jnp.bfloat16)
            lse = peak * factor + jnp.log2(total)
            high = lse.astype(jnp.bfloat16).astype(jnp.float32)
            middle = (lse - high).astype(jnp.bfloat16).astype(jnp.float32)
            low = lse - high - middle
            lse_ref[slots[b]] = jnp.where(
                lane == 0, high, jnp.where(lane == 1, middle, low)
            ).astype(jnp.bfloat16)


def attend_cache(order, length, used, query, pool, lat, factor):
    batch = 4
    slots, rows, padded = query.shape
    _, width, cache_rows = pool.shape
    whole = pl.BlockSpec((slots, rows, padded), lambda i, *_: (0, 0, 0))

    def pool_spec(b):
        return pl.BlockSpec(
            (None, width, cache_rows), lambda i, order, *_: (order[i * batch + b], 0, 0)
        )

    return pl.pallas_call(
        functools.partial(cache_body, lat, factor, batch),
        grid_spec=pltpu.PrefetchScalarGridSpec(
            num_scalar_prefetch=3,
            grid=(slots // batch,),
            in_specs=[whole] + [pool_spec(b) for b in range(batch)],
            out_specs=[
                pl.BlockSpec((slots, rows, lat), lambda i, *_: (0, 0, 0)),
                pl.BlockSpec((slots, rows, 128), lambda i, *_: (0, 0, 0)),
            ],
        ),
        out_shape=[
            jax.ShapeDtypeStruct((slots, rows, lat), jnp.bfloat16),
            jax.ShapeDtypeStruct((slots, rows, 128), jnp.bfloat16),
        ],
        compiler_params=pltpu.CompilerParams(vmem_limit_bytes=VMEM_BYTES),
        cost_estimate=pl.CostEstimate(
            flops=2 * slots * 128 * cache_rows * (width + lat),
            bytes_accessed=2 * slots * cache_rows * width,
            transcendentals=slots * rows * cache_rows,
        ),
        name="attend_cache",
    )(order, length, used, query, *([pool] * batch))


def merge_body(slot, back_ref, near_ref, near_lse_ref, out_ref):
    count = near_ref.shape[0]
    width = near_ref.shape[2]
    for r in range(count):
        back = back_ref[slot[r]].astype(jnp.float32)
        far = back[:, :width]
        far_lse = back[:, width : width + 1] + back[:, width + 1 : width + 2]
        far_lse = far_lse + back[:, width + 2 : width + 3]
        near_lse = near_lse_ref[r][:, :1]
        peak = jnp.maximum(far_lse, near_lse)
        far_part = jnp.exp2(far_lse - peak)
        near_part = jnp.exp2(near_lse - peak)
        mixed = far * far_part + near_ref[r] * near_part
        out_ref[r] = (mixed / (far_part + near_part)).astype(jnp.bfloat16)


def merge_decode(slot, back, near, near_lse):
    smem = pl.BlockSpec(memory_space=pltpu.SMEM)
    vmem = pl.BlockSpec(memory_space=pltpu.VMEM)
    return pl.pallas_call(
        merge_body,
        in_specs=[smem, vmem, vmem, vmem],
        out_specs=vmem,
        out_shape=jax.ShapeDtypeStruct(near.shape, jnp.bfloat16),
        compiler_params=pltpu.CompilerParams(vmem_limit_bytes=VMEM_BYTES),
        name="merge_decode",
    )(slot, back, near, near_lse)


def swap_core(value):
    return lax.ppermute(value, "grp", [(0, 1), (1, 0)])


def fetch_tp(value, shift):
    return lax.ppermute(value, "tp", [((i + shift) % 4, i) for i in range(4)])


def fetch_ring(value, shift, turn):
    moves = []
    for i in range(16):
        z, x = i // 4, i % 4
        for c in range(2):
            if (c + turn) % 2 == 0:
                origin = z * 4 + (x + shift) % 4
            else:
                origin = (z + shift) % 4 * 4 + x
            moves.append((origin * 2 + c, i * 2 + c))
    return lax.ppermute(value, ("seq", "grp"), moves)


def on_device(
    group_hidden,
    group_query,
    past_cache,
    past_len,
    decode_hidden,
    decode_query,
    decode_pool,
    owner,
    dec_len,
    w_latent,
    kv_gain,
    w_value,
):
    seq_count = lax.axis_size("seq")
    seq_place = lax.axis_index("seq")
    tp_place = lax.axis_index("tp")
    core = lax.axis_index("grp")
    z_place, x_place = seq_place >> 2, seq_place & 3
    prompt_count, group_local, head_local, row_width = group_query.shape
    past_local = past_cache.shape[1]
    request_local = decode_query.shape[0]
    lat = kv_gain.shape[0]
    value_width = w_value.shape[2]
    slot_count = decode_pool.shape[0]
    pair_limit = slot_count // seq_count
    query_pairs = 2 * head_local
    factor = (value_width + row_width - lat) ** (-0.5) * log2_e

    half = past_local // 2
    past_part = lax.dynamic_slice(past_cache, (tp_place, core * half, 0), (1, half, row_width))
    past_all = lax.all_gather(
        past_part.reshape(half, row_width), ("seq", "tp", "grp"), axis=0, tiled=False
    ).reshape(seq_count, prompt_count, 2, half, row_width)

    half_tokens = group_local // 2
    pairs = 2 * request_local
    partial_group = jnp.einsum(
        "ptd,dc->ptc", group_hidden, w_latent, preferred_element_type=jnp.float32
    ).astype(jnp.bfloat16)
    partial_group = partial_group.reshape(prompt_count, 2, half_tokens, row_width)
    partial_decode = jnp.einsum(
        "rd,dc->rc",
        decode_hidden.reshape(pairs, -1),
        w_latent,
        preferred_element_type=jnp.float32,
    ).astype(jnp.bfloat16)
    group_part = prompt_count * half_tokens

    def both(chosen):
        part = lax.dynamic_index_in_dim(partial_group, chosen, axis=1, keepdims=False)
        return jnp.concatenate([part.reshape(group_part, row_width), partial_decode])

    pair_sum = both(core).astype(jnp.float32) + swap_core(both(1 - core)).astype(jnp.float32)
    pair_sum = pair_sum.astype(jnp.bfloat16)

    latent = pair_sum.astype(jnp.float32)
    for shift in range(1, 4):
        latent = latent + fetch_tp(pair_sum, shift).astype(jnp.float32)
    half_order = jnp.arange(half_tokens, dtype=jnp.int32)
    group_positions = (
        past_len[:, None] + seq_place * group_local + core * half_tokens + half_order[None, :]
    )
    decode_positions = (
        past_len[0]
        + group_local * seq_count
        + (dec_len[:, None] + jnp.arange(2, dtype=jnp.int32)).reshape(-1)
    )
    positions = jnp.concatenate([group_positions.reshape(-1), decode_positions])
    rows_own = make_rows(latent, kv_gain, positions)
    fresh = jnp.pad(rows_own[group_part:], ((0, 128 - pairs), (0, 0)))

    past_zero = lax.dynamic_slice(past_cache, (0, core * half, 0), (1, half, row_width))
    piece_blocks = half // half_tokens
    line = jnp.concatenate([past_zero.reshape(half, row_width), rows_own[:group_part]])
    line = line.reshape(-1, half_tokens, row_width)
    line = jnp.stack([line] + [fetch_ring(line, shift, 0) for shift in range(1, 4)])
    lines = [line] + [fetch_ring(line, shift, 1) for shift in range(1, 4)]

    targets = owner[:, 0]
    request_order = jnp.arange(request_local, dtype=jnp.int32)
    earlier = (targets[:, None] == targets[None, :]) & (
        request_order[None, :] < request_order[:, None]
    )
    slot_rank = jnp.sum(earlier.astype(jnp.int32), axis=1)
    destination = targets * pair_limit + slot_rank
    matches = jnp.arange(slot_count, dtype=jnp.int32)[:, None] == destination[None, :]
    source = jnp.sum(jnp.where(matches, request_order[None, :], 0), axis=1)
    send_length = jnp.sum(jnp.where(matches, dec_len[None, :], 0), axis=1)
    send_query = dispatch_queries(
        source,
        send_length,
        decode_query.reshape(request_local, query_pairs, row_width),
        row_width + 64,
    )
    arrived = lax.all_to_all(
        send_query.reshape(seq_count, pair_limit * query_pairs, row_width + 64),
        "seq",
        split_axis=0,
        concat_axis=0,
        tiled=True,
    ).reshape(slot_count, query_pairs, row_width + 64)
    marks = arrived[:, 0, row_width:].astype(jnp.float32)
    slot_length = (marks[:, 0] * 16 + marks[:, 32]).astype(jnp.int32)

    is_used = slot_length > 0
    used_rank = jnp.cumsum(is_used.astype(jnp.int32)) - 1
    used = jnp.sum(is_used.astype(jnp.int32))
    slots = jnp.arange(slot_count, dtype=jnp.int32)
    wanted = jnp.minimum(slots, jnp.maximum(used - 1, 0))
    order = jnp.sum(
        jnp.where(is_used[None, :] & (used_rank[None, :] == wanted[:, None]), slots[None, :], 0),
        axis=1,
    )
    cache_latent, cache_lse = attend_cache(
        order, slot_length, used.reshape(1), arrived, jnp.swapaxes(decode_pool, 1, 2), lat, factor
    )
    lines[1:], cache_latent = lax.optimization_barrier((lines[1:], cache_latent))
    pieces = lines + [swap_core(piece) for piece in lines]
    cache_value = jnp.einsum(
        "nshc,hcv->nshv",
        cache_latent.reshape(slot_count, 2, head_local, lat),
        w_value,
        preferred_element_type=jnp.float32,
    ).astype(jnp.bfloat16)
    back = jnp.concatenate(
        [cache_value.reshape(slot_count, query_pairs, value_width), cache_lse], axis=-1
    )
    back = lax.all_to_all(
        back.reshape(seq_count, pair_limit * query_pairs, 2 * value_width),
        "seq",
        split_axis=0,
        concat_axis=0,
        tiled=True,
    ).reshape(slot_count, query_pairs, 2 * value_width)

    info = jnp.stack(
        [past_len[p] for p in range(prompt_count)]
        + [seq_place * group_local, z_place, x_place, core]
    ).astype(jnp.int32)
    queries = group_query.reshape(prompt_count, group_local * head_local, row_width)
    decode_rows, _ = lax.optimization_barrier((decode_query, cache_value))
    first_latent, near_latent, near_lse = attend_first(
        info,
        queries,
        decode_rows.reshape(request_local * query_pairs, row_width),
        pieces,
        piece_blocks,
        fresh,
        lat,
        factor,
        head_local,
    )
    near = jnp.einsum(
        "rshc,hcv->rshv",
        near_latent.reshape(request_local, 2, head_local, lat),
        w_value,
        preferred_element_type=jnp.float32,
    )
    decode_out = merge_decode(
        destination,
        back,
        near.reshape(request_local, query_pairs, value_width),
        near_lse.reshape(request_local, query_pairs, 128),
    ).reshape(request_local, 2, head_local, value_width)

    queries, _ = lax.optimization_barrier((queries, decode_out))
    later_latent = attend_later(
        info, queries, past_all, pieces, piece_blocks, 1, lat, factor, head_local
    )
    prefill_out = jnp.concatenate(
        [
            jnp.einsum(
                "pthc,hcv->pthv",
                value.reshape(-1, group_local, head_local, lat),
                w_value,
                preferred_element_type=jnp.float32,
            ).astype(jnp.bfloat16)
            for value in (first_latent, later_latent)
        ]
    )
    return (prefill_out, decode_out)


def solution(mesh):
    in_specs = (
        P(None, "seq", ("tp", "grp")),
        P(None, "seq", ("tp", "grp"), None),
        P(None, "seq", None),
        P(),
        P("seq", None, ("tp", "grp")),
        P("seq", None, ("tp", "grp"), None),
        P("seq", None, None),
        P("seq", None),
        P("seq"),
        P(("tp", "grp"), None),
        P(),
        P(("tp", "grp"), None, None),
    )
    out_specs = (P(None, "seq", ("tp", "grp"), None), P("seq", None, ("tp", "grp"), None))
    return jax.shard_map(
        on_device, mesh=mesh, in_specs=in_specs, out_specs=out_specs, check_vma=False
    )
```

```python
import functools

import jax
import jax.numpy as jnp
from jax import lax
from jax.experimental import pallas as pl
from jax.experimental.pallas import tpu as pltpu
from jax.sharding import PartitionSpec as P

epsilon = 1e-06
negative = -1e30
log2_e = 1.4426950408889634
NT = (((1,), (1,)), ((), ()))
NN = (((1,), (0,)), ((), ()))
VMEM_BYTES = 56 * 2**20


def rotate(rope_part, positions):
    half_width = rope_part.shape[-1] // 2
    frequency = jnp.exp(-jnp.log(10000.0) * jnp.arange(half_width).astype(jnp.float32) / half_width)
    angles = positions.astype(jnp.float32)[..., None] * frequency
    cosine = jnp.cos(angles)
    sine_part = jnp.sin(angles)
    former = rope_part[..., :half_width]
    latter = rope_part[..., half_width:]
    return jnp.concatenate(
        [former * cosine - latter * sine_part, latter * cosine + former * sine_part], axis=-1
    )


def make_rows(latent, kv_gain, positions):
    lat_width = kv_gain.shape[0]
    latent_part = latent[..., :lat_width]
    spread = jnp.mean(latent_part * latent_part, axis=-1, keepdims=True)
    normed = latent_part * lax.rsqrt(spread + epsilon) * kv_gain
    return jnp.concatenate([normed, rotate(latent[..., lat_width:], positions)], axis=-1).astype(
        jnp.bfloat16
    )


def dot(left, right, dims):
    return lax.dot_general(left, right, dims, preferred_element_type=jnp.float32)


def key_scores(queries, keys, lat, dims):
    if dims is NT:
        return dot(queries[:, :lat], keys[:, :lat], NT) + dot(queries[:, lat:], keys[:, lat:], NT)
    return dot(queries[:, :lat], keys[:lat], NN) + dot(queries[:, lat:], keys[lat:], NN)


def lane_fold(op, total, block):
    for start in range(0, block.shape[1], 128):
        part = block[:, start : start + 128]
        total = part if total is None else op(total, part)
    return total


def attend_tiles(config, count, load, store, hold, keys, masks, ready=None):
    lat, factor = config
    for i in range(count):
        queries = load(i)
        row = lax.broadcasted_iota(jnp.int32, (queries.shape[0], 1), 0) + i * queries.shape[0]
        highest = None
        end = 0
        for number, (block, mask) in enumerate(zip(keys, masks)):
            if ready is not None and i == 0 and number == ready[0]:
                ready[1]()
            values = block()
            scores = key_scores(queries, values, lat, NT)
            allowed = mask(row)
            if allowed is not None:
                scores = jnp.where(allowed, scores, negative)
            hold[i % 2, :, end : end + values.shape[0]] = scores
            end += values.shape[0]
            highest = lane_fold(jnp.maximum, highest, scores)
        peak = jnp.max(highest, axis=1, keepdims=True)
        total = None
        summed = None
        end = 0
        for block in keys:
            values = block()
            weights = jnp.exp2((hold[i % 2, :, end : end + values.shape[0]] - peak) * factor)
            end += values.shape[0]
            total = lane_fold(jnp.add, total, weights)
            part = dot(weights.astype(jnp.bfloat16), values[:, :lat], NN)
            summed = part if summed is None else summed + part
        total = jnp.sum(total, axis=1, keepdims=True)
        store(i, summed / total, peak * factor + jnp.log2(total))


def gather_group(piece_refs, group):
    for c in range(2):
        for s in range(4):
            group[c, s] = piece_refs[c * 4 + s][...].reshape(group.shape[2:])


def first_body(config, chunk, head_local, info, q_ref, dq_ref, fresh_ref, *rest):
    pieces = rest[:8]
    group_refs = rest[8:16]
    out_ref, decode_ref, lse_ref, hold, past, group, arrive = rest[16:]
    step = pl.program_id(0)
    tile = hold.shape[1]
    holders, piece_blocks, half_tokens, width = past.shape
    lines = 16
    held = chunk // (piece_blocks * half_tokens)
    past_count = holders // held
    past_len = info[0]
    z_place, x_place, core = info[5], info[6], info[7]

    copies = []
    for c in range(2):
        side = core if c == 0 else 1 - core
        for s in range(4):
            for j in range(4):
                dz = s + (j - s) * side
                dx = j + (s - j) * side
                holder = ((z_place + dz) & 3) * 4 + ((x_place + dx) & 3)
                copies.append(
                    pltpu.make_async_copy(
                        pieces[c * 4 + s].at[j, pl.ds(0, piece_blocks)],
                        past.at[holder * 2 + side],
                        arrive.at[c * 16 + s * 4 + j],
                    )
                )

    @pl.when(step == 0)
    def _():
        for copy in copies:
            copy.start()
        gather_group(group_refs, group)

    def placed():
        for copy in copies:
            copy.wait()

    def past_keys(j):
        return lambda: past[j * held : (j + 1) * held].reshape(chunk, width)

    def past_mask(j):
        def allowed(row):
            if 2 * (j + 1) <= past_count:
                return None
            return lax.broadcasted_iota(jnp.int32, (1, chunk), 1) + j * chunk < past_len

        return allowed

    def group_mask(side):
        def allowed(row):
            place = lax.broadcasted_iota(jnp.int32, (1, lines * half_tokens), 1)
            outer = place // (4 * half_tokens)
            inner = (place // half_tokens) & 3
            z_from = (z_place + outer + (inner - outer) * side) & 3
            x_from = (x_place + inner + (outer - inner) * side) & 3
            key_token = (z_from * 4 + x_from) * (2 * half_tokens) + side * half_tokens
            key_token = key_token + (place & (half_tokens - 1))
            return key_token <= info[4] + row // head_local

        return allowed

    def fresh_mask(row):
        place = lax.broadcasted_iota(jnp.int32, (1, fresh_ref.shape[0]), 1)
        return (place >= row // (2 * head_local) * 2) & (place <= row // head_local)

    keys = [past_keys(j) for j in range(past_count)]
    masks = [past_mask(j) for j in range(past_count)]
    group_keys = [
        lambda: group[0].reshape(lines * half_tokens, width),
        lambda: group[1].reshape(lines * half_tokens, width),
    ]

    def store_decode(i, value, lse):
        decode_ref[i * tile : (i + 1) * tile, :] = value.astype(jnp.bfloat16)
        lse_ref[i * tile : (i + 1) * tile, :] = jnp.broadcast_to(lse, (tile, lse_ref.shape[1]))

    def store(i, value, lse):
        out_ref[i * tile : (i + 1) * tile, :] = value.astype(jnp.bfloat16)

    def run_decode(count):
        attend_tiles(
            config,
            dq_ref.shape[0] // tile,
            lambda i: dq_ref[i * tile : (i + 1) * tile, :],
            store_decode,
            hold,
            group_keys + [lambda: fresh_ref[...]] + keys[:count],
            [lambda row: None, lambda row: None, fresh_mask] + masks[:count],
            (3, placed),
        )

    def run_prompt(count):
        attend_tiles(
            config,
            q_ref.shape[0] // tile,
            lambda i: q_ref[i * tile : (i + 1) * tile, :],
            store,
            hold,
            group_keys + keys[:count],
            [group_mask(core), group_mask(1 - core)] + masks[:count],
        )

    short = past_len <= (past_count - 1) * chunk
    for number, run in enumerate((run_decode, run_prompt)):

        @pl.when((step == number) & short)
        def _(run=run):
            run(past_count - 1)

        @pl.when((step == number) & jnp.logical_not(short))
        def _(run=run):
            run(past_count)


def group_specs(pieces, block):
    count, _, half_tokens, width = pieces[0].shape
    return [pl.BlockSpec((count, None, half_tokens, width), block) for _ in pieces]


def attend_first(info, query, decode_query, pieces, piece_blocks, fresh, lat, factor, head_local):
    _, rows, width = query.shape
    decode_rows = decode_query.shape[0]
    half_tokens = pieces[0].shape[2]
    holders = 4 * len(pieces)
    keys = holders * (piece_blocks + 1) * half_tokens + fresh.shape[0]
    tile = 256
    chunk = 768
    return pl.pallas_call(
        functools.partial(first_body, (lat, factor), chunk, head_local),
        grid_spec=pltpu.PrefetchScalarGridSpec(
            num_scalar_prefetch=1,
            grid=(2,),
            in_specs=[
                pl.BlockSpec((None, rows, width), lambda i, _: (0, 0, 0)),
                pl.BlockSpec((decode_rows, width), lambda i, _: (0, 0)),
                pl.BlockSpec(fresh.shape, lambda i, _: (0, 0)),
            ]
            + [pl.BlockSpec(memory_space=pl.ANY)] * len(pieces)
            + group_specs(pieces, lambda i, _: (0, piece_blocks, 0, 0)),
            out_specs=[
                pl.BlockSpec((None, rows, lat), lambda i, _: (0, 0, 0)),
                pl.BlockSpec((decode_rows, lat), lambda i, _: (0, 0)),
                pl.BlockSpec((decode_rows, 128), lambda i, _: (0, 0)),
            ],
            scratch_shapes=[
                pltpu.VMEM((2, tile, keys), jnp.float32),
                pltpu.VMEM((holders, piece_blocks, half_tokens, width), jnp.bfloat16),
                pltpu.VMEM((2, 4, 4 * half_tokens, width), jnp.bfloat16),
                pltpu.SemaphoreType.DMA((holders,)),
            ],
        ),
        out_shape=[
            jax.ShapeDtypeStruct((1, rows, lat), jnp.bfloat16),
            jax.ShapeDtypeStruct((decode_rows, lat), jnp.bfloat16),
            jax.ShapeDtypeStruct((decode_rows, 128), jnp.float32),
        ],
        compiler_params=pltpu.CompilerParams(vmem_limit_bytes=VMEM_BYTES),
        cost_estimate=pl.CostEstimate(
            flops=2 * (rows + decode_rows) * keys * (768 + lat),
            bytes_accessed=2 * (keys + 2 * rows + 2 * decode_rows) * width,
            transcendentals=(rows + decode_rows) * keys,
        ),
        name="attend_first",
    )(info, query, decode_query, fresh, *pieces, *pieces)


def later_body(config, chunk, head_local, first, info, q_ref, past_ref, *rest):
    group_refs = rest[:8]
    out_ref, hold, group = rest[8:]
    step = pl.program_id(0)
    tile = hold.shape[1]
    seq_count, piece_rows, width = past_ref.shape
    lines = 16
    half_tokens = group_refs[0].shape[1]
    gather_group(group_refs, group)
    held = chunk // piece_rows
    past_count = seq_count // held
    past_len = info[step + first]
    z_place, x_place, core = info[5], info[6], info[7]

    def past_keys(j):
        return lambda: past_ref[j * held : (j + 1) * held].reshape(chunk, width)

    def past_mask(j):
        def allowed(row):
            if 2 * (j + 1) <= past_count:
                return None
            return lax.broadcasted_iota(jnp.int32, (1, chunk), 1) + j * chunk < past_len

        return allowed

    def group_mask(side):
        def allowed(row):
            place = lax.broadcasted_iota(jnp.int32, (1, lines * half_tokens), 1)
            outer = place // (4 * half_tokens)
            inner = (place // half_tokens) & 3
            z_from = (z_place + outer + (inner - outer) * side) & 3
            x_from = (x_place + inner + (outer - inner) * side) & 3
            key_token = (z_from * 4 + x_from) * (2 * half_tokens) + side * half_tokens
            key_token = key_token + (place & (half_tokens - 1))
            return key_token <= info[4] + row // head_local

        return allowed

    keys = [past_keys(j) for j in range(past_count)]
    keys += [
        lambda: group[0].reshape(lines * half_tokens, width),
        lambda: group[1].reshape(lines * half_tokens, width),
    ]
    masks = [past_mask(j) for j in range(past_count)]

    def store(i, value, lse):
        out_ref[i * tile : (i + 1) * tile, :] = value.astype(jnp.bfloat16)

    def run(count):
        attend_tiles(
            config,
            q_ref.shape[0] // tile,
            lambda i: q_ref[i * tile : (i + 1) * tile, :],
            store,
            hold,
            keys[:count] + keys[past_count:],
            masks[:count] + [group_mask(core), group_mask(1 - core)],
        )

    short = past_len <= (past_count - 1) * chunk

    @pl.when(short)
    def _():
        run(past_count - 1)

    @pl.when(jnp.logical_not(short))
    def _():
        run(past_count)


def attend_later(info, query, past, pieces, piece_blocks, first, lat, factor, head_local):
    prompts, rows, width = query.shape
    count = prompts - first
    seq_count, _, piece_rows, _ = past.shape
    half_tokens = pieces[0].shape[2]
    keys = seq_count * (piece_rows + 2 * half_tokens)
    tile = 256
    chunk = 768
    return pl.pallas_call(
        functools.partial(later_body, (lat, factor), chunk, head_local, first),
        grid_spec=pltpu.PrefetchScalarGridSpec(
            num_scalar_prefetch=1,
            grid=(count,),
            in_specs=[
                pl.BlockSpec((None, rows, width), lambda i, _: (i + first, 0, 0)),
                pl.BlockSpec(
                    (seq_count, None, piece_rows, width), lambda i, _: (0, i, 0, 0)
                ),
            ]
            + group_specs(pieces, lambda i, _: (0, piece_blocks + i + first, 0, 0)),
            out_specs=pl.BlockSpec((None, rows, lat), lambda i, _: (i, 0, 0)),
            scratch_shapes=[
                pltpu.VMEM((2, tile, keys), jnp.float32),
                pltpu.VMEM((2, 4, 4 * half_tokens, width), jnp.bfloat16),
            ],
        ),
        out_shape=jax.ShapeDtypeStruct((count, rows, lat), jnp.bfloat16),
        compiler_params=pltpu.CompilerParams(vmem_limit_bytes=VMEM_BYTES),
        cost_estimate=pl.CostEstimate(
            flops=2 * count * rows * keys * (768 + lat),
            bytes_accessed=2 * count * (keys + 2 * rows) * width,
            transcendentals=count * rows * keys,
        ),
        name="attend_later",
    )(info, query, past, *pieces)


def dispatch_body(source, length, q_ref, out_ref):
    slots, rows, width = out_ref.shape
    lat_rope = q_ref.shape[2]
    lane = lax.broadcasted_iota(jnp.int32, (rows, width - lat_rope), 1)
    for slot in range(slots):
        out_ref[slot, :, :lat_rope] = q_ref[source[slot]]
        size = length[slot]
        tail = jnp.where(lane < 32, size >> 4, size & 15)
        out_ref[slot, :, lat_rope:] = tail.astype(jnp.float32).astype(jnp.bfloat16)


def dispatch_queries(source, length, query, width):
    slots = source.shape[0]
    _, rows, _ = query.shape
    smem = pl.BlockSpec(memory_space=pltpu.SMEM)
    vmem = pl.BlockSpec(memory_space=pltpu.VMEM)
    return pl.pallas_call(
        dispatch_body,
        in_specs=[smem, smem, vmem],
        out_specs=vmem,
        out_shape=jax.ShapeDtypeStruct((slots, rows, width), jnp.bfloat16),
        compiler_params=pltpu.CompilerParams(vmem_limit_bytes=VMEM_BYTES),
        name="dispatch_queries",
    )(source, length, query)


def cache_body(lat, factor, batch, order, length, used, q_ref, *rest):
    pool_refs = rest[:batch]
    out_ref, lse_ref = rest[batch:]
    step = pl.program_id(0)
    rows = q_ref.shape[1]
    width, cache_rows = pool_refs[0].shape

    slots = [order[step * batch + b] for b in range(batch)]
    longest = length[slots[0]]

    def run(columns):
        place = lax.broadcasted_iota(jnp.int32, (1, columns), 1)
        lane = lax.broadcasted_iota(jnp.int32, (rows, lse_ref.shape[2]), 1)
        scores = [
            key_scores(q_ref[slots[b], :, :width], pool_refs[b][:, :columns], lat, NN)
            for b in range(batch)
        ]
        for b in range(batch):
            masked = jnp.where(place < length[slots[b]], scores[b], negative)
            peak = jnp.max(masked, axis=1, keepdims=True)
            weights = jnp.exp2((masked - peak) * factor)
            total = jnp.sum(weights, axis=1, keepdims=True)
            summed = dot(weights.astype(jnp.bfloat16), pool_refs[b][:lat, :columns], NT)
            out_ref[slots[b]] = (summed / total).astype(jnp.bfloat16)
            lse = peak * factor + jnp.log2(total)
            high = lse.astype(jnp.bfloat16).astype(jnp.float32)
            middle = (lse - high).astype(jnp.bfloat16).astype(jnp.float32)
            low = lse - high - middle
            lse_ref[slots[b]] = jnp.where(
                lane == 0, high, jnp.where(lane == 1, middle, low)
            ).astype(jnp.bfloat16)

    for columns in range(128, cache_rows + 1, 128):

        @pl.when(
            (step * batch < used[0]) & (longest > columns - 128) & (longest <= columns)
        )
        def _(columns=columns):
            run(columns)


def attend_cache(order, length, used, query, pool, lat, factor):
    batch = 4
    slots, rows, padded = query.shape
    _, width, cache_rows = pool.shape
    whole = pl.BlockSpec((slots, rows, padded), lambda i, *_: (0, 0, 0))

    def pool_spec(b):
        return pl.BlockSpec(
            (None, width, cache_rows), lambda i, order, *_: (order[i * batch + b], 0, 0)
        )

    return pl.pallas_call(
        functools.partial(cache_body, lat, factor, batch),
        grid_spec=pltpu.PrefetchScalarGridSpec(
            num_scalar_prefetch=3,
            grid=(slots // batch,),
            in_specs=[whole] + [pool_spec(b) for b in range(batch)],
            out_specs=[
                pl.BlockSpec((slots, rows, lat), lambda i, *_: (0, 0, 0)),
                pl.BlockSpec((slots, rows, 128), lambda i, *_: (0, 0, 0)),
            ],
        ),
        out_shape=[
            jax.ShapeDtypeStruct((slots, rows, lat), jnp.bfloat16),
            jax.ShapeDtypeStruct((slots, rows, 128), jnp.bfloat16),
        ],
        compiler_params=pltpu.CompilerParams(vmem_limit_bytes=VMEM_BYTES),
        cost_estimate=pl.CostEstimate(
            flops=2 * slots * 128 * cache_rows * (width + lat),
            bytes_accessed=2 * slots * cache_rows * width,
            transcendentals=slots * rows * cache_rows,
        ),
        name="attend_cache",
    )(order, length, used, query, *([pool] * batch))


def merge_body(slot, back_ref, near_ref, near_lse_ref, out_ref):
    count = near_ref.shape[0]
    width = near_ref.shape[2]
    for r in range(count):
        back = back_ref[slot[r]].astype(jnp.float32)
        far = back[:, :width]
        far_lse = back[:, width : width + 1] + back[:, width + 1 : width + 2]
        far_lse = far_lse + back[:, width + 2 : width + 3]
        near_lse = near_lse_ref[r][:, :1]
        peak = jnp.maximum(far_lse, near_lse)
        far_part = jnp.exp2(far_lse - peak)
        near_part = jnp.exp2(near_lse - peak)
        mixed = far * far_part + near_ref[r] * near_part
        out_ref[r] = (mixed / (far_part + near_part)).astype(jnp.bfloat16)


def merge_decode(slot, back, near, near_lse):
    smem = pl.BlockSpec(memory_space=pltpu.SMEM)
    vmem = pl.BlockSpec(memory_space=pltpu.VMEM)
    return pl.pallas_call(
        merge_body,
        in_specs=[smem, vmem, vmem, vmem],
        out_specs=vmem,
        out_shape=jax.ShapeDtypeStruct(near.shape, jnp.bfloat16),
        compiler_params=pltpu.CompilerParams(vmem_limit_bytes=VMEM_BYTES),
        name="merge_decode",
    )(slot, back, near, near_lse)


def swap_core(value):
    return lax.ppermute(value, "grp", [(0, 1), (1, 0)])


def fetch_tp(value, shift):
    return lax.ppermute(value, "tp", [((i + shift) % 4, i) for i in range(4)])


def fetch_ring(value, shift, turn):
    moves = []
    for i in range(16):
        z, x = i // 4, i % 4
        for c in range(2):
            if (c + turn) % 2 == 0:
                origin = z * 4 + (x + shift) % 4
            else:
                origin = (z + shift) % 4 * 4 + x
            moves.append((origin * 2 + c, i * 2 + c))
    return lax.ppermute(value, ("seq", "grp"), moves)


def on_device(
    group_hidden,
    group_query,
    past_cache,
    past_len,
    decode_hidden,
    decode_query,
    decode_pool,
    owner,
    dec_len,
    w_latent,
    kv_gain,
    w_value,
):
    seq_count = lax.axis_size("seq")
    seq_place = lax.axis_index("seq")
    tp_place = lax.axis_index("tp")
    core = lax.axis_index("grp")
    z_place, x_place = seq_place >> 2, seq_place & 3
    prompt_count, group_local, head_local, row_width = group_query.shape
    past_local = past_cache.shape[1]
    request_local = decode_query.shape[0]
    lat = kv_gain.shape[0]
    value_width = w_value.shape[2]
    slot_count = decode_pool.shape[0]
    pair_limit = slot_count // seq_count
    query_pairs = 2 * head_local
    factor = (value_width + row_width - lat) ** (-0.5) * log2_e

    half = past_local // 2
    later_rows = past_cache[1:].reshape((prompt_count - 1) * past_local, row_width)
    eighth = later_rows.shape[0] // 8
    past_part = lax.dynamic_slice_in_dim(
        later_rows, (tp_place * 2 + core) * eighth, eighth, axis=0
    )
    past_all = lax.all_gather(past_part, ("seq", "tp", "grp"), axis=0, tiled=True)
    past_all = past_all.reshape(seq_count, prompt_count - 1, past_local, row_width)

    half_tokens = group_local // 2
    pairs = 2 * request_local
    partial_group = jnp.einsum(
        "ptd,dc->ptc", group_hidden, w_latent, preferred_element_type=jnp.float32
    ).astype(jnp.bfloat16)
    partial_group = partial_group.reshape(prompt_count, 2, half_tokens, row_width)
    partial_decode = jnp.einsum(
        "rd,dc->rc",
        decode_hidden.reshape(pairs, -1),
        w_latent,
        preferred_element_type=jnp.float32,
    ).astype(jnp.bfloat16)
    group_part = prompt_count * half_tokens

    def both(chosen):
        part = lax.dynamic_index_in_dim(partial_group, chosen, axis=1, keepdims=False)
        return jnp.concatenate([part.reshape(group_part, row_width), partial_decode])

    pair_sum = both(core).astype(jnp.float32) + swap_core(both(1 - core)).astype(jnp.float32)
    pair_sum = pair_sum.astype(jnp.bfloat16)

    latent = pair_sum.astype(jnp.float32)
    for shift in range(1, 4):
        latent = latent + fetch_tp(pair_sum, shift).astype(jnp.float32)
    half_order = jnp.arange(half_tokens, dtype=jnp.int32)
    group_positions = (
        past_len[:, None] + seq_place * group_local + core * half_tokens + half_order[None, :]
    )
    decode_positions = (
        past_len[0]
        + group_local * seq_count
        + (dec_len[:, None] + jnp.arange(2, dtype=jnp.int32)).reshape(-1)
    )
    positions = jnp.concatenate([group_positions.reshape(-1), decode_positions])
    rows_own = make_rows(latent, kv_gain, positions)
    fresh = jnp.pad(rows_own[group_part:], ((0, 128 - pairs), (0, 0)))

    past_zero = lax.dynamic_slice(past_cache, (0, core * half, 0), (1, half, row_width))
    piece_blocks = half // half_tokens
    line = jnp.concatenate([past_zero.reshape(half, row_width), rows_own[:group_part]])
    line = line.reshape(-1, half_tokens, row_width)
    line = jnp.stack([line] + [fetch_ring(line, shift, 0) for shift in range(1, 4)])
    lines = [line] + [fetch_ring(line, shift, 1) for shift in range(1, 4)]

    targets = owner[:, 0]
    request_order = jnp.arange(request_local, dtype=jnp.int32)
    earlier = (targets[:, None] == targets[None, :]) & (
        request_order[None, :] < request_order[:, None]
    )
    slot_rank = jnp.sum(earlier.astype(jnp.int32), axis=1)
    destination = targets * pair_limit + slot_rank
    matches = jnp.arange(slot_count, dtype=jnp.int32)[:, None] == destination[None, :]
    source = jnp.sum(jnp.where(matches, request_order[None, :], 0), axis=1)
    send_length = jnp.sum(jnp.where(matches, dec_len[None, :], 0), axis=1)
    send_query = dispatch_queries(
        source,
        send_length,
        decode_query.reshape(request_local, query_pairs, row_width),
        row_width + 64,
    )
    arrived = lax.all_to_all(
        send_query.reshape(seq_count, pair_limit * query_pairs, row_width + 64),
        "seq",
        split_axis=0,
        concat_axis=0,
        tiled=True,
    ).reshape(slot_count, query_pairs, row_width + 64)
    marks = arrived[:, 0, row_width:].astype(jnp.float32)
    slot_length = (marks[:, 0] * 16 + marks[:, 32]).astype(jnp.int32)

    slots = jnp.arange(slot_count, dtype=jnp.int32)
    longer = (slot_length[None, :] > slot_length[:, None]) | (
        (slot_length[None, :] == slot_length[:, None]) & (slots[None, :] < slots[:, None])
    )
    rank = jnp.sum(longer.astype(jnp.int32), axis=1)
    used = jnp.sum((slot_length > 0).astype(jnp.int32))
    wanted = jnp.minimum(slots, jnp.maximum(used - 1, 0))
    order = jnp.sum(jnp.where(rank[None, :] == wanted[:, None], slots[None, :], 0), axis=1)
    cache_latent, cache_lse = attend_cache(
        order, slot_length, used.reshape(1), arrived, jnp.swapaxes(decode_pool, 1, 2), lat, factor
    )
    lines[1:], cache_latent = lax.optimization_barrier((lines[1:], cache_latent))
    pieces = lines + [swap_core(piece) for piece in lines]
    cache_value = jnp.einsum(
        "nshc,hcv->nshv",
        cache_latent.reshape(slot_count, 2, head_local, lat),
        w_value,
        preferred_element_type=jnp.float32,
    ).astype(jnp.bfloat16)
    back = jnp.concatenate(
        [cache_value.reshape(slot_count, query_pairs, value_width), cache_lse], axis=-1
    )
    back = lax.all_to_all(
        back.reshape(seq_count, pair_limit * query_pairs, 2 * value_width),
        "seq",
        split_axis=0,
        concat_axis=0,
        tiled=True,
    ).reshape(slot_count, query_pairs, 2 * value_width)

    info = jnp.stack(
        [past_len[p] for p in range(prompt_count)]
        + [seq_place * group_local, z_place, x_place, core]
    ).astype(jnp.int32)
    queries = group_query.reshape(prompt_count, group_local * head_local, row_width)
    decode_rows, _ = lax.optimization_barrier((decode_query, cache_value))
    first_latent, near_latent, near_lse = attend_first(
        info,
        queries,
        decode_rows.reshape(request_local * query_pairs, row_width),
        pieces,
        piece_blocks,
        fresh,
        lat,
        factor,
        head_local,
    )
    near = jnp.einsum(
        "rshc,hcv->rshv",
        near_latent.reshape(request_local, 2, head_local, lat),
        w_value,
        preferred_element_type=jnp.float32,
    )
    decode_out = merge_decode(
        destination,
        back,
        near.reshape(request_local, query_pairs, value_width),
        near_lse.reshape(request_local, query_pairs, 128),
    ).reshape(request_local, 2, head_local, value_width)

    queries, _ = lax.optimization_barrier((queries, decode_out))
    later_latent = attend_later(
        info, queries, past_all, pieces, piece_blocks, 1, lat, factor, head_local
    )
    prefill_out = jnp.concatenate(
        [
            jnp.einsum(
                "pthc,hcv->pthv",
                value.reshape(-1, group_local, head_local, lat),
                w_value,
                preferred_element_type=jnp.float32,
            ).astype(jnp.bfloat16)
            for value in (first_latent, later_latent)
        ]
    )
    return (prefill_out, decode_out)


def solution(mesh):
    in_specs = (
        P(None, "seq", ("tp", "grp")),
        P(None, "seq", ("tp", "grp"), None),
        P(None, "seq", None),
        P(),
        P("seq", None, ("tp", "grp")),
        P("seq", None, ("tp", "grp"), None),
        P("seq", None, None),
        P("seq", None),
        P("seq"),
        P(("tp", "grp"), None),
        P(),
        P(("tp", "grp"), None, None),
    )
    out_specs = (P(None, "seq", ("tp", "grp"), None), P("seq", None, ("tp", "grp"), None))
    return jax.shard_map(
        on_device, mesh=mesh, in_specs=in_specs, out_specs=out_specs, check_vma=False
    )
```

```python
import functools

import jax
import jax.numpy as jnp
from jax import lax
from jax.experimental import pallas as pl
from jax.experimental.pallas import tpu as pltpu
from jax.sharding import PartitionSpec as P

epsilon = 1e-06
negative = -1e30
log2_e = 1.4426950408889634
NT = (((1,), (1,)), ((), ()))
NN = (((1,), (0,)), ((), ()))
VMEM_BYTES = 56 * 2**20


def rotate(rope_part, positions):
    half_width = rope_part.shape[-1] // 2
    frequency = jnp.exp(-jnp.log(10000.0) * jnp.arange(half_width).astype(jnp.float32) / half_width)
    angles = positions.astype(jnp.float32)[..., None] * frequency
    cosine = jnp.cos(angles)
    sine_part = jnp.sin(angles)
    former = rope_part[..., :half_width]
    latter = rope_part[..., half_width:]
    return jnp.concatenate(
        [former * cosine - latter * sine_part, latter * cosine + former * sine_part], axis=-1
    )


def make_rows(latent, kv_gain, positions):
    lat_width = kv_gain.shape[0]
    latent_part = latent[..., :lat_width]
    spread = jnp.mean(latent_part * latent_part, axis=-1, keepdims=True)
    normed = latent_part * lax.rsqrt(spread + epsilon) * kv_gain
    return jnp.concatenate([normed, rotate(latent[..., lat_width:], positions)], axis=-1).astype(
        jnp.bfloat16
    )


def dot(left, right, dims):
    return lax.dot_general(left, right, dims, preferred_element_type=jnp.float32)


def key_scores(queries, keys, lat, dims):
    if dims is NT:
        return dot(queries[:, :lat], keys[:, :lat], NT) + dot(queries[:, lat:], keys[:, lat:], NT)
    return dot(queries[:, :lat], keys[:lat], NN) + dot(queries[:, lat:], keys[lat:], NN)


def lane_fold(op, total, block):
    for start in range(0, block.shape[1], 128):
        part = block[:, start : start + 128]
        total = part if total is None else op(total, part)
    return total


def attend_tiles(config, count, load, store, hold, keys, masks):
    lat, factor = config
    for i in range(count):
        queries = load(i)
        row = lax.broadcasted_iota(jnp.int32, (queries.shape[0], 1), 0) + i * queries.shape[0]
        highest = None
        end = 0
        for block, mask in zip(keys, masks):
            values = block()
            scores = key_scores(queries, values, lat, NT)
            allowed = mask(row)
            if allowed is not None:
                scores = jnp.where(allowed, scores, negative)
            hold[i % 2, :, end : end + values.shape[0]] = scores
            end += values.shape[0]
            highest = lane_fold(jnp.maximum, highest, scores)
        peak = jnp.max(highest, axis=1, keepdims=True)
        total = None
        summed = None
        end = 0
        for block in keys:
            values = block()
            weights = jnp.exp2((hold[i % 2, :, end : end + values.shape[0]] - peak) * factor)
            end += values.shape[0]
            total = lane_fold(jnp.add, total, weights)
            part = dot(weights.astype(jnp.bfloat16), values[:, :lat], NN)
            summed = part if summed is None else summed + part
        total = jnp.sum(total, axis=1, keepdims=True)
        store(i, summed / total, peak * factor + jnp.log2(total))


def gather_group(piece_refs, group):
    for c in range(2):
        for s in range(4):
            group[c, s] = piece_refs[c * 4 + s][...].reshape(group.shape[2:])


def first_body(config, chunk, head_local, info, q_ref, dq_ref, fresh_ref, *rest):
    pieces = rest[:8]
    group_refs = rest[8:16]
    out_ref, decode_ref, lse_ref, hold, past, group, arrive = rest[16:]
    step = pl.program_id(0)
    tile = hold.shape[1]
    holders, piece_blocks, half_tokens, width = past.shape
    lines = 16
    held = chunk // (piece_blocks * half_tokens)
    past_count = holders // held
    past_len = info[0]
    z_place, x_place, core = info[5], info[6], info[7]

    @pl.when(step == 0)
    def _():
        copies = []
        for c in range(2):
            side = core if c == 0 else 1 - core
            for s in range(4):
                for j in range(4):
                    dz = s + (j - s) * side
                    dx = j + (s - j) * side
                    holder = ((z_place + dz) & 3) * 4 + ((x_place + dx) & 3)
                    copies.append(
                        pltpu.make_async_copy(
                            pieces[c * 4 + s].at[j, pl.ds(0, piece_blocks)],
                            past.at[holder * 2 + side],
                            arrive.at[c * 16 + s * 4 + j],
                        )
                    )
        for copy in copies:
            copy.start()
        gather_group(group_refs, group)
        for copy in copies:
            copy.wait()

    def past_keys(j):
        return lambda: past[j * held : (j + 1) * held].reshape(chunk, width)

    def past_mask(j):
        def allowed(row):
            if 2 * (j + 1) <= past_count:
                return None
            return lax.broadcasted_iota(jnp.int32, (1, chunk), 1) + j * chunk < past_len

        return allowed

    def group_mask(side):
        def allowed(row):
            place = lax.broadcasted_iota(jnp.int32, (1, lines * half_tokens), 1)
            outer = place // (4 * half_tokens)
            inner = (place // half_tokens) & 3
            z_from = (z_place + outer + (inner - outer) * side) & 3
            x_from = (x_place + inner + (outer - inner) * side) & 3
            key_token = (z_from * 4 + x_from) * (2 * half_tokens) + side * half_tokens
            key_token = key_token + (place & (half_tokens - 1))
            return key_token <= info[4] + row // head_local

        return allowed

    def fresh_mask(row):
        place = lax.broadcasted_iota(jnp.int32, (1, fresh_ref.shape[0]), 1)
        return (place >= row // (2 * head_local) * 2) & (place <= row // head_local)

    keys = [past_keys(j) for j in range(past_count)]
    keys += [
        lambda: group[0].reshape(lines * half_tokens, width),
        lambda: group[1].reshape(lines * half_tokens, width),
    ]
    masks = [past_mask(j) for j in range(past_count)]

    @pl.when(step == 0)
    def _():
        def store(i, value, lse):
            decode_ref[i * tile : (i + 1) * tile, :] = value.astype(jnp.bfloat16)
            lse_ref[i * tile : (i + 1) * tile, :] = jnp.broadcast_to(lse, (tile, lse_ref.shape[1]))

        attend_tiles(
            config,
            dq_ref.shape[0] // tile,
            lambda i: dq_ref[i * tile : (i + 1) * tile, :],
            store,
            hold,
            keys + [lambda: fresh_ref[...]],
            masks + [lambda row: None, lambda row: None, fresh_mask],
        )

    @pl.when(step > 0)
    def _():
        def store(i, value, lse):
            out_ref[i * tile : (i + 1) * tile, :] = value.astype(jnp.bfloat16)

        attend_tiles(
            config,
            q_ref.shape[0] // tile,
            lambda i: q_ref[i * tile : (i + 1) * tile, :],
            store,
            hold,
            keys,
            masks + [group_mask(core), group_mask(1 - core)],
        )


def group_specs(pieces, block):
    count, _, half_tokens, width = pieces[0].shape
    return [pl.BlockSpec((count, None, half_tokens, width), block) for _ in pieces]


def attend_first(info, query, decode_query, pieces, piece_blocks, fresh, lat, factor, head_local):
    _, rows, width = query.shape
    decode_rows = decode_query.shape[0]
    half_tokens = pieces[0].shape[2]
    holders = 4 * len(pieces)
    keys = holders * (piece_blocks + 1) * half_tokens + fresh.shape[0]
    tile = 256
    chunk = 768
    return pl.pallas_call(
        functools.partial(first_body, (lat, factor), chunk, head_local),
        grid_spec=pltpu.PrefetchScalarGridSpec(
            num_scalar_prefetch=1,
            grid=(2,),
            in_specs=[
                pl.BlockSpec((None, rows, width), lambda i, _: (0, 0, 0)),
                pl.BlockSpec((decode_rows, width), lambda i, _: (0, 0)),
                pl.BlockSpec(fresh.shape, lambda i, _: (0, 0)),
            ]
            + [pl.BlockSpec(memory_space=pl.ANY)] * len(pieces)
            + group_specs(pieces, lambda i, _: (0, piece_blocks, 0, 0)),
            out_specs=[
                pl.BlockSpec((None, rows, lat), lambda i, _: (0, 0, 0)),
                pl.BlockSpec((decode_rows, lat), lambda i, _: (0, 0)),
                pl.BlockSpec((decode_rows, 128), lambda i, _: (0, 0)),
            ],
            scratch_shapes=[
                pltpu.VMEM((2, tile, keys), jnp.float32),
                pltpu.VMEM((holders, piece_blocks, half_tokens, width), jnp.bfloat16),
                pltpu.VMEM((2, 4, 4 * half_tokens, width), jnp.bfloat16),
                pltpu.SemaphoreType.DMA((holders,)),
            ],
        ),
        out_shape=[
            jax.ShapeDtypeStruct((1, rows, lat), jnp.bfloat16),
            jax.ShapeDtypeStruct((decode_rows, lat), jnp.bfloat16),
            jax.ShapeDtypeStruct((decode_rows, 128), jnp.float32),
        ],
        compiler_params=pltpu.CompilerParams(vmem_limit_bytes=VMEM_BYTES),
        cost_estimate=pl.CostEstimate(
            flops=2 * (rows + decode_rows) * keys * (768 + lat),
            bytes_accessed=2 * (keys + 2 * rows + 2 * decode_rows) * width,
            transcendentals=(rows + decode_rows) * keys,
        ),
        name="attend_first",
    )(info, query, decode_query, fresh, *pieces, *pieces)


def later_body(config, chunk, head_local, first, info, q_ref, past_ref, *rest):
    group_refs = rest[:8]
    out_ref, hold, group = rest[8:]
    step = pl.program_id(0)
    tile = hold.shape[1]
    seq_count, piece_rows, width = past_ref.shape
    lines = 16
    half_tokens = group_refs[0].shape[1]
    gather_group(group_refs, group)
    held = chunk // piece_rows
    past_count = seq_count // held
    past_len = info[step + first]
    z_place, x_place, core = info[5], info[6], info[7]

    def past_keys(j):
        return lambda: past_ref[j * held : (j + 1) * held].reshape(chunk, width)

    def past_mask(j):
        def allowed(row):
            if 2 * (j + 1) <= past_count:
                return None
            return lax.broadcasted_iota(jnp.int32, (1, chunk), 1) + j * chunk < past_len

        return allowed

    def group_mask(side):
        def allowed(row):
            place = lax.broadcasted_iota(jnp.int32, (1, lines * half_tokens), 1)
            outer = place // (4 * half_tokens)
            inner = (place // half_tokens) & 3
            z_from = (z_place + outer + (inner - outer) * side) & 3
            x_from = (x_place + inner + (outer - inner) * side) & 3
            key_token = (z_from * 4 + x_from) * (2 * half_tokens) + side * half_tokens
            key_token = key_token + (place & (half_tokens - 1))
            return key_token <= info[4] + row // head_local

        return allowed

    keys = [past_keys(j) for j in range(past_count)]
    keys += [
        lambda: group[0].reshape(lines * half_tokens, width),
        lambda: group[1].reshape(lines * half_tokens, width),
    ]
    masks = [past_mask(j) for j in range(past_count)]

    def store(i, value, lse):
        out_ref[i * tile : (i + 1) * tile, :] = value.astype(jnp.bfloat16)

    def run(count):
        attend_tiles(
            config,
            q_ref.shape[0] // tile,
            lambda i: q_ref[i * tile : (i + 1) * tile, :],
            store,
            hold,
            keys[:count] + keys[past_count:],
            masks[:count] + [group_mask(core), group_mask(1 - core)],
        )

    short = past_len <= (past_count - 1) * chunk

    @pl.when(short)
    def _():
        run(past_count - 1)

    @pl.when(jnp.logical_not(short))
    def _():
        run(past_count)


def attend_later(info, query, past, pieces, piece_blocks, first, lat, factor, head_local):
    prompts, rows, width = query.shape
    count = prompts - first
    seq_count, _, piece_rows, _ = past.shape
    half_tokens = pieces[0].shape[2]
    keys = seq_count * (piece_rows + 2 * half_tokens)
    tile = 256
    chunk = 768
    return pl.pallas_call(
        functools.partial(later_body, (lat, factor), chunk, head_local, first),
        grid_spec=pltpu.PrefetchScalarGridSpec(
            num_scalar_prefetch=1,
            grid=(count,),
            in_specs=[
                pl.BlockSpec((None, rows, width), lambda i, _: (i + first, 0, 0)),
                pl.BlockSpec(
                    (seq_count, None, piece_rows, width), lambda i, _: (0, i, 0, 0)
                ),
            ]
            + group_specs(pieces, lambda i, _: (0, piece_blocks + i + first, 0, 0)),
            out_specs=pl.BlockSpec((None, rows, lat), lambda i, _: (i, 0, 0)),
            scratch_shapes=[
                pltpu.VMEM((2, tile, keys), jnp.float32),
                pltpu.VMEM((2, 4, 4 * half_tokens, width), jnp.bfloat16),
            ],
        ),
        out_shape=jax.ShapeDtypeStruct((count, rows, lat), jnp.bfloat16),
        compiler_params=pltpu.CompilerParams(vmem_limit_bytes=VMEM_BYTES),
        cost_estimate=pl.CostEstimate(
            flops=2 * count * rows * keys * (768 + lat),
            bytes_accessed=2 * count * (keys + 2 * rows) * width,
            transcendentals=count * rows * keys,
        ),
        name="attend_later",
    )(info, query, past, *pieces)


def dispatch_body(source, length, q_ref, out_ref):
    slots, rows, width = out_ref.shape
    lat_rope = q_ref.shape[2]
    lane = lax.broadcasted_iota(jnp.int32, (rows, width - lat_rope), 1)
    for slot in range(slots):
        out_ref[slot, :, :lat_rope] = q_ref[source[slot]]
        size = length[slot]
        tail = jnp.where(lane < 32, size >> 4, size & 15)
        out_ref[slot, :, lat_rope:] = tail.astype(jnp.float32).astype(jnp.bfloat16)


def dispatch_queries(source, length, query, width):
    slots = source.shape[0]
    _, rows, _ = query.shape
    smem = pl.BlockSpec(memory_space=pltpu.SMEM)
    vmem = pl.BlockSpec(memory_space=pltpu.VMEM)
    return pl.pallas_call(
        dispatch_body,
        in_specs=[smem, smem, vmem],
        out_specs=vmem,
        out_shape=jax.ShapeDtypeStruct((slots, rows, width), jnp.bfloat16),
        compiler_params=pltpu.CompilerParams(vmem_limit_bytes=VMEM_BYTES),
        name="dispatch_queries",
    )(source, length, query)


def cache_body(lat, factor, batch, order, length, used, q_ref, *rest):
    pool_refs = rest[:batch]
    out_ref, lse_ref = rest[batch:]
    step = pl.program_id(0)
    rows = q_ref.shape[1]
    width, cache_rows = pool_refs[0].shape

    slots = [order[step * batch + b] for b in range(batch)]
    longest = length[slots[0]]

    def run(columns):
        place = lax.broadcasted_iota(jnp.int32, (1, columns), 1)
        lane = lax.broadcasted_iota(jnp.int32, (rows, lse_ref.shape[2]), 1)
        scores = [
            key_scores(q_ref[slots[b], :, :width], pool_refs[b][:, :columns], lat, NN)
            for b in range(batch)
        ]
        for b in range(batch):
            masked = jnp.where(place < length[slots[b]], scores[b], negative)
            peak = jnp.max(masked, axis=1, keepdims=True)
            weights = jnp.exp2((masked - peak) * factor)
            total = jnp.sum(weights, axis=1, keepdims=True)
            summed = dot(weights.astype(jnp.bfloat16), pool_refs[b][:lat, :columns], NT)
            out_ref[slots[b]] = (summed / total).astype(jnp.bfloat16)
            lse = peak * factor + jnp.log2(total)
            high = lse.astype(jnp.bfloat16).astype(jnp.float32)
            middle = (lse - high).astype(jnp.bfloat16).astype(jnp.float32)
            low = lse - high - middle
            lse_ref[slots[b]] = jnp.where(
                lane == 0, high, jnp.where(lane == 1, middle, low)
            ).astype(jnp.bfloat16)

    for columns in range(128, cache_rows + 1, 128):

        @pl.when(
            (step * batch < used[0]) & (longest > columns - 128) & (longest <= columns)
        )
        def _(columns=columns):
            run(columns)


def attend_cache(order, length, used, query, pool, lat, factor):
    batch = 4
    slots, rows, padded = query.shape
    _, width, cache_rows = pool.shape
    whole = pl.BlockSpec((slots, rows, padded), lambda i, *_: (0, 0, 0))

    def pool_spec(b):
        return pl.BlockSpec(
            (None, width, cache_rows), lambda i, order, *_: (order[i * batch + b], 0, 0)
        )

    return pl.pallas_call(
        functools.partial(cache_body, lat, factor, batch),
        grid_spec=pltpu.PrefetchScalarGridSpec(
            num_scalar_prefetch=3,
            grid=(slots // batch,),
            in_specs=[whole] + [pool_spec(b) for b in range(batch)],
            out_specs=[
                pl.BlockSpec((slots, rows, lat), lambda i, *_: (0, 0, 0)),
                pl.BlockSpec((slots, rows, 128), lambda i, *_: (0, 0, 0)),
            ],
        ),
        out_shape=[
            jax.ShapeDtypeStruct((slots, rows, lat), jnp.bfloat16),
            jax.ShapeDtypeStruct((slots, rows, 128), jnp.bfloat16),
        ],
        compiler_params=pltpu.CompilerParams(vmem_limit_bytes=VMEM_BYTES),
        cost_estimate=pl.CostEstimate(
            flops=2 * slots * 128 * cache_rows * (width + lat),
            bytes_accessed=2 * slots * cache_rows * width,
            transcendentals=slots * rows * cache_rows,
        ),
        name="attend_cache",
    )(order, length, used, query, *([pool] * batch))


def merge_body(slot, back_ref, near_ref, near_lse_ref, out_ref):
    count = near_ref.shape[0]
    width = near_ref.shape[2]
    for r in range(count):
        back = back_ref[slot[r]].astype(jnp.float32)
        far = back[:, :width]
        far_lse = back[:, width : width + 1] + back[:, width + 1 : width + 2]
        far_lse = far_lse + back[:, width + 2 : width + 3]
        near_lse = near_lse_ref[r][:, :1]
        peak = jnp.maximum(far_lse, near_lse)
        far_part = jnp.exp2(far_lse - peak)
        near_part = jnp.exp2(near_lse - peak)
        mixed = far * far_part + near_ref[r] * near_part
        out_ref[r] = (mixed / (far_part + near_part)).astype(jnp.bfloat16)


def merge_decode(slot, back, near, near_lse):
    smem = pl.BlockSpec(memory_space=pltpu.SMEM)
    vmem = pl.BlockSpec(memory_space=pltpu.VMEM)
    return pl.pallas_call(
        merge_body,
        in_specs=[smem, vmem, vmem, vmem],
        out_specs=vmem,
        out_shape=jax.ShapeDtypeStruct(near.shape, jnp.bfloat16),
        compiler_params=pltpu.CompilerParams(vmem_limit_bytes=VMEM_BYTES),
        name="merge_decode",
    )(slot, back, near, near_lse)


def swap_core(value):
    return lax.ppermute(value, "grp", [(0, 1), (1, 0)])


def fetch_tp(value, shift):
    return lax.ppermute(value, "tp", [((i + shift) % 4, i) for i in range(4)])


def fetch_ring(value, shift, turn):
    moves = []
    for i in range(16):
        z, x = i // 4, i % 4
        for c in range(2):
            if (c + turn) % 2 == 0:
                origin = z * 4 + (x + shift) % 4
            else:
                origin = (z + shift) % 4 * 4 + x
            moves.append((origin * 2 + c, i * 2 + c))
    return lax.ppermute(value, ("seq", "grp"), moves)


def on_device(
    group_hidden,
    group_query,
    past_cache,
    past_len,
    decode_hidden,
    decode_query,
    decode_pool,
    owner,
    dec_len,
    w_latent,
    kv_gain,
    w_value,
):
    seq_count = lax.axis_size("seq")
    seq_place = lax.axis_index("seq")
    tp_place = lax.axis_index("tp")
    core = lax.axis_index("grp")
    z_place, x_place = seq_place >> 2, seq_place & 3
    prompt_count, group_local, head_local, row_width = group_query.shape
    past_local = past_cache.shape[1]
    request_local = decode_query.shape[0]
    lat = kv_gain.shape[0]
    value_width = w_value.shape[2]
    slot_count = decode_pool.shape[0]
    pair_limit = slot_count // seq_count
    query_pairs = 2 * head_local
    factor = (value_width + row_width - lat) ** (-0.5) * log2_e

    half = past_local // 2
    eighth = (prompt_count - 1) * past_local // 8
    past_part = lax.dynamic_slice_in_dim(
        past_cache.reshape(prompt_count * past_local, row_width),
        past_local + (tp_place * 2 + core) * eighth,
        eighth,
        axis=0,
    )
    past_all = lax.all_gather(past_part, ("seq", "tp", "grp"), axis=0, tiled=True)
    past_all = past_all.reshape(seq_count, prompt_count - 1, past_local, row_width)

    half_tokens = group_local // 2
    pairs = 2 * request_local
    partial_group = jnp.einsum(
        "ptd,dc->ptc", group_hidden, w_latent, preferred_element_type=jnp.float32
    ).astype(jnp.bfloat16)
    partial_group = partial_group.reshape(prompt_count, 2, half_tokens, row_width)
    partial_decode = jnp.einsum(
        "rd,dc->rc",
        decode_hidden.reshape(pairs, -1),
        w_latent,
        preferred_element_type=jnp.float32,
    ).astype(jnp.bfloat16)
    group_part = prompt_count * half_tokens

    def both(chosen):
        part = lax.dynamic_index_in_dim(partial_group, chosen, axis=1, keepdims=False)
        return jnp.concatenate([part.reshape(group_part, row_width), partial_decode])

    pair_sum = both(core).astype(jnp.float32) + swap_core(both(1 - core)).astype(jnp.float32)
    pair_sum = pair_sum.astype(jnp.bfloat16)

    latent = pair_sum.astype(jnp.float32)
    for shift in range(1, 4):
        latent = latent + fetch_tp(pair_sum, shift).astype(jnp.float32)
    half_order = jnp.arange(half_tokens, dtype=jnp.int32)
    group_positions = (
        past_len[:, None] + seq_place * group_local + core * half_tokens + half_order[None, :]
    )
    decode_positions = (
        past_len[0]
        + group_local * seq_count
        + (dec_len[:, None] + jnp.arange(2, dtype=jnp.int32)).reshape(-1)
    )
    positions = jnp.concatenate([group_positions.reshape(-1), decode_positions])
    rows_own = make_rows(latent, kv_gain, positions)
    fresh = jnp.pad(rows_own[group_part:], ((0, 128 - pairs), (0, 0)))

    past_zero = lax.dynamic_slice(past_cache, (0, core * half, 0), (1, half, row_width))
    piece_blocks = half // half_tokens
    line = jnp.concatenate([past_zero.reshape(half, row_width), rows_own[:group_part]])
    line = line.reshape(-1, half_tokens, row_width)
    line = jnp.stack([line] + [fetch_ring(line, shift, 0) for shift in range(1, 4)])
    lines = [line] + [fetch_ring(line, shift, 1) for shift in range(1, 4)]

    targets = owner[:, 0]
    request_order = jnp.arange(request_local, dtype=jnp.int32)
    earlier = (targets[:, None] == targets[None, :]) & (
        request_order[None, :] < request_order[:, None]
    )
    slot_rank = jnp.sum(earlier.astype(jnp.int32), axis=1)
    destination = targets * pair_limit + slot_rank
    matches = jnp.arange(slot_count, dtype=jnp.int32)[:, None] == destination[None, :]
    source = jnp.sum(jnp.where(matches, request_order[None, :], 0), axis=1)
    send_length = jnp.sum(jnp.where(matches, dec_len[None, :], 0), axis=1)
    send_query = dispatch_queries(
        source,
        send_length,
        decode_query.reshape(request_local, query_pairs, row_width),
        row_width + 64,
    )
    arrived = lax.all_to_all(
        send_query.reshape(seq_count, pair_limit * query_pairs, row_width + 64),
        "seq",
        split_axis=0,
        concat_axis=0,
        tiled=True,
    ).reshape(slot_count, query_pairs, row_width + 64)
    marks = arrived[:, 0, row_width:].astype(jnp.float32)
    slot_length = (marks[:, 0] * 16 + marks[:, 32]).astype(jnp.int32)

    slots = jnp.arange(slot_count, dtype=jnp.int32)
    longer = (slot_length[None, :] > slot_length[:, None]) | (
        (slot_length[None, :] == slot_length[:, None]) & (slots[None, :] < slots[:, None])
    )
    rank = jnp.sum(longer.astype(jnp.int32), axis=1)
    used = jnp.sum((slot_length > 0).astype(jnp.int32))
    wanted = jnp.minimum(slots, jnp.maximum(used - 1, 0))
    order = jnp.sum(jnp.where(rank[None, :] == wanted[:, None], slots[None, :], 0), axis=1)
    cache_latent, cache_lse = attend_cache(
        order, slot_length, used.reshape(1), arrived, jnp.swapaxes(decode_pool, 1, 2), lat, factor
    )
    lines[1:], cache_latent = lax.optimization_barrier((lines[1:], cache_latent))
    pieces = lines + [swap_core(piece) for piece in lines]
    cache_value = jnp.einsum(
        "nshc,hcv->nshv",
        cache_latent.reshape(slot_count, 2, head_local, lat),
        w_value,
        preferred_element_type=jnp.float32,
    ).astype(jnp.bfloat16)
    back = jnp.concatenate(
        [cache_value.reshape(slot_count, query_pairs, value_width), cache_lse], axis=-1
    )
    back = lax.all_to_all(
        back.reshape(seq_count, pair_limit * query_pairs, 2 * value_width),
        "seq",
        split_axis=0,
        concat_axis=0,
        tiled=True,
    ).reshape(slot_count, query_pairs, 2 * value_width)

    info = jnp.stack(
        [past_len[p] for p in range(prompt_count)]
        + [seq_place * group_local, z_place, x_place, core]
    ).astype(jnp.int32)
    queries = group_query.reshape(prompt_count, group_local * head_local, row_width)
    decode_rows, _ = lax.optimization_barrier((decode_query, cache_value))
    first_latent, near_latent, near_lse = attend_first(
        info,
        queries,
        decode_rows.reshape(request_local * query_pairs, row_width),
        pieces,
        piece_blocks,
        fresh,
        lat,
        factor,
        head_local,
    )
    near = jnp.einsum(
        "rshc,hcv->rshv",
        near_latent.reshape(request_local, 2, head_local, lat),
        w_value,
        preferred_element_type=jnp.float32,
    )
    decode_out = merge_decode(
        destination,
        back,
        near.reshape(request_local, query_pairs, value_width),
        near_lse.reshape(request_local, query_pairs, 128),
    ).reshape(request_local, 2, head_local, value_width)

    queries, _ = lax.optimization_barrier((queries, decode_out))
    later_latent = attend_later(
        info, queries, past_all, pieces, piece_blocks, 1, lat, factor, head_local
    )
    prefill_out = jnp.concatenate(
        [
            jnp.einsum(
                "pthc,hcv->pthv",
                value.reshape(-1, group_local, head_local, lat),
                w_value,
                preferred_element_type=jnp.float32,
            ).astype(jnp.bfloat16)
            for value in (first_latent, later_latent)
        ]
    )
    return (prefill_out, decode_out)


def solution(mesh):
    in_specs = (
        P(None, "seq", ("tp", "grp")),
        P(None, "seq", ("tp", "grp"), None),
        P(None, "seq", None),
        P(),
        P("seq", None, ("tp", "grp")),
        P("seq", None, ("tp", "grp"), None),
        P("seq", None, None),
        P("seq", None),
        P("seq"),
        P(("tp", "grp"), None),
        P(),
        P(("tp", "grp"), None, None),
    )
    out_specs = (P(None, "seq", ("tp", "grp"), None), P("seq", None, ("tp", "grp"), None))
    return jax.shard_map(
        on_device, mesh=mesh, in_specs=in_specs, out_specs=out_specs, check_vma=False
    )
```

```python
import functools

import jax
import jax.numpy as jnp
from jax import lax
from jax.experimental import pallas as pl
from jax.experimental.pallas import tpu as pltpu
from jax.sharding import PartitionSpec as P

epsilon = 1e-06
negative = -1e30
log2_e = 1.4426950408889634
NT = (((1,), (1,)), ((), ()))
NN = (((1,), (0,)), ((), ()))
VMEM_BYTES = 56 * 2**20


def rotate(rope_part, positions):
    half_width = rope_part.shape[-1] // 2
    frequency = jnp.exp(-jnp.log(10000.0) * jnp.arange(half_width).astype(jnp.float32) / half_width)
    angles = positions.astype(jnp.float32)[..., None] * frequency
    cosine = jnp.cos(angles)
    sine_part = jnp.sin(angles)
    former = rope_part[..., :half_width]
    latter = rope_part[..., half_width:]
    return jnp.concatenate(
        [former * cosine - latter * sine_part, latter * cosine + former * sine_part], axis=-1
    )


def make_rows(latent, kv_gain, positions):
    lat_width = kv_gain.shape[0]
    latent_part = latent[..., :lat_width]
    spread = jnp.mean(latent_part * latent_part, axis=-1, keepdims=True)
    normed = latent_part * lax.rsqrt(spread + epsilon) * kv_gain
    return jnp.concatenate([normed, rotate(latent[..., lat_width:], positions)], axis=-1).astype(
        jnp.bfloat16
    )


def dot(left, right, dims):
    return lax.dot_general(left, right, dims, preferred_element_type=jnp.float32)


def key_scores(queries, keys, lat, dims):
    if dims is NT:
        return dot(queries[:, :lat], keys[:, :lat], NT) + dot(queries[:, lat:], keys[:, lat:], NT)
    return dot(queries[:, :lat], keys[:lat], NN) + dot(queries[:, lat:], keys[lat:], NN)


def lane_fold(op, total, block):
    for start in range(0, block.shape[1], 128):
        part = block[:, start : start + 128]
        total = part if total is None else op(total, part)
    return total


def attend_tiles(config, count, load, store, hold, keys, masks):
    lat, factor = config
    for i in range(count):
        queries = load(i)
        row = lax.broadcasted_iota(jnp.int32, (queries.shape[0], 1), 0) + i * queries.shape[0]
        highest = None
        end = 0
        for block, mask in zip(keys, masks):
            values = block()
            scores = key_scores(queries, values, lat, NT)
            allowed = mask(row)
            if allowed is not None:
                scores = jnp.where(allowed, scores, negative)
            hold[i % 2, :, end : end + values.shape[0]] = scores
            end += values.shape[0]
            highest = lane_fold(jnp.maximum, highest, scores)
        peak = jnp.max(highest, axis=1, keepdims=True)
        total = None
        summed = None
        end = 0
        for block in keys:
            values = block()
            weights = jnp.exp2((hold[i % 2, :, end : end + values.shape[0]] - peak) * factor)
            end += values.shape[0]
            total = lane_fold(jnp.add, total, weights)
            part = dot(weights.astype(jnp.bfloat16), values[:, :lat], NN)
            summed = part if summed is None else summed + part
        total = jnp.sum(total, axis=1, keepdims=True)
        store(i, summed / total, peak * factor + jnp.log2(total))


def gather_group(piece_refs, group):
    for c in range(2):
        for s in range(4):
            group[c, s] = piece_refs[c * 4 + s][...].reshape(group.shape[2:])


def first_body(config, chunk, head_local, info, q_ref, dq_ref, fresh_ref, *rest):
    pieces = rest[:8]
    group_refs = rest[8:16]
    out_ref, decode_ref, lse_ref, hold, past, group, arrive = rest[16:]
    step = pl.program_id(0)
    tile = hold.shape[1]
    holders, piece_blocks, half_tokens, width = past.shape
    lines = 16
    held = chunk // (piece_blocks * half_tokens)
    past_count = holders // held
    past_len = info[0]
    z_place, x_place, core = info[5], info[6], info[7]

    @pl.when(step == 0)
    def _():
        copies = []
        for c in range(2):
            side = core if c == 0 else 1 - core
            for s in range(4):
                for j in range(4):
                    dz = s + (j - s) * side
                    dx = j + (s - j) * side
                    holder = ((z_place + dz) & 3) * 4 + ((x_place + dx) & 3)
                    copies.append(
                        pltpu.make_async_copy(
                            pieces[c * 4 + s].at[j, pl.ds(0, piece_blocks)],
                            past.at[holder * 2 + side],
                            arrive.at[c * 16 + s * 4 + j],
                        )
                    )
        for copy in copies:
            copy.start()
        gather_group(group_refs, group)
        for copy in copies:
            copy.wait()

    def past_keys(j):
        return lambda: past[j * held : (j + 1) * held].reshape(chunk, width)

    def past_mask(j):
        def allowed(row):
            if 2 * (j + 1) <= past_count:
                return None
            return lax.broadcasted_iota(jnp.int32, (1, chunk), 1) + j * chunk < past_len

        return allowed

    def group_mask(side):
        def allowed(row):
            place = lax.broadcasted_iota(jnp.int32, (1, lines * half_tokens), 1)
            outer = place // (4 * half_tokens)
            inner = (place // half_tokens) & 3
            z_from = (z_place + outer + (inner - outer) * side) & 3
            x_from = (x_place + inner + (outer - inner) * side) & 3
            key_token = (z_from * 4 + x_from) * (2 * half_tokens) + side * half_tokens
            key_token = key_token + (place & (half_tokens - 1))
            return key_token <= info[4] + row // head_local

        return allowed

    def fresh_mask(row):
        place = lax.broadcasted_iota(jnp.int32, (1, fresh_ref.shape[0]), 1)
        return (place >= row // (2 * head_local) * 2) & (place <= row // head_local)

    keys = [past_keys(j) for j in range(past_count)]
    keys += [
        lambda: group[0].reshape(lines * half_tokens, width),
        lambda: group[1].reshape(lines * half_tokens, width),
    ]
    masks = [past_mask(j) for j in range(past_count)]

    @pl.when(step == 0)
    def _():
        def store(i, value, lse):
            decode_ref[i * tile : (i + 1) * tile, :] = value.astype(jnp.bfloat16)
            lse_ref[i * tile : (i + 1) * tile, :] = jnp.broadcast_to(lse, (tile, lse_ref.shape[1]))

        attend_tiles(
            config,
            dq_ref.shape[0] // tile,
            lambda i: dq_ref[i * tile : (i + 1) * tile, :],
            store,
            hold,
            keys + [lambda: fresh_ref[...]],
            masks + [lambda row: None, lambda row: None, fresh_mask],
        )

    @pl.when(step > 0)
    def _():
        def store(i, value, lse):
            out_ref[i * tile : (i + 1) * tile, :] = value.astype(jnp.bfloat16)

        attend_tiles(
            config,
            q_ref.shape[0] // tile,
            lambda i: q_ref[i * tile : (i + 1) * tile, :],
            store,
            hold,
            keys,
            masks + [group_mask(core), group_mask(1 - core)],
        )


def group_specs(pieces, block):
    count, _, half_tokens, width = pieces[0].shape
    return [pl.BlockSpec((count, None, half_tokens, width), block) for _ in pieces]


def attend_first(info, query, decode_query, pieces, piece_blocks, fresh, lat, factor, head_local):
    _, rows, width = query.shape
    decode_rows = decode_query.shape[0]
    half_tokens = pieces[0].shape[2]
    holders = 4 * len(pieces)
    keys = holders * (piece_blocks + 1) * half_tokens + fresh.shape[0]
    tile = 256
    chunk = 768
    return pl.pallas_call(
        functools.partial(first_body, (lat, factor), chunk, head_local),
        grid_spec=pltpu.PrefetchScalarGridSpec(
            num_scalar_prefetch=1,
            grid=(2,),
            in_specs=[
                pl.BlockSpec((None, rows, width), lambda i, _: (0, 0, 0)),
                pl.BlockSpec((decode_rows, width), lambda i, _: (0, 0)),
                pl.BlockSpec(fresh.shape, lambda i, _: (0, 0)),
            ]
            + [pl.BlockSpec(memory_space=pl.ANY)] * len(pieces)
            + group_specs(pieces, lambda i, _: (0, piece_blocks, 0, 0)),
            out_specs=[
                pl.BlockSpec((None, rows, lat), lambda i, _: (0, 0, 0)),
                pl.BlockSpec((decode_rows, lat), lambda i, _: (0, 0)),
                pl.BlockSpec((decode_rows, 128), lambda i, _: (0, 0)),
            ],
            scratch_shapes=[
                pltpu.VMEM((2, tile, keys), jnp.float32),
                pltpu.VMEM((holders, piece_blocks, half_tokens, width), jnp.bfloat16),
                pltpu.VMEM((2, 4, 4 * half_tokens, width), jnp.bfloat16),
                pltpu.SemaphoreType.DMA((holders,)),
            ],
        ),
        out_shape=[
            jax.ShapeDtypeStruct((1, rows, lat), jnp.bfloat16),
            jax.ShapeDtypeStruct((decode_rows, lat), jnp.bfloat16),
            jax.ShapeDtypeStruct((decode_rows, 128), jnp.float32),
        ],
        compiler_params=pltpu.CompilerParams(vmem_limit_bytes=VMEM_BYTES),
        cost_estimate=pl.CostEstimate(
            flops=2 * (rows + decode_rows) * keys * (768 + lat),
            bytes_accessed=2 * (keys + 2 * rows + 2 * decode_rows) * width,
            transcendentals=(rows + decode_rows) * keys,
        ),
        name="attend_first",
    )(info, query, decode_query, fresh, *pieces, *pieces)


def later_body(config, chunk, head_local, first, info, q_ref, past_ref, *rest):
    group_refs = rest[:8]
    out_ref, hold, group = rest[8:]
    step = pl.program_id(0)
    tile = hold.shape[1]
    seq_count, piece_rows, width = past_ref.shape
    lines = 16
    half_tokens = group_refs[0].shape[1]
    gather_group(group_refs, group)
    held = chunk // piece_rows
    past_count = seq_count // held
    past_len = info[step + first]
    z_place, x_place, core = info[5], info[6], info[7]

    def past_keys(j):
        return lambda: past_ref[j * held : (j + 1) * held].reshape(chunk, width)

    def past_mask(j):
        def allowed(row):
            if 2 * (j + 1) <= past_count:
                return None
            return lax.broadcasted_iota(jnp.int32, (1, chunk), 1) + j * chunk < past_len

        return allowed

    def group_mask(side):
        def allowed(row):
            place = lax.broadcasted_iota(jnp.int32, (1, lines * half_tokens), 1)
            outer = place // (4 * half_tokens)
            inner = (place // half_tokens) & 3
            z_from = (z_place + outer + (inner - outer) * side) & 3
            x_from = (x_place + inner + (outer - inner) * side) & 3
            key_token = (z_from * 4 + x_from) * (2 * half_tokens) + side * half_tokens
            key_token = key_token + (place & (half_tokens - 1))
            return key_token <= info[4] + row // head_local

        return allowed

    keys = [past_keys(j) for j in range(past_count)]
    keys += [
        lambda: group[0].reshape(lines * half_tokens, width),
        lambda: group[1].reshape(lines * half_tokens, width),
    ]
    masks = [past_mask(j) for j in range(past_count)]

    def store(i, value, lse):
        out_ref[i * tile : (i + 1) * tile, :] = value.astype(jnp.bfloat16)

    def run(count):
        attend_tiles(
            config,
            q_ref.shape[0] // tile,
            lambda i: q_ref[i * tile : (i + 1) * tile, :],
            store,
            hold,
            keys[:count] + keys[past_count:],
            masks[:count] + [group_mask(core), group_mask(1 - core)],
        )

    short = past_len <= (past_count - 1) * chunk

    @pl.when(short)
    def _():
        run(past_count - 1)

    @pl.when(jnp.logical_not(short))
    def _():
        run(past_count)


def attend_later(info, query, past, pieces, piece_blocks, first, lat, factor, head_local):
    prompts, rows, width = query.shape
    count = prompts - first
    seq_count, _, piece_rows, _ = past.shape
    half_tokens = pieces[0].shape[2]
    keys = seq_count * (piece_rows + 2 * half_tokens)
    tile = 256
    chunk = 768
    return pl.pallas_call(
        functools.partial(later_body, (lat, factor), chunk, head_local, first),
        grid_spec=pltpu.PrefetchScalarGridSpec(
            num_scalar_prefetch=1,
            grid=(count,),
            in_specs=[
                pl.BlockSpec((None, rows, width), lambda i, _: (i + first, 0, 0)),
                pl.BlockSpec(
                    (seq_count, None, piece_rows, width), lambda i, _: (0, i, 0, 0)
                ),
            ]
            + group_specs(pieces, lambda i, _: (0, piece_blocks + i + first, 0, 0)),
            out_specs=pl.BlockSpec((None, rows, lat), lambda i, _: (i, 0, 0)),
            scratch_shapes=[
                pltpu.VMEM((2, tile, keys), jnp.float32),
                pltpu.VMEM((2, 4, 4 * half_tokens, width), jnp.bfloat16),
            ],
        ),
        out_shape=jax.ShapeDtypeStruct((count, rows, lat), jnp.bfloat16),
        compiler_params=pltpu.CompilerParams(vmem_limit_bytes=VMEM_BYTES),
        cost_estimate=pl.CostEstimate(
            flops=2 * count * rows * keys * (768 + lat),
            bytes_accessed=2 * count * (keys + 2 * rows) * width,
            transcendentals=count * rows * keys,
        ),
        name="attend_later",
    )(info, query, past, *pieces)


def dispatch_body(source, length, q_ref, out_ref):
    slots, rows, width = out_ref.shape
    lat_rope = q_ref.shape[2]
    lane = lax.broadcasted_iota(jnp.int32, (rows, width - lat_rope), 1)
    for slot in range(slots):
        out_ref[slot, :, :lat_rope] = q_ref[source[slot]]
        size = length[slot]
        tail = jnp.where(lane < 32, size >> 4, size & 15)
        out_ref[slot, :, lat_rope:] = tail.astype(jnp.float32).astype(jnp.bfloat16)


def dispatch_queries(source, length, query, width):
    slots = source.shape[0]
    _, rows, _ = query.shape
    smem = pl.BlockSpec(memory_space=pltpu.SMEM)
    vmem = pl.BlockSpec(memory_space=pltpu.VMEM)
    return pl.pallas_call(
        dispatch_body,
        in_specs=[smem, smem, vmem],
        out_specs=vmem,
        out_shape=jax.ShapeDtypeStruct((slots, rows, width), jnp.bfloat16),
        compiler_params=pltpu.CompilerParams(vmem_limit_bytes=VMEM_BYTES),
        name="dispatch_queries",
    )(source, length, query)


def cache_body(lat, factor, batch, order, length, used, q_ref, *rest):
    pool_refs = rest[:batch]
    out_ref, lse_ref = rest[batch:]
    step = pl.program_id(0)
    rows = q_ref.shape[1]
    width, cache_rows = pool_refs[0].shape

    slots = [order[step * batch + b] for b in range(batch)]
    longest = length[slots[0]]

    def run(columns):
        place = lax.broadcasted_iota(jnp.int32, (1, columns), 1)
        lane = lax.broadcasted_iota(jnp.int32, (rows, lse_ref.shape[2]), 1)
        scores = [
            key_scores(q_ref[slots[b], :, :width], pool_refs[b][:, :columns], lat, NN)
            for b in range(batch)
        ]
        for b in range(batch):
            masked = jnp.where(place < length[slots[b]], scores[b], negative)
            peak = jnp.max(masked, axis=1, keepdims=True)
            weights = jnp.exp2((masked - peak) * factor)
            total = jnp.sum(weights, axis=1, keepdims=True)
            summed = dot(weights.astype(jnp.bfloat16), pool_refs[b][:lat, :columns], NT)
            out_ref[slots[b]] = (summed / total).astype(jnp.bfloat16)
            lse = peak * factor + jnp.log2(total)
            high = lse.astype(jnp.bfloat16).astype(jnp.float32)
            middle = (lse - high).astype(jnp.bfloat16).astype(jnp.float32)
            low = lse - high - middle
            lse_ref[slots[b]] = jnp.where(
                lane == 0, high, jnp.where(lane == 1, middle, low)
            ).astype(jnp.bfloat16)

    for columns in range(128, cache_rows + 1, 128):

        @pl.when(
            (step * batch < used[0]) & (longest > columns - 128) & (longest <= columns)
        )
        def _(columns=columns):
            run(columns)


def attend_cache(order, length, used, query, pool, lat, factor):
    batch = 4
    slots, rows, padded = query.shape
    _, width, cache_rows = pool.shape
    whole = pl.BlockSpec((slots, rows, padded), lambda i, *_: (0, 0, 0))

    def pool_spec(b):
        return pl.BlockSpec(
            (None, width, cache_rows), lambda i, order, *_: (order[i * batch + b], 0, 0)
        )

    return pl.pallas_call(
        functools.partial(cache_body, lat, factor, batch),
        grid_spec=pltpu.PrefetchScalarGridSpec(
            num_scalar_prefetch=3,
            grid=(slots // batch,),
            in_specs=[whole] + [pool_spec(b) for b in range(batch)],
            out_specs=[
                pl.BlockSpec((slots, rows, lat), lambda i, *_: (0, 0, 0)),
                pl.BlockSpec((slots, rows, 128), lambda i, *_: (0, 0, 0)),
            ],
        ),
        out_shape=[
            jax.ShapeDtypeStruct((slots, rows, lat), jnp.bfloat16),
            jax.ShapeDtypeStruct((slots, rows, 128), jnp.bfloat16),
        ],
        compiler_params=pltpu.CompilerParams(vmem_limit_bytes=VMEM_BYTES),
        cost_estimate=pl.CostEstimate(
            flops=2 * slots * 128 * cache_rows * (width + lat),
            bytes_accessed=2 * slots * cache_rows * width,
            transcendentals=slots * rows * cache_rows,
        ),
        name="attend_cache",
    )(order, length, used, query, *([pool] * batch))


def merge_body(slot, back_ref, near_ref, near_lse_ref, out_ref):
    count = near_ref.shape[0]
    width = near_ref.shape[2]
    for r in range(count):
        back = back_ref[slot[r]].astype(jnp.float32)
        far = back[:, :width]
        far_lse = back[:, width : width + 1] + back[:, width + 1 : width + 2]
        far_lse = far_lse + back[:, width + 2 : width + 3]
        near_lse = near_lse_ref[r][:, :1]
        peak = jnp.maximum(far_lse, near_lse)
        far_part = jnp.exp2(far_lse - peak)
        near_part = jnp.exp2(near_lse - peak)
        mixed = far * far_part + near_ref[r] * near_part
        out_ref[r] = (mixed / (far_part + near_part)).astype(jnp.bfloat16)


def merge_decode(slot, back, near, near_lse):
    smem = pl.BlockSpec(memory_space=pltpu.SMEM)
    vmem = pl.BlockSpec(memory_space=pltpu.VMEM)
    return pl.pallas_call(
        merge_body,
        in_specs=[smem, vmem, vmem, vmem],
        out_specs=vmem,
        out_shape=jax.ShapeDtypeStruct(near.shape, jnp.bfloat16),
        compiler_params=pltpu.CompilerParams(vmem_limit_bytes=VMEM_BYTES),
        name="merge_decode",
    )(slot, back, near, near_lse)


def swap_core(value):
    return lax.ppermute(value, "grp", [(0, 1), (1, 0)])


def fetch_tp(value, shift):
    return lax.ppermute(value, "tp", [((i + shift) % 4, i) for i in range(4)])


def fetch_ring(value, shift, turn):
    moves = []
    for i in range(16):
        z, x = i // 4, i % 4
        for c in range(2):
            if (c + turn) % 2 == 0:
                origin = z * 4 + (x + shift) % 4
            else:
                origin = (z + shift) % 4 * 4 + x
            moves.append((origin * 2 + c, i * 2 + c))
    return lax.ppermute(value, ("seq", "grp"), moves)


def on_device(
    group_hidden,
    group_query,
    past_cache,
    past_len,
    decode_hidden,
    decode_query,
    decode_pool,
    owner,
    dec_len,
    w_latent,
    kv_gain,
    w_value,
):
    seq_count = lax.axis_size("seq")
    seq_place = lax.axis_index("seq")
    tp_place = lax.axis_index("tp")
    core = lax.axis_index("grp")
    z_place, x_place = seq_place >> 2, seq_place & 3
    prompt_count, group_local, head_local, row_width = group_query.shape
    past_local = past_cache.shape[1]
    request_local = decode_query.shape[0]
    lat = kv_gain.shape[0]
    value_width = w_value.shape[2]
    slot_count = decode_pool.shape[0]
    pair_limit = slot_count // seq_count
    query_pairs = 2 * head_local
    factor = (value_width + row_width - lat) ** (-0.5) * log2_e

    half = past_local // 2
    eighth = (prompt_count - 1) * past_local // 8
    past_part = lax.dynamic_slice_in_dim(
        past_cache.reshape(prompt_count * past_local, row_width),
        past_local + (tp_place * 2 + core) * eighth,
        eighth,
        axis=0,
    )
    past_all = lax.all_gather(past_part, ("seq", "tp", "grp"), axis=0, tiled=True)
    past_all = past_all.reshape(seq_count, prompt_count - 1, past_local, row_width)

    half_tokens = group_local // 2
    pairs = 2 * request_local
    partial_group = jnp.einsum(
        "ptd,dc->ptc", group_hidden, w_latent, preferred_element_type=jnp.float32
    ).astype(jnp.bfloat16)
    partial_group = partial_group.reshape(prompt_count, 2, half_tokens, row_width)
    partial_decode = jnp.einsum(
        "rd,dc->rc",
        decode_hidden.reshape(pairs, -1),
        w_latent,
        preferred_element_type=jnp.float32,
    ).astype(jnp.bfloat16)
    group_part = prompt_count * half_tokens

    def both(chosen):
        part = lax.dynamic_index_in_dim(partial_group, chosen, axis=1, keepdims=False)
        return jnp.concatenate([part.reshape(group_part, row_width), partial_decode])

    pair_sum = both(core).astype(jnp.float32) + swap_core(both(1 - core)).astype(jnp.float32)
    pair_sum = pair_sum.astype(jnp.bfloat16)

    latent = pair_sum.astype(jnp.float32)
    for shift in range(1, 4):
        latent = latent + fetch_tp(pair_sum, shift).astype(jnp.float32)
    half_order = jnp.arange(half_tokens, dtype=jnp.int32)
    group_positions = (
        past_len[:, None] + seq_place * group_local + core * half_tokens + half_order[None, :]
    )
    decode_positions = (
        past_len[0]
        + group_local * seq_count
        + (dec_len[:, None] + jnp.arange(2, dtype=jnp.int32)).reshape(-1)
    )
    positions = jnp.concatenate([group_positions.reshape(-1), decode_positions])
    rows_own = make_rows(latent, kv_gain, positions)
    fresh = jnp.pad(rows_own[group_part:], ((0, 128 - pairs), (0, 0)))

    past_zero = lax.dynamic_slice(past_cache, (0, core * half, 0), (1, half, row_width))
    piece_blocks = half // half_tokens
    line = jnp.concatenate([past_zero.reshape(half, row_width), rows_own[:group_part]])
    line = line.reshape(-1, half_tokens, row_width)
    line = jnp.stack([line] + [fetch_ring(line, shift, 0) for shift in range(1, 4)])
    lines = [line] + [fetch_ring(line, shift, 1) for shift in range(1, 4)]

    targets = owner[:, 0]
    request_order = jnp.arange(request_local, dtype=jnp.int32)
    earlier = (targets[:, None] == targets[None, :]) & (
        request_order[None, :] < request_order[:, None]
    )
    slot_rank = jnp.sum(earlier.astype(jnp.int32), axis=1)
    destination = targets * pair_limit + slot_rank
    matches = jnp.arange(slot_count, dtype=jnp.int32)[:, None] == destination[None, :]
    source = jnp.sum(jnp.where(matches, request_order[None, :], 0), axis=1)
    send_length = jnp.sum(jnp.where(matches, dec_len[None, :], 0), axis=1)
    send_query = dispatch_queries(
        source,
        send_length,
        decode_query.reshape(request_local, query_pairs, row_width),
        row_width + 64,
    )
    arrived = lax.all_to_all(
        send_query.reshape(seq_count, pair_limit * query_pairs, row_width + 64),
        "seq",
        split_axis=0,
        concat_axis=0,
        tiled=True,
    ).reshape(slot_count, query_pairs, row_width + 64)
    marks = arrived[:, 0, row_width:].astype(jnp.float32)
    slot_length = (marks[:, 0] * 16 + marks[:, 32]).astype(jnp.int32)

    slots = jnp.arange(slot_count, dtype=jnp.int32)
    longer = (slot_length[None, :] > slot_length[:, None]) | (
        (slot_length[None, :] == slot_length[:, None]) & (slots[None, :] < slots[:, None])
    )
    rank = jnp.sum(longer.astype(jnp.int32), axis=1)
    used = jnp.sum((slot_length > 0).astype(jnp.int32))
    wanted = jnp.minimum(slots, jnp.maximum(used - 1, 0))
    order = jnp.sum(jnp.where(rank[None, :] == wanted[:, None], slots[None, :], 0), axis=1)
    cache_latent, cache_lse = attend_cache(
        order, slot_length, used.reshape(1), arrived, jnp.swapaxes(decode_pool, 1, 2), lat, factor
    )
    cache_value = jnp.einsum(
        "nshc,hcv->nshv",
        cache_latent.reshape(slot_count, 2, head_local, lat),
        w_value,
        preferred_element_type=jnp.float32,
    ).astype(jnp.bfloat16)
    back = jnp.concatenate(
        [cache_value.reshape(slot_count, query_pairs, value_width), cache_lse], axis=-1
    )
    lines[1:], _ = lax.optimization_barrier((lines[1:], back))
    pieces = lines + [swap_core(piece) for piece in lines]
    back = lax.all_to_all(
        back.reshape(seq_count, pair_limit * query_pairs, 2 * value_width),
        "seq",
        split_axis=0,
        concat_axis=0,
        tiled=True,
    ).reshape(slot_count, query_pairs, 2 * value_width)

    info = jnp.stack(
        [past_len[p] for p in range(prompt_count)]
        + [seq_place * group_local, z_place, x_place, core]
    ).astype(jnp.int32)
    queries = group_query.reshape(prompt_count, group_local * head_local, row_width)
    decode_rows, _ = lax.optimization_barrier((decode_query, cache_value))
    first_latent, near_latent, near_lse = attend_first(
        info,
        queries,
        decode_rows.reshape(request_local * query_pairs, row_width),
        pieces,
        piece_blocks,
        fresh,
        lat,
        factor,
        head_local,
    )
    near = jnp.einsum(
        "rshc,hcv->rshv",
        near_latent.reshape(request_local, 2, head_local, lat),
        w_value,
        preferred_element_type=jnp.float32,
    )
    decode_out = merge_decode(
        destination,
        back,
        near.reshape(request_local, query_pairs, value_width),
        near_lse.reshape(request_local, query_pairs, 128),
    ).reshape(request_local, 2, head_local, value_width)

    queries, _ = lax.optimization_barrier((queries, decode_out))
    later_latent = attend_later(
        info, queries, past_all, pieces, piece_blocks, 1, lat, factor, head_local
    )
    prefill_out = jnp.concatenate(
        [
            jnp.einsum(
                "pthc,hcv->pthv",
                value.reshape(-1, group_local, head_local, lat),
                w_value,
                preferred_element_type=jnp.float32,
            ).astype(jnp.bfloat16)
            for value in (first_latent, later_latent)
        ]
    )
    return (prefill_out, decode_out)


def solution(mesh):
    in_specs = (
        P(None, "seq", ("tp", "grp")),
        P(None, "seq", ("tp", "grp"), None),
        P(None, "seq", None),
        P(),
        P("seq", None, ("tp", "grp")),
        P("seq", None, ("tp", "grp"), None),
        P("seq", None, None),
        P("seq", None),
        P("seq"),
        P(("tp", "grp"), None),
        P(),
        P(("tp", "grp"), None, None),
    )
    out_specs = (P(None, "seq", ("tp", "grp"), None), P("seq", None, ("tp", "grp"), None))
    return jax.shard_map(
        on_device, mesh=mesh, in_specs=in_specs, out_specs=out_specs, check_vma=False
    )
```
